32 devices in a mesh: dp: 8 (over z, x), tensor: 4 (over y, core).
Axes of the slice: x: 2, y: 2, z: 4, core: 2. Of those that a mesh axis runs over, the one named last changes fastest.
Arguments:
- tokens: bfloat16 [8192, 1024], P(('dp', 'tensor')), may hold values from -6 to 6
- segments: int32 [8, 1024], P('dp'), may hold values from 0 to 3, never falling along the last dimension, each value on 1 to 512 neighbouring positions
- cotangent: bfloat16 [8192, 1024], P(('dp', 'tensor')), may hold values from -6 to 6
- timestep_norm_gain: float32 [1024], replicated, may hold values from 0.5 to 1.5
- ema_alpha: float32 [1024, 16], P('tensor'), may hold values from 0.05 to 0.95
- ema_delta: float32 [1024, 16], P('tensor'), may hold values from 0.05 to 0.95
- ema_theta: float32 [1024, 16], P('tensor'), may hold values from -1 to 1
- ema_beta: float32 [1024, 16], P('tensor'), may hold values from -3 to 3
- eta_real: float32 [1024, 16], P('tensor'), may hold values from -1 to 1
- eta_imag: float32 [1024, 16], P('tensor'), may hold values from -1 to 1
- ema_omega: float32 [1024], P('tensor'), may hold values from -2 to 2
- w_shared: bfloat16 [1024, 256], P('tensor'), may hold values from -0.1875 to 0.1875
- q_gain: float32 [256], replicated, may hold values from 0.5 to 1.5
- q_bias: float32 [256], replicated, may hold values from -2 to 2
- k_gain: float32 [256], replicated, may hold values from 0.5 to 1.5
- w_attgate: bfloat16 [1024, 2048], P(None, 'tensor'), may hold values from -0.1875 to 0.1875
- w_value: bfloat16 [1024, 2048], P(None, 'tensor'), may hold values from -0.1875 to 0.1875
- w_attout: bfloat16 [2048, 1024], P('tensor'), may hold values from -0.75 to 0.75
- rms_gain: float32 [1024], replicated, may hold values from 0.5 to 1.5
- w_gate: bfloat16 [1024, 2560], P(None, 'tensor'), may hold values from -0.1875 to 0.1875
- w_up: bfloat16 [1024, 2560], P(None, 'tensor'), may hold values from -0.1875 to 0.1875
- w_down: bfloat16 [2560, 1024], P('tensor'), may hold values from -0.25 to 0.25
Outputs:
- output: bfloat16 [8192, 1024], P(('dp', 'tensor'))
- grad_tokens: bfloat16 [8192, 1024], P(('dp', 'tensor'))
- grad_norm_gain: float32 [1024], replicated
- grad_alpha: float32 [1024, 16], P('tensor')
- grad_delta: float32 [1024, 16], P('tensor')
- grad_theta: float32 [1024, 16], P('tensor')
- grad_beta: float32 [1024, 16], P('tensor')
- grad_eta_real: float32 [1024, 16], P('tensor')
- grad_eta_imag: float32 [1024, 16], P('tensor')
- grad_omega: float32 [1024], P('tensor')
- grad_shared: float32 [1024, 256], P('tensor')
- grad_q_gain: float32 [256], replicated
- grad_q_bias: float32 [256], replicated
- grad_k_gain: float32 [256], replicated
- grad_attgate: float32 [1024, 2048], P(None, 'tensor')
- grad_value: float32 [1024, 2048], P(None, 'tensor')
- grad_attout: float32 [2048, 1024], P('tensor')
- grad_rms_gain: float32 [1024], replicated
- grad_gate: float32 [1024, 2560], P(None, 'tensor')
- grad_up: float32 [1024, 2560], P(None, 'tensor')
- grad_down: float32 [2560, 1024], P('tensor')
The draws below stay inside these ranges and needn't reach their ends.
Inputs may be any that keep to these rules, and one draw needn't show every extreme that they name: `segments`: within each row segment numbers never fall; each of the 4 documents has 1 to 512 tokens and one has exactly 512.
All inputs are finite; a program needn't handle non-finite values.
Results may differ from the reference program's by a relative error of at most 0.017.
Values may be sent and summed in bfloat16 or wider, within the bound.
A program may use at most 256 MiB of HBM per device.

```python
import math
import jax
import jax.numpy as jnp
import numpy as np
from jax import lax

D = 1024
Z = 256
V = 2048
FF = 2560
NDIM = 16
TOK_DEV = 1024
DOCS = 4
SEQS = 8
TOKENS = 8192


def levels(stream_key, extent, pieces, least, high):
    factor_of, own = 1.0, jax.random.fold_in(stream_key, 6)
    for dim, blocks in pieces:
        heights = jnp.exp(jax.random.uniform(jax.random.fold_in(own, dim), (blocks,), jnp.float32, least / len(pieces), high / len(pieces)))
        factor_of = factor_of * jnp.repeat(heights, extent[dim] // blocks).reshape([-1 if axis == dim else 1 for axis in range(len(extent))])
    return factor_of


def profile(amount, total, reach, skew):
    loads = [(1 << 20) // math.isqrt(standing ** skew) + 1 for standing in range(2, amount + 1)]
    spare, holding = total - reach - (amount - 1), [1] * (amount - 1)
    while spare > 0:
        candidates = [i for i in range(amount - 1) if holding[i] < reach]
        whole, remaining = sum([loads[i] for i in candidates]), spare
        for i in candidates:
            more = min(reach - holding[i], max(1, remaining * loads[i] // whole), spare)
            holding[i] = holding[i] + more
            spare = spare - more
    return np.array([reach] + holding)


def ragged(own_key, number_of, total, reach, slope):
    if number_of == 2:
        one = jax.random.randint(own_key, (), max(1, total - reach), min(reach, total - 1) + 1)
        return jnp.stack([one, total - one])
    lengths = jnp.asarray(profile(number_of, total, reach, slope), jnp.int32)
    pairs = (number_of - 1) // 2
    giver, taker = lengths[1:1 + 2 * pairs:2], lengths[2:2 + 2 * pairs:2]
    room = jnp.minimum(giver - 1, reach - taker)
    passed = jax.random.randint(jax.random.fold_in(own_key, 1), (pairs,), 0, 1 << 20) % (room + 1)
    lengths = lengths.at[1:1 + 2 * pairs:2].set(giver - passed).at[2:2 + 2 * pairs:2].set(taker + passed)
    return lengths[jax.random.permutation(jax.random.fold_in(own_key, 2), number_of)]


def centred(stream_key, dims, deviation, bound, pieces=(), dtype=jnp.bfloat16):
    entries = deviation * jax.random.normal(stream_key, dims, jnp.float32)
    if pieces:
        entries = entries * levels(stream_key, dims, pieces, -0.22, 0.18)
    return jnp.clip(entries, -bound, bound).astype(dtype)


def setup_inputs(seed: int = 0) -> dict:
    key_list = jax.random.split(jax.random.key(seed), 23)
    return {
        "tokens": centred(key_list[0], (TOKENS, D), 1.0, 6.0, ((0, 32),)),
        "segments": jax.vmap(lambda own: jnp.searchsorted(jnp.cumsum(ragged(own, DOCS, TOK_DEV, TOK_DEV // 2, 1)), jnp.arange(TOK_DEV), side="right"))(jax.random.split(key_list[1], SEQS)).reshape((SEQS, TOK_DEV)).astype(jnp.int32),
        "cotangent": centred(key_list[2], (TOKENS, D), 1.0, 6.0, ((0, 32),)),
        "timestep_norm_gain": jnp.clip(1.0 + 0.1 * jax.random.normal(key_list[3], (D,), jnp.float32), 0.5, 1.5),
        "ema_alpha": jnp.clip(0.05 + 0.9 * jax.random.uniform(key_list[4], (D, NDIM), jnp.float32) ** levels(key_list[4], (D, NDIM), ((0, 4),), -0.2, 0.2), 0.05, 0.95),
        "ema_delta": jnp.clip(0.05 + 0.9 * jax.random.uniform(key_list[5], (D, NDIM), jnp.float32) ** levels(key_list[5], (D, NDIM), ((0, 4),), -0.2, 0.2), 0.05, 0.95),
        "ema_theta": jnp.clip(jax.random.uniform(key_list[6], (D, NDIM), jnp.float32, -1.0, 1.0) * levels(key_list[6], (D, NDIM), ((0, 4),), -0.4, 0.0), -1.0, 1.0),
        "ema_beta": centred(key_list[7], (D, NDIM), 1.0, 3.0, ((0, 4),), jnp.float32),
        "eta_real": centred(key_list[8], (D, NDIM), 0.25, 1.0, ((0, 4),), jnp.float32),
        "eta_imag": centred(key_list[9], (D, NDIM), 0.25, 1.0, ((0, 4),), jnp.float32),
        "ema_omega": centred(key_list[10], (D,), 0.5, 2.0, ((0, 4),), jnp.float32),
        "w_shared": centred(key_list[11], (D, Z), D ** -0.5, 0.1875, ((0, 4),)),
        "q_gain": jnp.clip(1.0 + 0.1 * jax.random.normal(key_list[12], (Z,), jnp.float32), 0.5, 1.5),
        "q_bias": centred(key_list[13], (Z,), 0.5, 2.0, (), jnp.float32),
        "k_gain": jnp.clip(1.0 + 0.1 * jax.random.normal(key_list[14], (Z,), jnp.float32), 0.5, 1.5),
        "w_attgate": centred(key_list[15], (D, V), D ** -0.5, 0.1875, ((1, 4),)),
        "w_value": centred(key_list[16], (D, V), D ** -0.5, 0.1875, ((1, 4),)),
        "w_attout": centred(key_list[17], (V, D), (V // 32) ** -0.5, 0.75, ((0, 4),)),
        "rms_gain": jnp.clip(1.0 + 0.1 * jax.random.normal(key_list[18], (D,), jnp.float32), 0.5, 1.5),
        "w_gate": centred(key_list[19], (D, FF), D ** -0.5, 0.1875, ((1, 4),)),
        "w_up": centred(key_list[20], (D, FF), D ** -0.5, 0.1875, ((1, 4),)),
        "w_down": centred(key_list[21], (FF, D), (FF // 4) ** -0.5, 0.25, ((0, 4),)),
    }


@jax.custom_vjp
def low(v):
    return lax.optimization_barrier(v.astype(jnp.bfloat16)).astype(jnp.float32)

@jax.custom_vjp
def low_back(v):
    return v

def low_keep(v):
    return (low(v), None)

def low_pass(kept, grad):
    return (grad,)

def back_keep(v):
    return (v, None)

def back_low(kept, grad):
    return (low(grad),)
low.defvjp(low_keep, low_pass)
low_back.defvjp(back_keep, back_low)
epsilon = 1e-05
masked_score = -1000000000.0

def matmul(left, right):
    return jnp.dot(left, right, precision=lax.Precision.HIGHEST, preferred_element_type=jnp.float32)

def decay_filter(signal, seg_row, ema_alpha, ema_delta, ema_theta, ema_beta, eta_real, eta_imag):
    magnitude = 1.0 - ema_alpha * ema_delta
    root_real = magnitude * jnp.cos(ema_theta)
    root_imag = magnitude * jnp.sin(ema_theta)
    scaled = ema_alpha * ema_beta
    same_doc = (seg_row[1:] == seg_row[:-1]).astype(jnp.float32)
    carry_flags = jnp.concatenate([jnp.zeros((1,), jnp.float32), same_doc])

    def advance(state, item):
        state_real, state_imag = state
        column, flag = item
        next_real = flag * (root_real * state_real - root_imag * state_imag) + scaled * column[:, None]
        next_imag = flag * (root_real * state_imag + root_imag * state_real)
        emitted = lax.optimization_barrier(jnp.sum(eta_real * next_real - eta_imag * next_imag, axis=1))
        return ((next_real, next_imag), emitted)
    zero_state = jnp.zeros(ema_alpha.shape, jnp.float32)
    _, result = lax.scan(advance, (zero_state, zero_state), (signal, carry_flags))
    return result

def layer(layer_inputs, seg_row, params):
    timestep_norm_gain, ema_alpha, ema_delta, ema_theta, ema_beta, eta_real, eta_imag, ema_omega, w_shared, q_gain, q_bias, k_gain, w_attgate, w_value, w_attout, rms_gain, w_gate, w_up, w_down = params
    places = jnp.arange(TOK_DEV)
    allowed = (seg_row[:, None] == seg_row[None, :]) & (places[:, None] >= places[None, :])
    weights = allowed.astype(jnp.float32)
    counts = lax.optimization_barrier(jnp.sum(weights, axis=1)) * D
    first_sum = matmul(weights, lax.optimization_barrier(jnp.sum(layer_inputs, axis=1)))
    second_sum = matmul(weights, lax.optimization_barrier(jnp.sum(layer_inputs * layer_inputs, axis=1)))
    running_mean = first_sum / counts
    inverse_deviation = lax.rsqrt(second_sum / counts - running_mean * running_mean + epsilon)
    standardized_input = (layer_inputs - running_mean[:, None]) * inverse_deviation[:, None]
    normed_output = standardized_input * timestep_norm_gain
    filtered = decay_filter(normed_output, seg_row, ema_alpha, ema_delta, ema_theta, ema_beta, eta_real, eta_imag) + ema_omega * normed_output
    mixed = low(jax.nn.silu(filtered))
    normed_low = low(normed_output)
    value_pre = low_back(matmul(normed_low, w_value))
    values = low(jax.nn.silu(value_pre))
    gate_pre = low_back(matmul(mixed, w_attgate))
    shared = low_back(matmul(mixed, w_shared))
    queries = low(shared * q_gain + q_bias)
    keys = low(shared * k_gain)
    scores = jnp.where(allowed, matmul(queries, keys.T) * (1.0 / math.sqrt(Z)), masked_score)
    probs = low(jax.nn.softmax(scores, axis=1))
    attended = low_back(matmul(probs, values))
    product = low(attended * jax.nn.silu(gate_pre))
    branch = low_back(matmul(product, w_attout))
    resid = layer_inputs + branch
    scale_rms = lax.rsqrt(lax.optimization_barrier(jnp.mean(resid * resid, axis=1, keepdims=True)) + epsilon)
    resid_low = low(resid * scale_rms * rms_gain)
    gate = low_back(matmul(resid_low, w_gate))
    up_proj = low_back(matmul(resid_low, w_up))
    hidden = low(jax.nn.silu(gate) * up_proj)
    return resid + matmul(hidden, w_down)

def reference(tokens, segments, cotangent, timestep_norm_gain, ema_alpha, ema_delta, ema_theta, ema_beta, eta_real, eta_imag, ema_omega, w_shared, q_gain, q_bias, k_gain, w_attgate, w_value, w_attout, rms_gain, w_gate, w_up, w_down):
    params = tuple((entry.astype(jnp.float32) for entry in (timestep_norm_gain, ema_alpha, ema_delta, ema_theta, ema_beta, eta_real, eta_imag, ema_omega, w_shared, q_gain, q_bias, k_gain, w_attgate, w_value, w_attout, rms_gain, w_gate, w_up, w_down)))
    stacked = tokens.astype(jnp.float32).reshape(SEQS, TOK_DEV, D)
    pulled = cotangent.astype(jnp.float32).reshape(SEQS, TOK_DEV, D)

    def one_sequence(totals, entry):
        block_in, seg_row, cot_block = entry

        def forward(layer_inputs, weights):
            return layer(layer_inputs, seg_row, weights)
        result, pull = jax.vjp(forward, block_in, params)
        grad_inputs, grad_weights = pull(cot_block)
        totals = jax.tree.map(lambda left, right: left + right, totals, grad_weights)
        return (totals, (result.astype(jnp.bfloat16), grad_inputs.astype(jnp.bfloat16)))
    initial = jax.tree.map(jnp.zeros_like, params)
    grads, (outputs, input_grads) = lax.scan(one_sequence, initial, (stacked, segments, pulled))
    return (outputs.reshape(TOKENS, D), input_grads.reshape(TOKENS, D), grads[0], grads[1], grads[2], grads[3], grads[4], grads[5], grads[6], grads[7], grads[8], grads[9], grads[10], grads[11], grads[12], grads[13], grads[14], grads[15], grads[16], grads[17], grads[18])
```

```python
import functools
import math
import types

import jax
import jax.numpy as jnp
from jax import lax
from jax.experimental import pallas as pl
from jax.experimental.pallas import tpu as pltpu
from jax.sharding import PartitionSpec as P

epsilon = 1e-05
masked_score = -1000000000.0
f32 = jnp.float32
bf16 = jnp.bfloat16
MESH = pl.DeviceIdType.MESH
LANES = 128
SUB = 8
SPAN = 64
MAX_DOC = 512
PACK_TAIL = 32
VMEM_BYTES = 60 * 2**20


def plain(left, right):
    return jnp.dot(left, right, preferred_element_type=f32)


def cross(left, right):
    return lax.dot_general(
        left, right, (((1,), (1,)), ((), ())), preferred_element_type=f32
    )


def inner(left, right):
    return lax.dot_general(
        left, right, (((0,), (0,)), ((), ())), preferred_element_type=f32
    )


def sigmoid(value):
    return 1.0 / (1.0 + jnp.exp(-value))


def at(index, size):
    return pl.ds(pl.multiple_of(index * size, size), size)


class Stage:
    def __init__(self, ins, outs, scratch, refs):
        self.pending = {}
        self.flushed = []
        count = len(ins)
        self.hbm_in = dict(zip(ins, refs[:count]))
        self.hbm_out = dict(zip(outs, refs[count : count + len(outs)]))
        rest = refs[count + len(outs) :]
        names = list(ins) + list(outs) + list(scratch)
        self.refs = dict(zip(names, rest[: len(names)]))
        self.load_sem, self.flush_sem, self.send_sem, self.recv_sem = rest[len(names) :]
        self.order = {name: k for k, name in enumerate(ins)}
        self.out_order = {name: k for k, name in enumerate(outs)}
        self.used = 0
        self.names = {id(ref): name for name, ref in self.refs.items()}

    def __getitem__(self, name):
        return self.refs[name]

    def __getattr__(self, name):
        return self.refs[name]

    def load(self, *refs):
        for name in [self.names[id(ref)] for ref in refs]:
            copy = pltpu.make_async_copy(
                self.hbm_in[name], self.refs[name], self.load_sem.at[self.order[name]]
            )
            copy.start()
            self.pending[name] = copy

    def need(self, *refs):
        for name in [self.names[id(ref)] for ref in refs]:
            copy = self.pending.pop(name, None)
            if copy is not None:
                copy.wait()

    def flush(self, *refs):
        for name in [self.names[id(ref)] for ref in refs]:
            copy = pltpu.make_async_copy(
                self.refs[name], self.hbm_out[name], self.flush_sem.at[self.out_order[name]]
            )
            copy.start()
            self.flushed.append(copy)

    def close(self):
        for copy in self.flushed:
            copy.wait()

    def sems(self, count):
        first = self.used
        self.used += count
        return first

    def remote(self, source, target_ref, index, device):
        return pltpu.make_async_remote_copy(
            src_ref=source,
            dst_ref=target_ref,
            send_sem=self.send_sem.at[index],
            recv_sem=self.recv_sem.at[index],
            device_id=device,
            device_id_type=MESH,
        )


def run_stage(body, ins, outs, scratch, sems, collective):
    ins = vars(ins)

    def kernel(*refs):
        body(Stage(list(ins), list(outs), list(scratch), refs))

    buffers = [pltpu.VMEM(array.shape, array.dtype) for array in ins.values()]
    buffers += [pltpu.VMEM(shape, kind) for shape, kind in outs.values()]
    buffers += [pltpu.VMEM(shape, kind) for shape, kind in scratch.values()]
    results = pl.pallas_call(
        kernel,
        out_shape=tuple(jax.ShapeDtypeStruct(shape, kind) for shape, kind in outs.values()),
        in_specs=[pl.BlockSpec(memory_space=pl.ANY)] * len(ins),
        out_specs=tuple(pl.BlockSpec(memory_space=pl.ANY) for _ in outs),
        scratch_shapes=buffers
        + [
            pltpu.SemaphoreType.DMA((len(ins),)),
            pltpu.SemaphoreType.DMA((len(outs),)),
            pltpu.SemaphoreType.DMA((sems,)),
            pltpu.SemaphoreType.DMA((sems,)),
        ],
        compiler_params=pltpu.CompilerParams(
            collective_id=collective, has_side_effects=True, vmem_limit_bytes=VMEM_BYTES
        ),
    )(*ins.values())
    return types.SimpleNamespace(**dict(zip(outs, results)))


class Group:
    def __init__(self):
        self.me = lax.axis_index("tensor")
        chip = self.me // 2
        core = self.me % 2
        self.sib = chip * 2 + (1 - core)
        self.opp = (1 - chip) * 2 + core
        self.diag = (1 - chip) * 2 + (1 - core)

    def greet(self):
        barrier = pltpu.get_barrier_semaphore()
        for device in (self.sib, self.opp, self.diag):
            pl.semaphore_signal(barrier, inc=1, device_id={"tensor": device}, device_id_type=MESH)
        pl.semaphore_wait(barrier, 3)


class Gather:
    def __init__(self, stage, group, source, place, pieces):
        self.g = group
        self.pieces = pieces
        base = stage.sems(3 * pieces)
        opp = {"tensor": group.opp}
        sib = {"tensor": group.sib}
        self.to_opp = [
            stage.remote(source(s), place(group.me, s), base + s, opp) for s in range(pieces)
        ]
        self.to_sib = [
            stage.remote(source(s), place(group.me, s), base + pieces + s, sib)
            for s in range(pieces)
        ]
        self.passed = [
            stage.remote(place(group.opp, s), place(group.opp, s), base + 2 * pieces + s, sib)
            for s in range(pieces)
        ]

    def send(self, s):
        self.to_opp[s].start()
        self.to_sib[s].start()

    def forward(self, s):
        self.to_opp[s].wait_recv()
        self.passed[s].start()

    def near(self):
        for s in range(self.pieces):
            self.to_sib[s].wait_recv()

    def far(self):
        for s in range(self.pieces):
            self.passed[s].wait_recv()

    def close(self):
        for copy in self.to_opp + self.to_sib + self.passed:
            copy.wait_send()


class Scatter:
    def __init__(self, stage, group, name, pieces, order=None):
        self.order = list(order or range(pieces))
        self.out_diag = stage[name + "_od"]
        self.out_sib = stage[name + "_os"]
        self.out_opp = stage[name + "_oo"]
        self.in_opp = stage[name + "_io"]
        self.in_own = stage[name + "_iw"]
        self.in_far = stage[name + "_if"]
        self.rows = self.out_diag.shape[0] // pieces
        base = stage.sems(3 * pieces)

        def copies(source, target, first, device):
            return [
                stage.remote(
                    source.at[self.part(s)], target.at[self.part(s)], first + s, {"tensor": device}
                )
                for s in range(pieces)
            ]

        self.first = copies(self.out_diag, self.in_opp, base, group.sib)
        self.second = copies(self.out_sib, self.in_own, base + pieces, group.sib)
        self.across = copies(self.out_opp, self.in_far, base + 2 * pieces, group.opp)

    def part(self, s):
        return pl.ds(s * self.rows, self.rows)

    def put_diag(self, value):
        for s in self.order:
            self.out_diag[self.part(s), :] = value(s).astype(bf16)
            self.first[s].start()

    def put_opp(self, value):
        for s in self.order:
            mine = value(s)
            self.first[s].wait_recv()
            total = mine + self.in_opp[self.part(s), :].astype(f32)
            self.out_opp[self.part(s), :] = total.astype(bf16)
            self.across[s].start()

    def put_sib(self, value):
        for s in self.order:
            self.out_sib[self.part(s), :] = value(s).astype(bf16)
            self.second[s].start()

    def take(self, s, own):
        self.second[s].wait_recv()
        near = own + self.in_own[self.part(s), :].astype(f32)
        self.across[s].wait_recv()
        return near + self.in_far[self.part(s), :].astype(f32)

    def close(self):
        for copy in self.first + self.second + self.across:
            copy.wait_send()


def pieces_of(value, count):
    rows = value.shape[0] // count
    return lambda s: value[s * rows : (s + 1) * rows]


def scatter_buffers(name, rows, width):
    return {
        name + tail: ((rows, width), bf16) for tail in ("_od", "_os", "_oo", "_io", "_iw", "_if")
    }


def ring_seats(count):
    index = lax.axis_index("dp")
    place = jnp.where(index % 2 == 0, index // 2, count - 1 - index // 2)

    def seat(p):
        p = lax.rem(p + 2 * count, count)
        return jnp.where(2 * p < count, 2 * p, 2 * (count - 1 - p) + 1)

    return place, seat


def ring_rows(shape, kind, count):
    tile = 16 if kind == bf16 else SUB
    if shape[0] % (2 * count * tile) == 0:
        return shape[0] // (2 * count), shape[1]
    if shape[0] % (count * tile) == 0 and shape[1] % (2 * LANES) == 0:
        return shape[0] // count, shape[1] // 2
    return None


class Ring:
    def __init__(self, m, count, items):
        self.m = m
        self.count = count
        self.items = items
        self.place, self.seat = ring_seats(count)
        self.steps = 2 * (count - 1)
        self.base = m.sems(len(items) * 2 * self.steps)
        self.sent = []

    def greet(self, barrier):
        for step in (-1, 1):
            device = self.seat(self.place + step)
            pl.semaphore_signal(barrier, inc=1, device_id={"dp": device}, device_id_type=MESH)

    def view(self, ref, chunk, way):
        shape = ref.shape
        rows, columns = ring_rows(shape, ref.dtype, self.count)
        chunk = lax.rem(chunk + 2 * self.count, self.count)
        if columns == shape[1]:
            return ref.at[pl.ds(pl.multiple_of((2 * chunk + way) * rows, rows), rows), :]
        return ref.at[
            pl.ds(pl.multiple_of(chunk * rows, rows), rows), pl.ds(way * columns, columns)
        ]

    def copy(self, item, way, step):
        own, box, total = self.items[item]
        sign = 1 - 2 * way
        last = self.count - 1
        index = self.base + (2 * item + way) * self.steps + step
        if step < last:
            source = self.view(own, self.place, way) if step == 0 else box.at[way, step - 1]
            target = box.at[way, step]
        else:
            source = self.view(total, self.place + sign - sign * (step - last), way)
            target = source
        return self.m.remote(source, target, index, {"dp": self.seat(self.place + sign)})

    def start(self, item, way, step):
        copy = self.copy(item, way, step)
        copy.start()
        self.sent.append(copy)

    def begin(self):
        for item in range(len(self.items)):
            for way in range(2):
                self.start(item, way, 0)

    def tick(self, step):
        last = self.count - 1
        for item, (own, box, total) in enumerate(self.items):
            for way in range(2):
                sign = 1 - 2 * way
                self.copy(item, way, step).wait_recv()
                if step < last:
                    chunk = self.place - sign * (step + 1)
                    value = box[way, step].astype(f32) + self.view(own, chunk, way)[...].astype(f32)
                    if step < last - 1:
                        box[way, step] = value.astype(box.dtype)
                    else:
                        self.view(total, chunk, way)[...] = value.astype(total.dtype)
                if step + 1 < self.steps:
                    self.start(item, way, step + 1)

    def close(self):
        for copy in self.sent:
            copy.wait_send()


def ring_box(shape, kind, count):
    rows, columns = ring_rows(shape, kind, count)
    return ((2, count - 1, rows, columns), kind)


def run_ring(arrays, count, collective):
    names = list(arrays)
    outs = {name + "t": (array.shape, array.dtype) for name, array in arrays.items()}
    scratch = {name + "b": ring_box(a.shape, a.dtype, count) for name, a in arrays.items()}

    def body(m):
        refs = [(m[name], m[name + "b"], m[name + "t"]) for name in names]
        m.load(*[own for own, _, _ in refs])
        ring = Ring(m, count, refs)
        barrier = pltpu.get_barrier_semaphore()
        ring.greet(barrier)
        pl.semaphore_wait(barrier, 2)
        m.need(*[own for own, _, _ in refs])
        ring.begin()
        for step in range(ring.steps):
            ring.tick(step)
        for _, _, total in refs:
            m.flush(total)
        ring.close()
        m.close()

    sems = len(names) * 4 * (count - 1)
    done = run_stage(
        body, types.SimpleNamespace(**arrays), outs, scratch, sems, collective
    )
    return [getattr(done, name + "t") for name in names]


def sum_over_dp(arrays, collective):
    count = lax.axis_size("dp")
    if count > 1 and count % 2 == 0 and all(
        ring_rows(a.shape, a.dtype, count) for a in arrays.values()
    ):
        return run_ring(arrays, count, collective)
    return lax.psum([array.astype(f32) for array in arrays.values()], "dp")


def tables_of(ema_alpha, ema_delta, ema_theta, ema_beta, eta_real, eta_imag):
    magnitude = 1.0 - ema_alpha * ema_delta
    cosine, sine = jnp.cos(ema_theta), jnp.sin(ema_theta)
    scaled = ema_alpha * ema_beta
    stacked = jnp.stack(
        [
            magnitude * cosine,
            magnitude * sine,
            scaled * eta_real,
            scaled * eta_imag,
            cosine,
            sine,
            ema_alpha,
            ema_delta,
            ema_beta,
            eta_real,
            eta_imag,
        ]
    )
    return jnp.swapaxes(stacked, 1, 2)


def groups(array):
    halves = array.shape[0] // SUB
    sides = array.shape[1] // LANES
    return [
        array[SUB * s : SUB * s + SUB, LANES * l : LANES * l + LANES]
        for s in range(halves)
        for l in range(sides)
    ]


def spread_row(ref, index):
    return jnp.broadcast_to(ref[index], (SUB, LANES))


def advance(state, coefs, keep, signals, sides):
    root_real, root_imag = coefs
    half = len(state) // 2
    kept = [value * keep for value in state]
    fresh = [None] * len(state)
    for g in range(half):
        a_real, a_imag = kept[g], kept[half + g]
        fresh[g] = (root_real[g] * a_real - root_imag[g] * a_imag) + signals[g % sides]
        fresh[half + g] = root_real[g] * a_imag + root_imag[g] * a_real
    return kept, fresh


def filter_forward(m, first, count, state):
    sides = m.xl.shape[0]
    tables = m.tab
    root_real, root_imag = groups(tables[0]), groups(tables[1])
    out_real, out_imag = groups(tables[2]), groups(tables[3])
    half = len(root_real)
    unroll = 16

    def chunk(ch, state):
        for g in range(2 * half):
            m.st[ch, g] = state[g]

        def steps(i, state):
            state = list(state)
            for j in range(unroll):
                t = ch * SPAN + i * unroll + j
                keep = spread_row(m.kf, (pl.ds(t, 1), slice(None)))
                signals = [
                    spread_row(m.xl, (l, pl.ds(t, 1), slice(None))) for l in range(sides)
                ]
                _, state = advance(state, (root_real, root_imag), keep, signals, sides)
                for l in range(sides):
                    total = None
                    for g in range(l, half, sides):
                        term = out_real[g] * state[g] - out_imag[g] * state[half + g]
                        total = term if total is None else total + term
                    m.part[l, pl.ds(pl.multiple_of((i * unroll + j) * SUB, SUB), SUB), :] = total
            return tuple(state)

        state = lax.fori_loop(0, SPAN // unroll, steps, state)
        rows = at(ch, SPAN)
        for l in range(sides):
            lanes = slice(LANES * l, LANES * l + LANES)
            value = m.om[:, lanes] * m.xl[l, rows, :]
            for s in range(SUB):
                value = value + m.part[l, pl.ds(s, SPAN, stride=SUB), :]
            gate = sigmoid(value)
            m.mxl[rows, lanes] = (value * gate).astype(bf16)
            m.se[rows, lanes] = gate * (1.0 + value * (1.0 - gate))
        return state

    return lax.fori_loop(first, first + count, chunk, state)


def window_mask(m, first_row, rows, first_key, keys):
    same = m.segc[pl.ds(pl.multiple_of(first_row, LANES), rows), :] == m.segr[
        :, pl.ds(pl.multiple_of(first_key, LANES), keys)
    ]
    row = first_row + lax.broadcasted_iota(jnp.int32, (rows, keys), 0)
    key = first_key + lax.broadcasted_iota(jnp.int32, (rows, keys), 1)
    return same & (row >= key)


def window_of(index, block, length):
    back = -(-MAX_DOC // block)
    keys = min((back + 1) * block, length)
    first = jnp.maximum(index - back, 0) * block
    first = jnp.minimum(first, length - keys)
    return pl.multiple_of(first, LANES), keys


def body_a(m):
    g = Group()
    length, width = m.xt.shape
    block = m.tok.shape[0]
    blocks = length // block
    channels = m.mxl.shape[1]
    sides = channels // LANES
    m.load(m.tok, m.wsh, m.kf, m.segc, m.segr, m.gain, m.tab, m.om, m.wv, m.cot, m.wag)
    m.load(m.qg, m.qb, m.kg, m.wo, m.rg)
    g.greet()

    own = at(g.me, block)
    half = block // 2
    tokens = Gather(
        m, g,
        lambda s: m.tok.at[pl.ds(s * half, half), :],
        lambda j, s: m.xt.at[pl.ds(pl.multiple_of(j * block + s * half, half), half), :],
        2,
    )
    shared = Gather(m, g, lambda s: m.wsh, lambda j, s: m.wsf.at[at(j, channels), :], 1)
    pieces = 4
    rows_piece = length // pieces
    mixed = Gather(
        m, g,
        lambda s: m.mxl.at[pl.ds(s * rows_piece, rows_piece), :],
        lambda j, s: m.mx.at[pl.ds(s * rows_piece, rows_piece), at(j, channels)],
        pieces,
    )
    cots = Gather(
        m, g,
        lambda s: m.cot.at[pl.ds(s * half, half), :],
        lambda j, s: m.cotf.at[pl.ds(pl.multiple_of(j * block + s * half, half), half), :],
        2,
    )
    normed = Gather(
        m, g,
        lambda s: m.yno.at[pl.ds(s * half, half), :],
        lambda j, s: m.yn.at[pl.ds(pl.multiple_of(j * block + s * half, half), half), :],
        2,
    )
    branch = Scatter(m, g, "br", 2)

    m.need(m.tok, m.wsh)
    tokens.send(0)
    tokens.send(1)
    shared.send(0)
    m.xt[own, :] = m.tok[...]
    m.wsf[at(g.me, channels), :] = m.wsh[...]
    m.need(m.kf, m.segc, m.segr, m.gain, m.tab, m.om)

    lane = lax.broadcasted_iota(jnp.int32, (SPAN, LANES), 1)

    def sums(j):
        def part(i, _):
            rows = pl.ds(pl.multiple_of(j * block + i * SPAN, SPAN), SPAN)
            one = jnp.zeros((SPAN, LANES), f32)
            two = jnp.zeros((SPAN, LANES), f32)
            for l in range(width // LANES):
                x = m.xt[rows, LANES * l : LANES * l + LANES].astype(f32)
                one = one + x
                two = two + x * x
            picked = jnp.where(lane == 6, 1.0, 0.0)
            for k, total in ((0, one), (3, two)):
                rest = jnp.sum(total, axis=1, keepdims=True)
                for n in range(3):
                    top = rest.astype(bf16).astype(f32)
                    picked = jnp.where(lane == k + n, top, picked)
                    rest = rest - top
            m.sums[rows, :] = picked.astype(bf16)
            return 0

        lax.fori_loop(0, block // SPAN, part, 0)

    sums(g.me)
    tokens.near()
    sums(g.sib)
    tokens.forward(0)
    tokens.forward(1)
    shared.forward(0)
    sums(g.opp)
    tokens.far()
    sums(g.diag)

    lane_wide = lax.broadcasted_iota(jnp.int32, (block, LANES), 1)

    def statistics(i, _):
        first, keys = window_of(i, block, length)
        seen = window_mask(m, i * block, block, first, keys).astype(bf16)
        got = plain(seen, m.sums[pl.ds(first, keys), :])
        pick = lambda low, high: jnp.sum(
            jnp.where((lane_wide >= low) & (lane_wide < high), got, 0.0), axis=1, keepdims=True
        )
        total = pick(6, 7) * width
        mean = pick(0, 3) / total
        var = pick(3, 6) / total - mean * mean
        rows = at(i, block)
        m.mean[rows, :] = jnp.broadcast_to(mean, (block, LANES))
        m.rstd[rows, :] = jnp.broadcast_to(lax.rsqrt(var + epsilon), (block, LANES))
        m.total[rows, :] = jnp.broadcast_to(total, (block, LANES))
        return 0

    lax.fori_loop(0, blocks, statistics, 0)

    def normalise(i, _):
        rows = at(i, SPAN)
        mean, rstd = m.mean[rows, :], m.rstd[rows, :]
        for l in range(width // LANES):
            lanes = slice(LANES * l, LANES * l + LANES)
            x = m.xt[rows, lanes].astype(f32)
            m.xn[rows, lanes] = ((x - mean) * rstd * m.gain[:, lanes]).astype(bf16)
        for l in range(sides):
            lanes = pl.ds(pl.multiple_of(g.me * channels + LANES * l, LANES), LANES)
            x = m.xt[rows, lanes].astype(f32)
            m.xl[l, rows, :] = (x - mean) * rstd * m.gain[:, lanes]
        return 0

    lax.fori_loop(0, length // SPAN, normalise, 0)
    own_stat = pl.ds(pl.multiple_of(g.me * block, block), block)
    m.so[0] = m.mean[own_stat, :]
    m.so[1] = m.rstd[own_stat, :]
    m.so[2] = m.total[own_stat, :]
    m.flush(m.xn, m.xl, m.so)

    zero = jnp.zeros((SUB, LANES), f32)
    state = tuple(zero for _ in range(m.st.shape[1]))
    per = length // SPAN // pieces
    for p in range(pieces):
        state = filter_forward(m, p * per, per, state)
        mixed.send(p)
        if p >= 2:
            mixed.forward(p - 2)
    m.need(m.cot)
    cots.send(0)
    cots.send(1)
    m.flush(m.se, m.st)
    for i in range(pieces):
        m.mx[pl.ds(i * rows_piece, rows_piece), at(g.me, channels)] = m.mxl[
            pl.ds(i * rows_piece, rows_piece), :
        ]
    m.cotf[own, :] = m.cot[...]
    m.need(m.wv)

    def values(i, _):
        rows = at(i, block)
        pre = plain(m.xn[rows, :], m.wv[...])
        gate = sigmoid(pre)
        m.v[rows, :] = (pre * gate).astype(bf16)
        m.sv[rows, :] = (gate * (1.0 + pre * (1.0 - gate))).astype(bf16)
        return 0

    lax.fori_loop(0, blocks, values, 0)
    m.flush(m.v, m.sv)
    for p in range(max(pieces - 2, 0), pieces):
        mixed.forward(p)
    shared.near()
    shared.far()
    mixed.near()
    mixed.far()
    m.need(m.qg, m.qb, m.kg, m.wag, m.wo, m.rg)

    def project(i, _):
        rows = at(i, block)
        z = plain(m.mx[rows, :], m.wsf[...])
        m.z[rows, :] = z
        m.q[rows, :] = (z * m.qg[...] + m.qb[...]).astype(bf16)
        m.k[rows, :] = (z * m.kg[...]).astype(bf16)
        return 0

    lax.fori_loop(0, blocks, project, 0)
    m.flush(m.mx, m.wsf, m.z, m.q, m.k)
    scale = 1.0 / math.sqrt(m.q.shape[1])

    def attend(i):
        rows = at(i, block)
        first, keys = window_of(i, block, length)
        window = pl.ds(first, keys)
        scores = cross(m.q[rows, :], m.k[window, :]) * scale
        scores = jnp.where(window_mask(m, i * block, block, first, keys), scores, masked_score)
        expo = jnp.exp(scores - jnp.max(scores, axis=1, keepdims=True))
        prob = (expo / jnp.sum(expo, axis=1, keepdims=True)).astype(bf16)
        m.p[i] = prob
        attended = plain(prob, m.v[window, :])
        pre = plain(m.mx[rows, :], m.wag[...])
        gate = sigmoid(pre)
        swish = pre * gate
        m.r[rows, :] = swish.astype(bf16)
        m.os[rows, :] = (attended * (gate * (1.0 + pre * (1.0 - gate)))).astype(bf16)
        m.w[rows, :] = (attended * swish).astype(bf16)
        return plain(m.w[rows, :], m.wo[...])

    branch.put_diag(pieces_of(attend(g.diag), 2))
    cots.forward(0)
    cots.forward(1)
    branch.put_opp(pieces_of(attend(g.opp), 2))
    branch.put_sib(pieces_of(attend(g.sib), 2))
    m.bp[...] = attend(g.me)
    m.flush(m.p, m.r, m.os, m.w)
    for s in range(2):
        piece = pl.ds(s * half, half)
        y = branch.take(s, m.bp[piece, :]) + m.tok[piece, :].astype(f32)
        m.y[piece, :] = y
        rms = lax.rsqrt(jnp.mean(y * y, axis=1, keepdims=True) + epsilon)
        m.rs[piece, :] = jnp.broadcast_to(rms, (half, LANES))
        m.yno[piece, :] = (y * rms * m.rg[...]).astype(bf16)
        normed.send(s)
    m.yn[own, :] = m.yno[...]
    m.flush(m.y, m.rs)
    cots.near()
    cots.far()
    m.flush(m.cotf)
    normed.forward(0)
    normed.forward(1)
    normed.near()
    normed.far()
    m.flush(m.yn)
    for moved in (tokens, shared, mixed, cots, normed, branch):
        moved.close()
    m.close()


def run_a(arrays, sizes):
    length, width, block, channels, shared, values = sizes
    blocks = length // block
    keys = min((-(-MAX_DOC // block) + 1) * block, length)
    sides = channels // LANES
    states = 2 * sides * (arrays.tab.shape[1] // SUB)
    outs = dict(
        xn=((length, width), bf16),
        xl=((sides, length, LANES), f32),
        so=((3, block, LANES), f32),
        se=((length, channels), f32),
        st=((length // SPAN, states, SUB, LANES), f32),
        mx=((length, width), bf16),
        v=((length, values), bf16),
        sv=((length, values), bf16),
        z=((length, shared), f32),
        q=((length, shared), bf16),
        k=((length, shared), bf16),
        wsf=((width, shared), bf16),
        p=((blocks, block, keys), bf16),
        r=((length, values), bf16),
        os=((length, values), bf16),
        w=((length, values), bf16),
        y=((block, width), f32),
        rs=((block, LANES), f32),
        yn=((length, width), bf16),
        cotf=((length, width), bf16),
    )
    scratch = dict(
        xt=((length, width), bf16),
        sums=((length, LANES), bf16),
        mean=((length, LANES), f32),
        rstd=((length, LANES), f32),
        total=((length, LANES), f32),
        part=((sides, SPAN * SUB, LANES), f32),
        mxl=((length, channels), bf16),
        bp=((block, width), f32),
        yno=((block, width), bf16),
        **scatter_buffers("br", block, width),
    )
    return run_stage(body_a, arrays, outs, scratch, 64, 1)


def transposed_product(m, left, right, out, step):
    def part(i, _):
        columns = at(i, step)
        out[columns, :] = inner(left[:, columns], right[...]).astype(bf16)
        return 0

    lax.fori_loop(0, left.shape[1] // step, part, 0)
    m.flush(out)


def body_b(m):
    g = Group()
    length, width = m.yn.shape
    block = m.y.shape[0]
    half = block // 2
    m.load(m.yn, m.wg, m.wu, m.wd, m.cotf, m.y, m.rs, m.cot, m.rg)
    g.greet()
    grads = Scatter(m, g, "dy", 2)
    fed = Scatter(m, g, "ff", 2)
    back = Gather(
        m, g,
        lambda s: m.dyo.at[pl.ds(s * half, half), :],
        lambda j, s: m.dyf.at[pl.ds(pl.multiple_of(j * block + s * half, half), half), :],
        2,
    )
    m.need(m.yn, m.wg, m.wu, m.wd, m.cotf)

    def feed(j):
        rows = at(j, block)
        low = m.yn[rows, :]
        gate = plain(low, m.wg[...])
        up = plain(low, m.wu[...])
        d_act = cross(m.cotf[rows, :], m.wd[...])
        sig = sigmoid(gate)
        swish = gate * sig
        m.act[rows, :] = (swish * up).astype(bf16)
        m.dg[rows, :] = (d_act * up * (sig * (1.0 + gate * (1.0 - sig)))).astype(bf16)
        m.du[rows, :] = (d_act * swish).astype(bf16)
        return cross(m.dg[rows, :], m.wg[...]) + cross(m.du[rows, :], m.wu[...])

    grads.put_diag(pieces_of(feed(g.diag), 2))
    grads.put_opp(pieces_of(feed(g.opp), 2))
    grads.put_sib(pieces_of(feed(g.sib), 2))
    m.bp[...] = feed(g.me)
    transposed_product(m, m.act, m.cotf, m.gd, LANES)
    m.need(m.y, m.rs, m.cot, m.rg)
    gain_sum = jnp.zeros((1, width), f32)
    for s in range(2):
        piece = pl.ds(s * half, half)
        d_yn = grads.take(s, m.bp[piece, :])
        rms = m.rs[piece, :][:, :1]
        hat = m.y[piece, :] * rms
        gain_sum = gain_sum + jnp.sum(d_yn * hat, axis=0, keepdims=True)
        d_hat = d_yn * m.rg[...]
        pull = d_hat - hat * jnp.mean(d_hat * hat, axis=1, keepdims=True)
        dy = m.cot[piece, :].astype(f32) + rms * pull
        m.dy[piece, :] = dy
        m.dyo[piece, :] = dy.astype(bf16)
        back.send(s)
    m.gr[...] = gain_sum
    m.dyf[at(g.me, block), :] = m.dyo[...]
    m.flush(m.dy, m.gr)
    share = lambda j: plain(m.act[at(j, block), :], m.wd[...])
    fed.put_diag(pieces_of(share(g.diag), 2))
    fed.put_opp(pieces_of(share(g.opp), 2))
    fed.put_sib(pieces_of(share(g.sib), 2))
    m.bp[...] = share(g.me)
    transposed_product(m, m.yn, m.dg, m.gg, 2 * LANES)
    back.forward(0)
    back.forward(1)
    transposed_product(m, m.yn, m.du, m.gu, 2 * LANES)
    back.near()
    back.far()
    m.flush(m.dyf)
    for s in range(2):
        piece = pl.ds(s * half, half)
        m.out[piece, :] = (fed.take(s, m.bp[piece, :]) + m.y[piece, :]).astype(bf16)
    m.flush(m.out)
    for moved in (grads, fed, back):
        moved.close()
    m.close()


def run_b(arrays, sizes):
    length, width, block, units = sizes
    outs = dict(
        gd=((units, width), bf16),
        gg=((width, units), bf16),
        gu=((width, units), bf16),
        dy=((block, width), f32),
        gr=((1, width), f32),
        dyf=((length, width), bf16),
        out=((block, width), bf16),
    )
    scratch = dict(
        act=((length, units), bf16),
        dg=((length, units), bf16),
        du=((length, units), bf16),
        bp=((block, width), f32),
        dyo=((block, width), bf16),
        **scatter_buffers("dy", block, width),
        **scatter_buffers("ff", block, width),
    )
    return run_stage(body_b, arrays, outs, scratch, 32, 2)


def filter_backward(m, last, count, gamma):
    sides = m.xl.shape[0]
    tables = m.tab
    root_real, root_imag = groups(tables[0]), groups(tables[1])
    out_real, out_imag = groups(tables[2]), groups(tables[3])
    half = len(root_real)
    unroll = 16

    def chunk(step, gamma):
        ch = last - step

        def again(i, state):
            state = list(state)
            for j in range(unroll):
                local = i * unroll + j
                t = ch * SPAN + local
                keep = spread_row(m.kf, (pl.ds(t, 1), slice(None)))
                signals = [
                    spread_row(m.xl, (l, pl.ds(t, 1), slice(None))) for l in range(sides)
                ]
                kept, state = advance(state, (root_real, root_imag), keep, signals, sides)
                for g in range(2 * half):
                    m.kept[local, g] = kept[g]
            return tuple(state)

        lax.fori_loop(0, SPAN // unroll, again, tuple(m.st[ch, g] for g in range(2 * half)))

        def reverse(i, carry):
            gamma, sums = list(carry[: 2 * half]), list(carry[2 * half :])
            for j in range(unroll):
                local = SPAN - 1 - (i * unroll + j)
                t = ch * SPAN + local
                keep = spread_row(m.kf, (pl.ds(t + 1, 1), slice(None)))
                signals = [
                    spread_row(m.de, (l, pl.ds(t, 1), slice(None))) for l in range(sides)
                ]
                _, gamma = advance(gamma, (root_real, root_imag), keep, signals, sides)
                for l in range(sides):
                    total = None
                    for g in range(l, half, sides):
                        g_real, g_imag = gamma[g], gamma[half + g]
                        a_real, a_imag = m.kept[local, g], m.kept[local, half + g]
                        term = out_real[g] * g_real - out_imag[g] * g_imag
                        total = term if total is None else total + term
                        sums[g] = sums[g] + (g_real * a_real - g_imag * a_imag)
                        sums[half + g] = sums[half + g] + (g_real * a_imag + g_imag * a_real)
                        sums[2 * half + g] = sums[2 * half + g] + signals[l] * a_real
                        sums[3 * half + g] = sums[3 * half + g] + signals[l] * a_imag
                    m.part[l, pl.ds(pl.multiple_of(local * SUB, SUB), SUB), :] = total
            return tuple(gamma) + tuple(sums)

        start = tuple(gamma) + tuple(m.acc[g] for g in range(4 * half))
        done = lax.fori_loop(0, SPAN // unroll, reverse, start)
        for g in range(4 * half):
            m.acc[g] = done[2 * half + g]
        rows = at(ch, SPAN)
        for l in range(sides):
            lanes = slice(LANES * l, LANES * l + LANES)
            signal = m.de[l, rows, :]
            value = m.om[:, lanes] * signal
            for s in range(SUB):
                value = value + m.part[l, pl.ds(s, SPAN, stride=SUB), :]
            m.dxb[rows, lanes] = value.astype(bf16)
            m.go[:, lanes] = m.go[:, lanes] + jnp.sum(
                signal * m.xl[l, rows, :], axis=0, keepdims=True
            )
        return done[: 2 * half]

    return lax.fori_loop(0, count, chunk, gamma)


def filter_gradients(m):
    sides = m.xl.shape[0]
    half = m.acc.shape[0] // 4
    dims = m.tab.shape[1]
    for g in range(half):
        s, l = g // sides, g % sides
        rows = slice(SUB * s, SUB * s + SUB)
        lanes = slice(LANES * l, LANES * l + LANES)
        q_re, q_im, c_re, c_im, cosine, sine, alpha, delta, beta, e_re, e_im = (
            m.tab[k, rows, lanes] for k in range(11)
        )
        lag_re, lag_im, sum_re, sum_im = (m.acc[k * half + g] for k in range(4))
        f_re = q_re * sum_re - q_im * sum_im + m.go[:, lanes]
        f_im = q_re * sum_im + q_im * sum_re
        scaled = alpha * beta
        d_scaled = e_re * f_re - e_im * f_im
        w_re = c_re * lag_re - c_im * lag_im
        w_im = c_re * lag_im + c_im * lag_re
        d_mag = w_re * cosine - w_im * sine
        m.pk[0 * dims + SUB * s : 0 * dims + SUB * s + SUB, lanes] = beta * d_scaled - delta * d_mag
        m.pk[1 * dims + SUB * s : 1 * dims + SUB * s + SUB, lanes] = -alpha * d_mag
        m.pk[2 * dims + SUB * s : 2 * dims + SUB * s + SUB, lanes] = -(w_re * q_im + w_im * q_re)
        m.pk[3 * dims + SUB * s : 3 * dims + SUB * s + SUB, lanes] = alpha * d_scaled
        m.pk[4 * dims + SUB * s : 4 * dims + SUB * s + SUB, lanes] = scaled * f_re
        m.pk[5 * dims + SUB * s : 5 * dims + SUB * s + SUB, lanes] = -scaled * f_im


def body_c(m):
    g = Group()
    length, width = m.dyf.shape
    block = m.tok.shape[0]
    blocks = length // block
    half = block // 2
    channels = m.se.shape[1]
    shared = m.q.shape[1]
    sides = channels // LANES
    m.load(m.dyf, m.wo, m.r, m.os, m.v, m.p, m.k, m.q, m.z, m.qg, m.kg, m.sv, m.wsf, m.wag)
    m.load(m.wv, m.w, m.mx, m.xn, m.se, m.st, m.xl, m.kf, m.tab, m.om, m.tok, m.so, m.gain)
    m.load(m.dy, m.gr, m.segc, m.segr)
    g.greet()
    pieces = 4
    dm = Scatter(m, g, "dm", pieces, range(pieces - 1, -1, -1))
    xv = Scatter(m, g, "xv", 2)
    sh = Scatter(m, g, "sh", 1)
    others = (g.sib, g.opp, g.diag)
    base = m.sems(9)
    parts = [
        m.remote(m.dxb.at[at(dev, block), :], m.dxr.at[k], base + k, {"tensor": dev})
        for k, dev in enumerate(others)
    ]
    small = [
        m.remote(m.smo, m.sm.at[g.me], base + 3 + k, {"tensor": dev})
        for k, dev in enumerate(others)
    ]
    tails = [
        m.remote(m.aro, m.ar.at[:, at(g.me, block)], base + 6 + k, {"tensor": dev})
        for k, dev in enumerate(others)
    ]

    scale = 1.0 / math.sqrt(shared)
    m.dk[...] = jnp.zeros(m.dk.shape, f32)
    m.dv[...] = jnp.zeros(m.dv.shape, f32)
    m.need(m.dyf, m.wo, m.r, m.os, m.v, m.p, m.k, m.q)

    def attend(i, _):
        rows = at(i, block)
        first, keys = window_of(i, block, length)
        window = pl.ds(first, keys)
        d_w = cross(m.dyf[rows, :], m.wo[...])
        d_o = (d_w * m.r[rows, :].astype(f32)).astype(bf16)
        m.drp[rows, :] = (d_w * m.os[rows, :].astype(f32)).astype(bf16)
        prob_low = m.p[i]
        prob = prob_low.astype(f32)
        weighed = prob * cross(d_o, m.v[window, :])
        d_s = (weighed - prob * jnp.sum(weighed, axis=1, keepdims=True)) * scale
        d_s = d_s.astype(bf16)
        m.dq[rows, :] = plain(d_s, m.k[window, :])
        m.dk[window, :] = m.dk[window, :] + inner(d_s, m.q[rows, :])
        m.dv[window, :] = m.dv[window, :] + inner(prob_low, d_o)
        return 0

    lax.fori_loop(0, blocks, attend, 0)
    m.need(m.z, m.qg, m.kg, m.sv, m.wsf, m.wag)

    def affine(i, sums):
        rows = at(i, block)
        d_q, d_k, z = m.dq[rows, :], m.dk[rows, :], m.z[rows, :]
        m.dz[rows, :] = (d_q * m.qg[...] + d_k * m.kg[...]).astype(bf16)
        m.dvp[rows, :] = (m.dv[rows, :] * m.sv[rows, :].astype(f32)).astype(bf16)
        new = (d_q * z, d_q, d_k * z)
        return tuple(s + jnp.sum(n, axis=0, keepdims=True) for s, n in zip(sums, new))

    aff = lax.fori_loop(0, blocks, affine, tuple(jnp.zeros((1, shared), f32) for _ in range(3)))
    m.smo[...] = jnp.zeros(m.smo.shape, f32)
    for n in range(3):
        m.smo[2 + n : 3 + n, :shared] = aff[n]

    def mixing(j):
        def value(s):
            rows = pl.ds(s * (length // pieces), length // pieces)
            return cross(m.dz[rows, :], m.wsf[at(j, channels), :]) + cross(
                m.drp[rows, :], m.wag[at(j, channels), :]
            )

        return value

    dm.put_diag(mixing(g.diag))
    dm.put_opp(mixing(g.opp))
    dm.put_sib(mixing(g.sib))
    m.need(m.wv)
    spread = lambda j: pieces_of(cross(m.dvp[at(j, block), :], m.wv[...]), 2)
    xv.put_diag(spread(g.diag))
    xv.put_opp(spread(g.opp))
    xv.put_sib(spread(g.sib))
    m.dxn[...] = cross(m.dvp[at(g.me, block), :], m.wv[...])
    m.need(m.w, m.mx, m.xn)
    transposed_product(m, m.w, m.dyf, m.gao, 2 * LANES)
    transposed_product(m, m.mx, m.drp, m.gag, 2 * LANES)
    transposed_product(m, m.xn, m.dvp, m.gv, 2 * LANES)
    split = lambda j: (lambda s: inner(m.mx[:, at(j, channels)], m.dz[...]))
    sh.put_diag(split(g.diag))
    sh.put_opp(split(g.opp))
    sh.put_sib(split(g.sib))
    m.shp[...] = split(g.me)(0)
    m.need(m.se, m.st, m.xl, m.kf, m.tab, m.om)
    half_states = m.acc.shape[0] // 4
    m.acc[...] = jnp.zeros(m.acc.shape, f32)
    m.go[...] = jnp.zeros(m.go.shape, f32)
    gamma = tuple(jnp.zeros((SUB, LANES), f32) for _ in range(2 * half_states))
    per = length // SPAN // pieces
    own_mix = mixing(g.me)
    for s in range(pieces - 1, -1, -1):
        rows = pl.ds(s * (length // pieces), length // pieces)
        d_e = dm.take(s, own_mix(s)) * m.se[rows, :]
        for l in range(sides):
            m.de[l, rows, :] = d_e[:, LANES * l : LANES * l + LANES]
        gamma = filter_backward(m, (s + 1) * per - 1, per, gamma)
        for k, dev in enumerate(others):

            @pl.when(dev == s)
            def _():
                parts[k].start()

    filter_gradients(m)
    base_row = m.pk.shape[0] - PACK_TAIL
    m.pk[base_row:, :] = jnp.zeros((PACK_TAIL, channels), f32)
    m.pk[base_row : base_row + 1, :] = m.go[...]
    m.gs[...] = sh.take(0, m.shp[...]).astype(bf16)
    m.flush(m.gs)
    m.need(m.tok, m.so, m.gain, m.dy, m.gr, m.segc, m.segr)
    for s in range(2):
        piece = pl.ds(s * half, half)
        m.dxn[piece, :] = xv.take(s, m.dxn[piece, :])
    own_columns = at(g.me, channels)
    m.dxn[:, own_columns] = m.dxn[:, own_columns] + m.dxb[at(g.me, block), :].astype(f32)
    for k, dev in enumerate(others):
        parts[k].wait_recv()
        columns = at(dev, channels)
        m.dxn[:, columns] = m.dxn[:, columns] + m.dxr[k].astype(f32)
    gain_sum = jnp.zeros((1, width), f32)
    lane = lax.broadcasted_iota(jnp.int32, (half, LANES), 1)
    for s in range(2):
        piece = pl.ds(s * half, half)
        mean, rstd, total = (m.so[n, piece, :][:, :1] for n in range(3))
        centred = m.tok[piece, :].astype(f32) - mean
        d_xn = m.dxn[piece, :]
        gain_sum = gain_sum + jnp.sum(d_xn * (centred * rstd), axis=0, keepdims=True)
        d_hat = d_xn * m.gain[...]
        d_var = -0.5 * rstd * rstd * rstd * jnp.sum(d_hat * centred, axis=1, keepdims=True)
        one = (-rstd * jnp.sum(d_hat, axis=1, keepdims=True) - 2.0 * mean * d_var) / total
        two = d_var / total
        m.dxn[piece, :] = d_hat * rstd + m.dy[piece, :]
        m.aw[piece, :] = jnp.where(lane == 0, one, jnp.where(lane == 1, two, 0.0))
    m.smo[0:1, :] = gain_sum
    m.smo[1:2, :] = m.gr[...]
    turned = m.aw[...].T
    for n in range(2):
        rest = turned[n : n + 1, :]
        for k in range(3):
            top = rest.astype(bf16).astype(f32)
            m.art[3 * n + k : 3 * n + k + 1, :] = top
            rest = rest - top
    m.art[6:8, :] = jnp.zeros((2, block), f32)
    m.art[8:16, :] = jnp.zeros((8, block), f32)
    m.aro[...] = m.art[...].astype(bf16)
    for copy in tails + small:
        copy.start()
    m.ar[:, at(g.me, block)] = m.aro[...]
    m.sm[g.me] = m.smo[...]
    back = -(-MAX_DOC // block)
    keys = min((back + 1) * block, length)
    first_key = pl.multiple_of(jnp.minimum(g.me * block, length - keys), LANES)
    first_row = pl.multiple_of(g.me * block, LANES)
    same = m.segc[pl.ds(first_row, block), :] == m.segr[:, pl.ds(first_key, keys)]
    row = first_row + lax.broadcasted_iota(jnp.int32, (block, keys), 0)
    key = first_key + lax.broadcasted_iota(jnp.int32, (block, keys), 1)
    seen = (same & (row <= key)).astype(bf16)
    for copy in tails:
        copy.wait_recv()
    pulled = cross(seen, m.ar[:, pl.ds(first_key, keys)])
    b_one = pulled[:, 0:1] + pulled[:, 1:2] + pulled[:, 2:3]
    b_two = pulled[:, 3:4] + pulled[:, 4:5] + pulled[:, 5:6]
    for s in range(2):
        piece = pl.ds(s * half, half)
        rows = slice(s * half, (s + 1) * half)
        x = m.tok[piece, :].astype(f32)
        m.gt[piece, :] = (m.dxn[piece, :] + b_one[rows] + 2.0 * x * b_two[rows]).astype(bf16)
    m.flush(m.gt)
    for copy in small:
        copy.wait_recv()
    total = m.sm[0]
    for j in range(1, m.sm.shape[0]):
        total = total + m.sm[j]
    per = width // channels
    for n in range(2):
        for k in range(per):
            row = base_row + 1 + n * per + k
            m.pk[row : row + 1, :] = total[n : n + 1, k * channels : (k + 1) * channels]
    for n in range(3):
        row = base_row + 1 + 2 * per + n
        m.pk[row : row + 1, :shared] = total[2 + n : 3 + n, :shared]
    m.flush(m.pk)
    for moved in (dm, xv, sh):
        moved.close()
    for copy in parts + small + tails:
        copy.wait_send()
    m.close()


def run_c(arrays, sizes):
    length, width, block, channels, shared, values = sizes
    sides = channels // LANES
    half_states = sides * (arrays.tab.shape[1] // SUB)
    outs = dict(
        gao=((values, width), bf16),
        gag=((width, values), bf16),
        gv=((width, values), bf16),
        gs=((channels, shared), bf16),
        pk=((6 * arrays.tab.shape[1] + PACK_TAIL, channels), f32),
        gt=((block, width), bf16),
    )
    scratch = dict(
        dk=((length, shared), f32),
        dv=((length, values), f32),
        dq=((length, shared), f32),
        drp=((length, values), bf16),
        dz=((length, shared), bf16),
        dvp=((length, values), bf16),
        dxn=((block, width), f32),
        shp=((channels, shared), f32),
        go=((1, channels), f32),
        acc=((4 * half_states, SUB, LANES), f32),
        kept=((SPAN, 2 * half_states, SUB, LANES), f32),
        part=((sides, SPAN * SUB, LANES), f32),
        de=((sides, length, LANES), f32),
        dxb=((length, channels), bf16),
        dxr=((3, block, channels), bf16),
        aw=((block, LANES), f32),
        art=((16, block), f32),
        aro=((16, block), bf16),
        ar=((16, length), bf16),
        smo=((SUB, width), f32),
        sm=((length // block, SUB, width), f32),
        **scatter_buffers("dm", length, channels),
        **scatter_buffers("xv", block, width),
        **scatter_buffers("sh", channels, shared),
    )
    done = run_stage(body_c, arrays, outs, scratch, 48, 3)
    done.dims = arrays.tab.shape[1]
    return done


def finish(a, b, c, shared):
    sums = sum_over_dp(
        dict(gg=b.gg, gu=b.gu, gd=b.gd, gao=c.gao, gag=c.gag, gv=c.gv, gs=c.gs, pk=c.pk), 4
    )
    gg, gu, gd, gao, gag, gv, gs, pk = (value.astype(f32) for value in sums)
    dims = c.dims
    tables = [pk[dims * k : dims * k + dims].T for k in range(6)]
    top = 6 * dims
    width = gao.shape[1]
    per = width // pk.shape[1]
    norm = pk[top + 1 : top + 1 + per].reshape(width)
    rms = pk[top + 1 + per : top + 1 + 2 * per].reshape(width)
    aff = pk[top + 1 + 2 * per :, :shared]
    return (
        b.out, c.gt, norm, *tables, pk[top], gs, aff[0], aff[1], aff[2], gag, gv, gao,
        rms, gg, gu, gd,
    )


def on_device(
    tokens,
    segments,
    cotangent,
    timestep_norm_gain,
    ema_alpha,
    ema_delta,
    ema_theta,
    ema_beta,
    eta_real,
    eta_imag,
    ema_omega,
    w_shared,
    q_gain,
    q_bias,
    k_gain,
    w_attgate,
    w_value,
    w_attout,
    rms_gain,
    w_gate,
    w_up,
    w_down,
):
    block, width = tokens.shape
    length = segments.shape[1]
    channels, dims = ema_alpha.shape
    shared = w_shared.shape[1]
    values = w_value.shape[1]
    units = w_gate.shape[1]
    tab = tables_of(ema_alpha, ema_delta, ema_theta, ema_beta, eta_real, eta_imag)
    om = ema_omega[None]
    gain, rg = timestep_norm_gain[None], rms_gain[None]
    qg, qb, kg = q_gain[None], q_bias[None], k_gain[None]
    segc, segr = segments.reshape(length, 1), segments
    keep = (segments[0, 1:] == segments[0, :-1]).astype(f32)
    keep = jnp.concatenate([jnp.zeros((1,), f32), keep, jnp.zeros((SUB,), f32)])
    kf = jnp.broadcast_to(keep[:, None], (length + SUB, LANES))
    a = run_a(
        types.SimpleNamespace(
            tok=tokens, cot=cotangent, wsh=w_shared, segc=segc, segr=segr, kf=kf, gain=gain,
            tab=tab, om=om, qg=qg, qb=qb, kg=kg, wag=w_attgate, wv=w_value, wo=w_attout, rg=rg,
        ),
        (length, width, block, channels, shared, values),
    )
    b = run_b(
        types.SimpleNamespace(
            yn=a.yn, wg=w_gate, wu=w_up, wd=w_down, cotf=a.cotf, y=a.y, rs=a.rs,
            cot=cotangent, rg=rg,
        ),
        (length, width, block, units),
    )
    c = run_c(
        types.SimpleNamespace(
            dyf=b.dyf, wo=w_attout, r=a.r, os=a.os, v=a.v, p=a.p, k=a.k,
            q=a.q, z=a.z, qg=qg, kg=kg, sv=a.sv, wsf=a.wsf, wag=w_attgate,
            wv=w_value, w=a.w, mx=a.mx, xn=a.xn, se=a.se, st=a.st, xl=a.xl,
            kf=kf, tab=tab, om=om, tok=tokens, so=a.so, gain=gain, dy=b.dy, gr=b.gr,
            segc=segc, segr=segr,
        ),
        (length, width, block, channels, shared, values),
    )
    return finish(a, b, c, shared)


def solution(mesh):
    placed = (
        P(("dp", "tensor"), None),
        P("dp", None),
        P(("dp", "tensor"), None),
        P(),
        P("tensor", None),
        P("tensor", None),
        P("tensor", None),
        P("tensor", None),
        P("tensor", None),
        P("tensor", None),
        P("tensor"),
        P("tensor", None),
        P(),
        P(),
        P(),
        P(None, "tensor"),
        P(None, "tensor"),
        P("tensor", None),
        P(),
        P(None, "tensor"),
        P(None, "tensor"),
        P("tensor", None),
    )
    return jax.shard_map(
        on_device,
        mesh=mesh,
        in_specs=placed,
        out_specs=(
            P(("dp", "tensor"), None),
            P(("dp", "tensor"), None),
            P(),
            P("tensor", None),
            P("tensor", None),
            P("tensor", None),
            P("tensor", None),
            P("tensor", None),
            P("tensor", None),
            P("tensor"),
            P("tensor", None),
            P(),
            P(),
            P(),
            P(None, "tensor"),
            P(None, "tensor"),
            P("tensor", None),
            P(),
            P(None, "tensor"),
            P(None, "tensor"),
            P("tensor", None),
        ),
        check_vma=False,
    )
```

```python
import functools
import math
import types

import jax
import jax.numpy as jnp
from jax import lax
from jax.experimental import pallas as pl
from jax.experimental.pallas import tpu as pltpu
from jax.sharding import PartitionSpec as P

epsilon = 1e-05
masked_score = -1000000000.0
f32 = jnp.float32
bf16 = jnp.bfloat16
MESH = pl.DeviceIdType.MESH
LANES = 128
SUB = 8
SPAN = 64
MAX_DOC = 512
PACK_TAIL = 32
VMEM_BYTES = 62 * 2**20


def plain(left, right):
    return jnp.dot(left, right, preferred_element_type=f32)


def cross(left, right):
    return lax.dot_general(
        left, right, (((1,), (1,)), ((), ())), preferred_element_type=f32
    )


def inner(left, right):
    return lax.dot_general(
        left, right, (((0,), (0,)), ((), ())), preferred_element_type=f32
    )


def sigmoid(value):
    return 1.0 / (1.0 + jnp.exp(-value))


def at(index, size):
    return pl.ds(pl.multiple_of(index * size, size), size)


class Stage:
    def __init__(self, ins, outs, bare, scratch, refs):
        self.pending = {}
        self.flushed = []
        count = len(ins)
        self.hbm_in = dict(zip(ins, refs[:count]))
        total = len(outs) + len(bare)
        self.hbm_out = dict(zip(list(outs) + list(bare), refs[count : count + total]))
        rest = refs[count + total :]
        names = list(ins) + list(outs) + list(scratch)
        self.refs = dict(zip(names, rest[: len(names)]))
        self.load_sem, self.flush_sem, self.send_sem, self.recv_sem = rest[len(names) :]
        self.order = {name: k for k, name in enumerate(ins)}
        self.out_order = {name: k for k, name in enumerate(self.hbm_out)}
        self.sends = self.receipts = 0
        self.names = {id(ref): name for name, ref in self.refs.items()}

    def __getitem__(self, name):
        return self.refs[name]

    def __getattr__(self, name):
        return self.refs[name]

    def load(self, *refs):
        for name in [self.names[id(ref)] for ref in refs]:
            copy = pltpu.make_async_copy(
                self.hbm_in[name], self.refs[name], self.load_sem.at[self.order[name]]
            )
            copy.start()
            self.pending[name] = copy

    def need(self, *refs):
        for name in [self.names[id(ref)] for ref in refs]:
            copy = self.pending.pop(name, None)
            if copy is not None:
                copy.wait()

    def flush(self, *refs):
        for name in [self.names[id(ref)] for ref in refs]:
            self.store(self.refs[name], name)

    def store(self, source, name):
        copy = pltpu.make_async_copy(
            source, self.hbm_out[name], self.flush_sem.at[self.out_order[name]]
        )
        copy.start()
        self.flushed.append(copy)

    def close(self):
        assert self.sends <= self.send_sem.shape[0]
        assert self.receipts <= self.recv_sem.shape[0]
        for copy in self.flushed:
            copy.wait()


    def sems(self, count, sends=None):
        first = self.sends, self.receipts
        self.sends += count if sends is None else sends
        self.receipts += count
        return first

    def remote(self, source, target_ref, base, index, device, sent=None):
        return pltpu.make_async_remote_copy(
            src_ref=source,
            dst_ref=target_ref,
            send_sem=self.send_sem.at[base[0] + (index if sent is None else sent)],
            recv_sem=self.recv_sem.at[base[1] + index],
            device_id=device,
            device_id_type=MESH,
        )


def run_stage(body, ins, outs, scratch, sems, collective, bare=()):
    ins = vars(ins)
    written = {**outs, **dict(bare)}

    def kernel(*refs):
        body(Stage(list(ins), list(outs), list(dict(bare)), list(scratch), refs))

    buffers = [pltpu.VMEM(array.shape, array.dtype) for array in ins.values()]
    buffers += [pltpu.VMEM(shape, kind) for shape, kind in outs.values()]
    buffers += [pltpu.VMEM(shape, kind) for shape, kind in scratch.values()]
    results = pl.pallas_call(
        kernel,
        out_shape=tuple(jax.ShapeDtypeStruct(shape, kind) for shape, kind in written.values()),
        in_specs=[pl.BlockSpec(memory_space=pl.ANY)] * len(ins),
        out_specs=tuple(pl.BlockSpec(memory_space=pl.ANY) for _ in written),
        scratch_shapes=buffers
        + [
            pltpu.SemaphoreType.DMA((len(ins),)),
            pltpu.SemaphoreType.DMA((len(written),)),
            pltpu.SemaphoreType.DMA((max(sems[0], 1),)),
            pltpu.SemaphoreType.DMA((max(sems[1], 1),)),
        ],
        compiler_params=pltpu.CompilerParams(
            collective_id=collective,
            has_side_effects=collective is not None,
            vmem_limit_bytes=VMEM_BYTES,
        ),
    )(*ins.values())
    return types.SimpleNamespace(**dict(zip(written, results)))


class Group:
    def __init__(self):
        self.me = lax.axis_index("tensor")
        chip = self.me // 2
        core = self.me % 2
        self.sib = chip * 2 + (1 - core)
        self.opp = (1 - chip) * 2 + core
        self.diag = (1 - chip) * 2 + (1 - core)

    def greet(self, more=()):
        barrier = pltpu.get_barrier_semaphore()
        for device in more:
            pl.semaphore_signal(barrier, inc=1, device_id={"dp": device}, device_id_type=MESH)
        for device in (self.sib, self.opp, self.diag):
            pl.semaphore_signal(barrier, inc=1, device_id={"tensor": device}, device_id_type=MESH)
        pl.semaphore_wait(barrier, 3 + len(more))


class Gather:
    def __init__(self, stage, group, source, place, pieces):
        self.g = group
        self.pieces = pieces
        base = stage.sems(3 * pieces)
        opp = {"tensor": group.opp}
        sib = {"tensor": group.sib}
        self.to_opp = [
            stage.remote(source(s), place(group.me, s), base, s, opp) for s in range(pieces)
        ]
        self.to_sib = [
            stage.remote(source(s), place(group.me, s), base, pieces + s, sib)
            for s in range(pieces)
        ]
        self.passed = [
            stage.remote(place(group.opp, s), place(group.opp, s), base, 2 * pieces + s, sib)
            for s in range(pieces)
        ]

    def send(self, s):
        self.to_opp[s].start()
        self.to_sib[s].start()

    def forward(self, s):
        self.to_opp[s].wait_recv()
        self.passed[s].start()

    def near(self):
        for s in range(self.pieces):
            self.to_sib[s].wait_recv()

    def far(self):
        for s in range(self.pieces):
            self.passed[s].wait_recv()

    def close(self):
        for copy in self.to_opp + self.to_sib + self.passed:
            copy.wait_send()


class Scatter:
    def __init__(self, stage, group, name, pieces, order=None):
        self.order = list(order or range(pieces))
        self.out_diag = stage[name + "_od"]
        self.out_sib = stage[name + "_os"]
        self.out_opp = stage[name + "_oo"]
        self.in_opp = stage[name + "_io"]
        self.in_own = stage[name + "_iw"]
        self.in_far = stage[name + "_if"]
        self.rows = self.out_diag.shape[0] // pieces
        base = stage.sems(3 * pieces)

        def copies(source, target, first, device):
            return [
                stage.remote(
                    source.at[self.part(s)], target.at[self.part(s)], base, first + s, {"tensor": device}
                )
                for s in range(pieces)
            ]

        self.first = copies(self.out_diag, self.in_opp, 0, group.sib)
        self.second = copies(self.out_sib, self.in_own, pieces, group.sib)
        self.across = copies(self.out_opp, self.in_far, 2 * pieces, group.opp)

    def part(self, s):
        return pl.ds(s * self.rows, self.rows)

    def put_diag(self, value):
        for s in self.order:
            self.out_diag[self.part(s), :] = value(s).astype(bf16)
            self.first[s].start()

    def put_opp(self, value):
        for s in self.order:
            mine = value(s)
            self.first[s].wait_recv()
            total = mine + self.in_opp[self.part(s), :].astype(f32)
            self.out_opp[self.part(s), :] = total.astype(bf16)
            self.across[s].start()

    def put_sib(self, value):
        for s in self.order:
            self.out_sib[self.part(s), :] = value(s).astype(bf16)
            self.second[s].start()

    def take(self, s, own):
        self.second[s].wait_recv()
        near = own + self.in_own[self.part(s), :].astype(f32)
        self.across[s].wait_recv()
        return near + self.in_far[self.part(s), :].astype(f32)

    def close(self):
        for copy in self.first + self.second + self.across:
            copy.wait_send()


def pieces_of(value, count):
    rows = value.shape[0] // count
    return lambda s: value[s * rows : (s + 1) * rows]


def scatter_buffers(name, rows, width):
    return {
        name + tail: ((rows, width), bf16) for tail in ("_od", "_os", "_oo", "_io", "_iw", "_if")
    }


def ring_seats(count):
    index = lax.axis_index("dp")
    place = jnp.where(index % 2 == 0, index // 2, count - 1 - index // 2)

    def seat(p):
        p = lax.rem(p + 2 * count, count)
        return jnp.where(2 * p < count, 2 * p, 2 * (count - 1 - p) + 1)

    return place, seat


def ring_rows(shape, kind, count):
    tile = 16 if kind == bf16 else SUB
    if shape[0] % (2 * count * tile) == 0:
        return shape[0] // (2 * count), shape[1]
    if shape[0] % (count * tile) == 0 and shape[1] % (2 * LANES) == 0:
        return shape[0] // count, shape[1] // 2
    return None


class Ring:
    def __init__(self, m, count, items):
        self.m = m
        self.count = count
        self.items = items
        self.place, self.seat = ring_seats(count)
        self.steps = 2 * (count - 1)
        self.base = m.sems(len(items) * 2 * count, len(items) * 2)
        self.step = 0

    def view(self, ref, chunk, way):
        shape = ref.shape
        rows, columns = ring_rows(shape, ref.dtype, self.count)
        chunk = lax.rem(chunk + 2 * self.count, self.count)
        if columns == shape[1]:
            return ref.at[pl.ds(pl.multiple_of((2 * chunk + way) * rows, rows), rows), :]
        return ref.at[
            pl.ds(pl.multiple_of(chunk * rows, rows), rows), pl.ds(way * columns, columns)
        ]

    def copy(self, item, way, step):
        own, box, _ = self.items[item]
        sign = 1 - 2 * way
        last = self.count - 1
        place = 2 * item + way
        index = place * self.count + step % self.count
        if step < last:
            source = self.view(own, self.place, way) if step == 0 else box.at[way, step - 1]
            target = box.at[way, step]
        else:
            source = self.view(own, self.place + sign - sign * (step - last), way)
            target = source
        device = {"dp": self.seat(self.place + sign)}
        return self.m.remote(source, target, self.base, index, device, place)

    def start(self, item, way, step):
        self.copy(item, way, step).start()

    def begin(self):
        for item in range(len(self.items)):
            for way in range(2):
                self.start(item, way, 0)

    def tick(self):
        last = self.count - 1
        step = self.step
        self.step = step + 1
        for item, (own, box, name) in enumerate(self.items):
            for way in range(2):
                sign = 1 - 2 * way
                self.copy(item, way, step).wait_recv()
                self.copy(item, way, step).wait_send()
                if step < last:
                    chunk = self.view(own, self.place - sign * (step + 1), way)
                    value = box[way, step].astype(f32) + chunk[...].astype(f32)
                    if step < last - 1:
                        box[way, step] = value.astype(box.dtype)
                    else:
                        chunk[...] = value.astype(own.dtype)
                if step + 1 < self.steps:
                    self.start(item, way, step + 1)
                if step >= last - 1:
                    self.keep(own, name, self.place + sign - sign * (step + 1 - last), way)
        return step + 1 == self.steps

    def keep(self, own, name, chunk, way):
        out = self.m.hbm_out[name]
        sem = self.m.flush_sem.at[self.m.out_order[name]]
        pltpu.make_async_copy(self.view(own, chunk, way), self.view(out, chunk, way), sem).start()

    def close(self):
        for own, _, name in self.items:
            sem = self.m.flush_sem.at[self.m.out_order[name]]
            pltpu.make_async_copy(own, self.m.hbm_out[name], sem).wait()


class Direct:
    def __init__(self, m, count, items):
        self.m = m
        self.count = count
        self.items = items
        self.me = lax.axis_index("dp")
        self.base = m.sems(2 * len(items) * (count - 1))
        self.step = 0

    def share(self, ref, index):
        return ref.at[at(index, ref.shape[0] // self.count), :]

    def copies(self, step):
        made = []
        for item, (own, box, total, _) in enumerate(self.items):
            for r in range(1, self.count):
                there = lax.rem(self.me + r, self.count)
                index = (2 * item + step) * (self.count - 1) + r - 1
                if step == 0:
                    source, target = self.share(own, there), box.at[r - 1]
                else:
                    source = target = self.share(total, self.me)
                made.append(self.m.remote(source, target, self.base, index, {"dp": there}))
        return made

    def begin(self):
        for copy in self.copies(0):
            copy.start()

    def tick(self):
        for copy in self.copies(self.step):
            copy.wait_recv()
        if self.step == 0:
            for own, box, total, _ in self.items:
                value = self.share(own, self.me)[...].astype(f32)
                for r in range(self.count - 1):
                    value = value + box[r].astype(f32)
                self.share(total, self.me)[...] = value.astype(total.dtype)
            for copy in self.copies(1):
                copy.start()
        self.step += 1
        return self.step == 2

    def close(self):
        for copy in self.copies(0) + self.copies(1):
            copy.wait_send()
        for _, _, total, name in self.items:
            self.m.store(total, name)


class Turns:
    def __init__(self):
        self.waiting = []
        self.rings = []

    def begin(self, ring):
        ring.begin()
        self.waiting.append(ring)
        self.rings.append(ring)

    def tick(self):
        if self.waiting:
            ring = self.waiting.pop(0)
            if not ring.tick():
                self.waiting.append(ring)

    def close(self):
        while self.waiting:
            self.tick()
        for ring in self.rings:
            ring.close()


def ring_box(shape, kind, count):
    rows, columns = ring_rows(shape, kind, count)
    return ((2, count - 1, rows, columns), kind)


def direct_box(shape, kind, count):
    return ((count - 1, shape[0] // count, shape[1]), kind)


def ring_fits(shapes, count):
    return (
        count > 1
        and count % 2 == 0
        and all(ring_rows(shape, kind, count) for shape, kind in shapes)
    )


def groups(array):
    halves = array.shape[0] // SUB
    sides = array.shape[1] // LANES
    return [
        array[SUB * s : SUB * s + SUB, LANES * l : LANES * l + LANES]
        for s in range(halves)
        for l in range(sides)
    ]


def spread_row(ref, index):
    return jnp.broadcast_to(ref[index], (SUB, LANES))


def advance(state, coefs, keep, signals, sides):
    root_real, root_imag = coefs
    half = len(state) // 2
    kept = [value * keep for value in state]
    fresh = [None] * len(state)
    for g in range(half):
        a_real, a_imag = kept[g], kept[half + g]
        fresh[g] = (root_real[g] * a_real - root_imag[g] * a_imag) + signals[g % sides]
        fresh[half + g] = root_real[g] * a_imag + root_imag[g] * a_real
    return kept, fresh


def filter_forward(m, first, count, state):
    sides = m.xl.shape[0]
    tables = m.tab
    root_real, root_imag = groups(tables[0]), groups(tables[1])
    out_real, out_imag = groups(tables[2]), groups(tables[3])
    half = len(root_real)
    unroll = 16

    def chunk(ch, state):
        for g in range(2 * half):
            m.st[ch, g] = state[g]

        def steps(i, state):
            state = list(state)
            for j in range(unroll):
                t = ch * SPAN + i * unroll + j
                keep = spread_row(m.kf, (pl.ds(t, 1), slice(None)))
                signals = [
                    spread_row(m.xl, (l, pl.ds(t, 1), slice(None))) for l in range(sides)
                ]
                _, state = advance(state, (root_real, root_imag), keep, signals, sides)
                for l in range(sides):
                    total = None
                    for g in range(l, half, sides):
                        term = out_real[g] * state[g] - out_imag[g] * state[half + g]
                        total = term if total is None else total + term
                    m.part[l, pl.ds(pl.multiple_of((i * unroll + j) * SUB, SUB), SUB), :] = total
            return tuple(state)

        state = lax.fori_loop(0, SPAN // unroll, steps, state)
        rows = at(ch, SPAN)
        for l in range(sides):
            lanes = slice(LANES * l, LANES * l + LANES)
            value = m.om[:, lanes] * m.xl[l, rows, :]
            for s in range(SUB):
                value = value + m.part[l, pl.ds(s, SPAN, stride=SUB), :]
            gate = sigmoid(value)
            m.mxl[rows, lanes] = (value * gate).astype(bf16)
            m.se[rows, lanes] = (gate * (1.0 + value * (1.0 - gate))).astype(bf16)
        return state

    return lax.fori_loop(first, first + count, chunk, state)


def window_mask(m, first_row, rows, first_key, keys):
    here = m.segb[pl.ds(pl.multiple_of(first_row + SUB, SUB), rows), :][:, :1]
    same = here == m.segr[:, pl.ds(pl.multiple_of(first_key, LANES), keys)].astype(f32)
    row = first_row + lax.broadcasted_iota(jnp.int32, (rows, keys), 0)
    key = first_key + lax.broadcasted_iota(jnp.int32, (rows, keys), 1)
    return same & (row >= key)


def window_of(index, block, length):
    back = -(-MAX_DOC // block)
    keys = min((back + 1) * block, length)
    first = jnp.maximum(index - back, 0) * block
    first = jnp.minimum(first, length - keys)
    return pl.multiple_of(first, LANES), keys


def keeping(m):
    length = m.segr.shape[1]
    m.segb[:SUB, :] = jnp.full((SUB, LANES), -1.0, f32)
    for k in range(length // LANES):
        row = m.segr[:, k * LANES : (k + 1) * LANES].astype(f32)
        m.segb[SUB + k * LANES : SUB + (k + 1) * LANES, :] = jnp.broadcast_to(row, (LANES, LANES)).T
    for k in range(length // LANES):
        now = m.segb[SUB + k * LANES : SUB + (k + 1) * LANES, :]
        before = m.segb[SUB - 1 + k * LANES : SUB - 1 + (k + 1) * LANES, :]
        m.kf[k * LANES : (k + 1) * LANES, :] = jnp.where(now == before, 1.0, 0.0)
    m.kf[length:, :] = jnp.zeros((SUB, LANES), f32)


def filter_tables(m):
    alpha, delta, theta, beta, e_re, e_im = (
        ref[...] for ref in (m.p0, m.p1, m.p2, m.p3, m.p4, m.p5)
    )
    magnitude = 1.0 - alpha * delta
    cosine, sine = jnp.cos(theta), jnp.sin(theta)
    scaled = alpha * beta
    entries = (
        magnitude * cosine, magnitude * sine, scaled * e_re, scaled * e_im,
        cosine, sine, alpha, delta, beta, e_re, e_im,
    )
    for k, entry in enumerate(entries):
        m.tab[k] = entry


def body_a(m):
    g = Group()
    length, width = m.xt.shape
    block = m.tok.shape[0]
    blocks = length // block
    channels = m.mxl.shape[1]
    sides = channels // LANES
    m.load(m.tok, m.wsh, m.cot, m.segr, m.p0, m.p1, m.p2, m.p3, m.p4, m.p5)
    m.load(m.gain, m.om, m.wv, m.wag)
    m.load(m.qg, m.qb, m.kg, m.wo, m.rg)
    g.greet()

    own = at(g.me, block)
    half = block // 2
    tokens = Gather(
        m, g,
        lambda s: m.tok.at[pl.ds(s * half, half), :],
        lambda j, s: m.xt.at[pl.ds(pl.multiple_of(j * block + s * half, half), half), :],
        2,
    )
    shared = Gather(m, g, lambda s: m.wsh, lambda j, s: m.wsf.at[at(j, channels), :], 1)
    pieces = 8
    rows_piece = length // pieces
    mixed = Gather(
        m, g,
        lambda s: m.mxl.at[pl.ds(s * rows_piece, rows_piece), :],
        lambda j, s: m.mx.at[pl.ds(s * rows_piece, rows_piece), at(j, channels)],
        pieces,
    )
    cots = Gather(
        m, g,
        lambda s: m.cot.at[pl.ds(s * half, half), :],
        lambda j, s: m.cotf.at[pl.ds(pl.multiple_of(j * block + s * half, half), half), :],
        2,
    )
    normed = Gather(
        m, g,
        lambda s: m.yno.at[pl.ds(s * half, half), :],
        lambda j, s: m.yn.at[pl.ds(pl.multiple_of(j * block + s * half, half), half), :],
        2,
    )
    branch = Scatter(m, g, "br", 2)

    m.need(m.tok, m.wsh)
    tokens.send(0)
    tokens.send(1)
    shared.send(0)
    m.need(m.cot)
    cots.send(0)
    m.xt[own, :] = m.tok[...]
    m.wsf[at(g.me, channels), :] = m.wsh[...]
    m.need(m.segr, m.p0, m.p1, m.p2, m.p3, m.p4, m.p5, m.gain, m.om)
    keeping(m)
    filter_tables(m)
    m.flush(m.kf, m.segb, m.tab)

    lane = lax.broadcasted_iota(jnp.int32, (SPAN, LANES), 1)

    def sums(j):
        def part(i, _):
            rows = pl.ds(pl.multiple_of(j * block + i * SPAN, SPAN), SPAN)
            one = jnp.zeros((SPAN, LANES), f32)
            two = jnp.zeros((SPAN, LANES), f32)
            for l in range(width // LANES):
                x = m.xt[rows, LANES * l : LANES * l + LANES].astype(f32)
                one = one + x
                two = two + x * x
            picked = jnp.where(lane == 6, 1.0, 0.0)
            for k, total in ((0, one), (3, two)):
                rest = jnp.sum(total, axis=1, keepdims=True)
                for n in range(3):
                    top = rest.astype(bf16).astype(f32)
                    picked = jnp.where(lane == k + n, top, picked)
                    rest = rest - top
            m.sums[rows, :] = picked.astype(bf16)
            return 0

        lax.fori_loop(0, block // SPAN, part, 0)

    sums(g.me)
    tokens.near()
    sums(g.sib)
    tokens.forward(0)
    tokens.forward(1)
    sums(g.opp)
    tokens.far()
    sums(g.diag)

    lane_wide = lax.broadcasted_iota(jnp.int32, (block, LANES), 1)

    def statistics(i, _):
        first, keys = window_of(i, block, length)
        seen = window_mask(m, i * block, block, first, keys).astype(bf16)
        got = plain(seen, m.sums[pl.ds(first, keys), :])
        pick = lambda low, high: jnp.sum(
            jnp.where((lane_wide >= low) & (lane_wide < high), got, 0.0), axis=1, keepdims=True
        )
        total = pick(6, 7) * width
        mean = pick(0, 3) / total
        var = pick(3, 6) / total - mean * mean
        rows = at(i, block)
        m.mean[rows, :] = jnp.broadcast_to(mean, (block, LANES))
        m.rstd[rows, :] = jnp.broadcast_to(lax.rsqrt(var + epsilon), (block, LANES))
        m.total[rows, :] = jnp.broadcast_to(total, (block, LANES))
        return 0

    lax.fori_loop(0, blocks, statistics, 0)

    def normalise(i, _):
        rows = at(i, SPAN)
        mean, rstd = m.mean[rows, :], m.rstd[rows, :]
        for l in range(width // LANES):
            lanes = slice(LANES * l, LANES * l + LANES)
            x = m.xt[rows, lanes].astype(f32)
            m.xn[rows, lanes] = ((x - mean) * rstd * m.gain[:, lanes]).astype(bf16)
        for l in range(sides):
            lanes = pl.ds(pl.multiple_of(g.me * channels + LANES * l, LANES), LANES)
            x = m.xt[rows, lanes].astype(f32)
            m.xl[l, rows, :] = (x - mean) * rstd * m.gain[:, lanes]
        return 0

    lax.fori_loop(0, length // SPAN, normalise, 0)
    own_stat = pl.ds(pl.multiple_of(g.me * block, block), block)
    m.so[0] = m.mean[own_stat, :]
    m.so[1] = m.rstd[own_stat, :]
    m.so[2] = m.total[own_stat, :]
    m.flush(m.xn, m.xl, m.so)

    zero = jnp.zeros((SUB, LANES), f32)
    state = tuple(zero for _ in range(m.st.shape[1]))
    per = length // SPAN // pieces
    for p in range(pieces):
        state = filter_forward(m, p * per, per, state)
        mixed.send(p)
        if p >= 2:
            mixed.forward(p - 2)
    cots.send(1)
    m.flush(m.se, m.st)
    for i in range(pieces):
        m.mx[pl.ds(i * rows_piece, rows_piece), at(g.me, channels)] = m.mxl[
            pl.ds(i * rows_piece, rows_piece), :
        ]
    m.cotf[own, :] = m.cot[...]
    m.need(m.wv)

    def values(i, _):
        rows = at(i, block)
        pre = plain(m.xn[rows, :], m.wv[...])
        gate = sigmoid(pre)
        m.v[rows, :] = (pre * gate).astype(bf16)
        m.sv[rows, :] = (gate * (1.0 + pre * (1.0 - gate))).astype(bf16)
        return 0

    lax.fori_loop(0, blocks, values, 0)
    m.flush(m.v, m.sv)
    for p in range(max(pieces - 2, 0), pieces):
        mixed.forward(p)
    shared.forward(0)
    shared.near()
    shared.far()
    mixed.near()
    mixed.far()
    m.need(m.qg, m.qb, m.kg, m.wag, m.wo, m.rg)

    def project(i, _):
        rows = at(i, block)
        z = plain(m.mx[rows, :], m.wsf[...])
        m.z[rows, :] = z.astype(bf16)
        m.q[rows, :] = (z * m.qg[...] + m.qb[...]).astype(bf16)
        m.k[rows, :] = (z * m.kg[...]).astype(bf16)
        return 0

    lax.fori_loop(0, blocks, project, 0)
    m.flush(m.mx, m.wsf, m.z, m.q, m.k)
    scale = 1.0 / math.sqrt(m.q.shape[1])

    def attend(i):
        rows = at(i, block)
        first, keys = window_of(i, block, length)
        window = pl.ds(first, keys)
        scores = cross(m.q[rows, :], m.k[window, :]) * scale
        scores = jnp.where(window_mask(m, i * block, block, first, keys), scores, masked_score)
        expo = jnp.exp(scores - jnp.max(scores, axis=1, keepdims=True))
        prob = (expo / jnp.sum(expo, axis=1, keepdims=True)).astype(bf16)
        m.p[i] = prob
        attended = plain(prob, m.v[window, :])
        pre = plain(m.mx[rows, :], m.wag[...])
        gate = sigmoid(pre)
        swish = pre * gate
        m.r[rows, :] = swish.astype(bf16)
        m.os[rows, :] = (attended * (gate * (1.0 + pre * (1.0 - gate)))).astype(bf16)
        m.w[rows, :] = (attended * swish).astype(bf16)
        return plain(m.w[rows, :], m.wo[...])

    branch.put_diag(pieces_of(attend(g.diag), 2))
    branch.put_opp(pieces_of(attend(g.opp), 2))
    cots.forward(0)
    branch.put_sib(pieces_of(attend(g.sib), 2))
    cots.forward(1)
    m.bp[...] = attend(g.me)
    m.flush(m.p, m.r, m.os, m.w)
    for s in range(2):
        piece = pl.ds(s * half, half)
        y = branch.take(s, m.bp[piece, :]) + m.tok[piece, :].astype(f32)
        m.y[piece, :] = y
        rms = lax.rsqrt(jnp.mean(y * y, axis=1, keepdims=True) + epsilon)
        m.rs[piece, :] = jnp.broadcast_to(rms, (half, LANES))
        m.yno[piece, :] = (y * rms * m.rg[...]).astype(bf16)
        normed.send(s)
    m.yn[own, :] = m.yno[...]
    m.flush(m.y, m.rs)
    cots.near()
    cots.far()
    m.flush(m.cotf)
    normed.forward(0)
    normed.forward(1)
    normed.near()
    normed.far()
    m.flush(m.yn)
    for moved in (tokens, shared, mixed, cots, normed, branch):
        moved.close()
    m.close()


def run_a(arrays, sizes):
    length, width, block, channels, shared, values = sizes
    blocks = length // block
    keys = min((-(-MAX_DOC // block) + 1) * block, length)
    sides = channels // LANES
    dims = arrays.p0.shape[0]
    states = 2 * sides * (dims // SUB)
    outs = dict(
        xn=((length, width), bf16),
        xl=((sides, length, LANES), f32),
        tab=((11, dims, channels), f32),
        kf=((length + SUB, LANES), f32),
        segb=((length + SUB, LANES), f32),
        so=((3, block, LANES), f32),
        se=((length, channels), bf16),
        st=((length // SPAN, states, SUB, LANES), f32),
        mx=((length, width), bf16),
        v=((length, values), bf16),
        sv=((length, values), bf16),
        z=((length, shared), bf16),
        q=((length, shared), bf16),
        k=((length, shared), bf16),
        wsf=((width, shared), bf16),
        p=((blocks, block, keys), bf16),
        r=((length, values), bf16),
        os=((length, values), bf16),
        w=((length, values), bf16),
        y=((block, width), f32),
        rs=((block, LANES), f32),
        yn=((length, width), bf16),
        cotf=((length, width), bf16),
    )
    scratch = dict(
        xt=((length, width), bf16),
        sums=((length, LANES), bf16),
        mean=((length, LANES), f32),
        rstd=((length, LANES), f32),
        total=((length, LANES), f32),
        part=((sides, SPAN * SUB, LANES), f32),
        mxl=((length, channels), bf16),
        bp=((block, width), f32),
        yno=((block, width), bf16),
        **scatter_buffers("br", block, width),
    )
    return run_stage(body_a, arrays, outs, scratch, (51, 51), 1)


def transposed_product(left, right, out, step):
    def part(i, _):
        columns = at(i, step)
        out[columns, :] = inner(left[:, columns], right[...]).astype(bf16)
        return 0

    lax.fori_loop(0, left.shape[1] // step, part, 0)


def body_b(m):
    g = Group()
    length, width = m.yn.shape
    block = m.y.shape[0]
    half = block // 2
    m.load(m.yn, m.wg, m.wu, m.wd, m.cotf, m.y, m.rs, m.cot, m.rg)
    g.greet()
    grads = Scatter(m, g, "dy", 2)
    m.need(m.yn, m.wg, m.wu, m.wd, m.cotf)

    def feed(j):
        rows = at(j, block)
        low = m.yn[rows, :]
        gate = plain(low, m.wg[...])
        up = plain(low, m.wu[...])
        d_act = cross(m.cotf[rows, :], m.wd[...])
        sig = sigmoid(gate)
        swish = gate * sig
        m.act[rows, :] = (swish * up).astype(bf16)
        m.dg[rows, :] = (d_act * up * (sig * (1.0 + gate * (1.0 - sig)))).astype(bf16)
        m.du[rows, :] = (d_act * swish).astype(bf16)
        return cross(m.dg[rows, :], m.wg[...]) + cross(m.du[rows, :], m.wu[...])

    grads.put_diag(pieces_of(feed(g.diag), 2))
    grads.put_opp(pieces_of(feed(g.opp), 2))
    grads.put_sib(pieces_of(feed(g.sib), 2))
    m.bp[...] = feed(g.me)
    m.flush(m.act)
    transposed_product(m.act, m.cotf, m.gd, LANES)
    m.flush(m.gd)
    transposed_product(m.yn, m.dg, m.gg, 2 * LANES)
    m.flush(m.gg)
    transposed_product(m.yn, m.du, m.gu, 2 * LANES)
    m.flush(m.gu)
    m.need(m.y, m.rs, m.cot, m.rg)
    gain_sum = jnp.zeros((1, width), f32)
    for s in range(2):
        piece = pl.ds(s * half, half)
        d_yn = grads.take(s, m.bp[piece, :])
        rms = m.rs[piece, :][:, :1]
        hat = m.y[piece, :] * rms
        gain_sum = gain_sum + jnp.sum(d_yn * hat, axis=0, keepdims=True)
        d_hat = d_yn * m.rg[...]
        pull = d_hat - hat * jnp.mean(d_hat * hat, axis=1, keepdims=True)
        dy = m.cot[piece, :].astype(f32) + rms * pull
        m.dy[piece, :] = dy
        m.dyo[piece, :] = dy.astype(bf16)
    m.gr[...] = gain_sum
    m.flush(m.dyo, m.dy, m.gr)
    grads.close()
    m.close()


def run_b(arrays, sizes):
    length, width, block, units = sizes
    outs = dict(
        gd=((units, width), bf16),
        gg=((width, units), bf16),
        gu=((width, units), bf16),
        dy=((block, width), f32),
        gr=((1, width), f32),
        dyo=((block, width), bf16),
        act=((length, units), bf16),
    )
    scratch = dict(
        dg=((length, units), bf16),
        du=((length, units), bf16),
        bp=((block, width), f32),
        **scatter_buffers("dy", block, width),
    )
    return run_stage(body_b, arrays, outs, scratch, (6, 6), 2)


def filter_backward(m, last, count, gamma):
    sides = m.xl.shape[0]
    tables = m.tab
    root_real, root_imag = groups(tables[0]), groups(tables[1])
    out_real, out_imag = groups(tables[2]), groups(tables[3])
    half = len(root_real)
    unroll = 16

    def chunk(step, gamma):
        ch = last - step

        def again(i, state):
            state = list(state)
            for j in range(unroll):
                local = i * unroll + j
                t = ch * SPAN + local
                keep = spread_row(m.kf, (pl.ds(t, 1), slice(None)))
                signals = [
                    spread_row(m.xl, (l, pl.ds(t, 1), slice(None))) for l in range(sides)
                ]
                kept, state = advance(state, (root_real, root_imag), keep, signals, sides)
                for g in range(2 * half):
                    m.kept[local, g] = kept[g]
            return tuple(state)

        lax.fori_loop(0, SPAN // unroll, again, tuple(m.st[ch, g] for g in range(2 * half)))

        def reverse(i, carry):
            gamma, sums = list(carry[: 2 * half]), list(carry[2 * half :])
            for j in range(unroll):
                local = SPAN - 1 - (i * unroll + j)
                t = ch * SPAN + local
                keep = spread_row(m.kf, (pl.ds(t + 1, 1), slice(None)))
                signals = [
                    spread_row(m.dq, (l, pl.ds(t, 1), slice(None))) for l in range(sides)
                ]
                _, gamma = advance(gamma, (root_real, root_imag), keep, signals, sides)
                for l in range(sides):
                    total = None
                    for g in range(l, half, sides):
                        g_real, g_imag = gamma[g], gamma[half + g]
                        a_real, a_imag = m.kept[local, g], m.kept[local, half + g]
                        term = out_real[g] * g_real - out_imag[g] * g_imag
                        total = term if total is None else total + term
                        sums[g] = sums[g] + (g_real * a_real - g_imag * a_imag)
                        sums[half + g] = sums[half + g] + (g_real * a_imag + g_imag * a_real)
                        sums[2 * half + g] = sums[2 * half + g] + signals[l] * a_real
                        sums[3 * half + g] = sums[3 * half + g] + signals[l] * a_imag
                    m.part[l, pl.ds(pl.multiple_of(local * SUB, SUB), SUB), :] = total
            return tuple(gamma) + tuple(sums)

        start = tuple(gamma) + tuple(m.acc[g] for g in range(4 * half))
        done = lax.fori_loop(0, SPAN // unroll, reverse, start)
        for g in range(4 * half):
            m.acc[g] = done[2 * half + g]
        rows = at(ch, SPAN)
        for l in range(sides):
            lanes = slice(LANES * l, LANES * l + LANES)
            signal = m.dq[l, rows, :]
            value = m.om[:, lanes] * signal
            for s in range(SUB):
                value = value + m.part[l, pl.ds(s, SPAN, stride=SUB), :]
            m.dxb[rows, lanes] = value.astype(bf16)
            m.go[:, lanes] = m.go[:, lanes] + jnp.sum(
                signal * m.xl[l, rows, :], axis=0, keepdims=True
            )
        return done[: 2 * half]

    return lax.fori_loop(0, count, chunk, gamma)


def filter_gradients(m):
    sides = m.xl.shape[0]
    half = m.acc.shape[0] // 4
    dims = m.tab.shape[1]
    for g in range(half):
        s, l = g // sides, g % sides
        rows = slice(SUB * s, SUB * s + SUB)
        lanes = slice(LANES * l, LANES * l + LANES)
        q_re, q_im, c_re, c_im, cosine, sine, alpha, delta, beta, e_re, e_im = (
            m.tab[k, rows, lanes] for k in range(11)
        )
        lag_re, lag_im, sum_re, sum_im = (m.acc[k * half + g] for k in range(4))
        f_re = q_re * sum_re - q_im * sum_im + m.go[:, lanes]
        f_im = q_re * sum_im + q_im * sum_re
        scaled = alpha * beta
        d_scaled = e_re * f_re - e_im * f_im
        w_re = c_re * lag_re - c_im * lag_im
        w_im = c_re * lag_im + c_im * lag_re
        d_mag = w_re * cosine - w_im * sine
        m.pk[0 * dims + SUB * s : 0 * dims + SUB * s + SUB, lanes] = beta * d_scaled - delta * d_mag
        m.pk[1 * dims + SUB * s : 1 * dims + SUB * s + SUB, lanes] = -alpha * d_mag
        m.pk[2 * dims + SUB * s : 2 * dims + SUB * s + SUB, lanes] = -(w_re * q_im + w_im * q_re)
        m.pk[3 * dims + SUB * s : 3 * dims + SUB * s + SUB, lanes] = alpha * d_scaled
        m.pk[4 * dims + SUB * s : 4 * dims + SUB * s + SUB, lanes] = scaled * f_re
        m.pk[5 * dims + SUB * s : 5 * dims + SUB * s + SUB, lanes] = -scaled * f_im


def body_c(count, m):
    g = Group()
    length, width = m.mx.shape
    block = m.tok.shape[0]
    blocks = length // block
    half = block // 2
    channels = m.se.shape[1]
    shared = m.q.shape[1]
    sides = channels // LANES
    m.load(m.dyo, m.gd, m.gg, m.gu, m.act, m.wd, m.w, m.wo, m.r, m.os, m.v, m.p, m.k, m.q, m.z)
    m.load(m.qg, m.kg, m.sv, m.wsf, m.wag, m.wv, m.y, m.mx, m.xn, m.se, m.st, m.xl, m.kf, m.tab)
    m.load(m.om, m.tok, m.so, m.gain, m.dy, m.gr, m.segb, m.segr)
    turns = Turns()
    down = inward = outer = tail = None
    if count:
        down = Ring(m, count, [(m.gd, m.gdb, "gdt")])
        inward = Ring(m, count, [(m.gg, m.ggb, "ggt"), (m.gu, m.gub, "gut")])
        outer = Ring(
            m, count, [(m.gao, m.gaob, "gaot"), (m.r, m.gagb, "gagt"), (m.os, m.gvb, "gvt")]
        )
        tail = Direct(
            m, count, [(m.gs, m.gsb, m.gss, "gst"), (m.pk, m.pkb, m.pks, "pkt")]
        )
        here = lax.axis_index("dp")
        g.greet([lax.rem(here + r, count) for r in range(1, count)])
    else:
        g.greet()
    fed = Scatter(m, g, "xv", 2)
    back = Gather(
        m, g,
        lambda s: m.dyo.at[pl.ds(s * half, half), :],
        lambda j, s: m.dyf.at[pl.ds(pl.multiple_of(j * block + s * half, half), half), :],
        2,
    )
    m.need(m.dyo, m.gd, m.gg, m.gu)
    back.send(0)
    back.send(1)
    m.dyf[at(g.me, block), :] = m.dyo[...]

    def begin(ring, *pairs):
        if ring is None:
            for ref, name in pairs:
                m.store(ref, name)
        else:
            turns.begin(ring)

    begin(down, (m.gd, "gdt"))
    begin(inward, (m.gg, "ggt"), (m.gu, "gut"))
    pieces = 4
    dm = Scatter(m, g, "dm", pieces, range(pieces - 1, -1, -1))
    sh = Scatter(m, g, "sh", 1)
    others = (g.sib, g.opp, g.diag)
    base = m.sems(9)
    parts = [
        m.remote(m.dxb.at[at(dev, block), :], m.dxr.at[k], base, k, {"tensor": dev})
        for k, dev in enumerate(others)
    ]
    small = [
        m.remote(m.smo, m.sm.at[g.me], base, 3 + k, {"tensor": dev})
        for k, dev in enumerate(others)
    ]
    tails = [
        m.remote(m.aro, m.ar.at[:, at(g.me, block)], base, 6 + k, {"tensor": dev})
        for k, dev in enumerate(others)
    ]

    scale = 1.0 / math.sqrt(shared)
    m.dk[...] = jnp.zeros(m.dk.shape, f32)
    m.dv[...] = jnp.zeros(m.dv.shape, f32)
    m.need(m.act, m.wd)
    share = lambda j: plain(m.act[at(j, block), :], m.wd[...])
    fed.put_diag(pieces_of(share(g.diag), 2))
    fed.put_sib(pieces_of(share(g.sib), 2))
    m.dxn[...] = share(g.me)
    turns.tick()
    turns.tick()
    back.forward(0)
    turns.tick()
    back.forward(1)
    fed.put_opp(pieces_of(share(g.opp), 2))
    turns.tick()
    back.near()
    back.far()
    m.need(m.w, m.wo, m.r, m.os, m.v, m.p, m.k, m.q)
    transposed_product(m.w, m.dyf, m.gao, 2 * LANES)
    turns.tick()

    def attend(i, _):
        rows = at(i, block)
        first, keys = window_of(i, block, length)
        window = pl.ds(first, keys)
        d_w = cross(m.dyf[rows, :], m.wo[...])
        d_o = (d_w * m.r[rows, :].astype(f32)).astype(bf16)
        m.drp[rows, :] = (d_w * m.os[rows, :].astype(f32)).astype(bf16)
        prob_low = m.p[i]
        prob = prob_low.astype(f32)
        weighed = prob * cross(d_o, m.v[window, :])
        d_s = (weighed - prob * jnp.sum(weighed, axis=1, keepdims=True)) * scale
        d_s = d_s.astype(bf16)
        d_q = plain(d_s, m.k[window, :])
        for l in range(shared // LANES):
            m.dq[l, rows, :] = d_q[:, LANES * l : LANES * l + LANES]
        m.dk[window, :] = m.dk[window, :] + inner(d_s, m.q[rows, :])
        m.dv[window, :] = m.dv[window, :] + inner(prob_low, d_o)
        return 0

    for n in range(blocks):
        attend(n, 0)
        turns.tick()
    m.need(m.z, m.qg, m.kg, m.sv, m.wsf, m.wag)

    def affine(i, sums):
        rows = at(i, block)
        d_q = jnp.concatenate([m.dq[l, rows, :] for l in range(shared // LANES)], axis=1)
        d_k, z = m.dk[rows, :], m.z[rows, :].astype(f32)
        m.dz[rows, :] = (d_q * m.qg[...] + d_k * m.kg[...]).astype(bf16)
        m.dvp[rows, :] = (m.dv[rows, :] * m.sv[rows, :].astype(f32)).astype(bf16)
        new = (d_q * z, d_q, d_k * z)
        return tuple(s + jnp.sum(n, axis=0, keepdims=True) for s, n in zip(sums, new))

    aff = lax.fori_loop(0, blocks, affine, tuple(jnp.zeros((1, shared), f32) for _ in range(3)))
    m.smo[...] = jnp.zeros(m.smo.shape, f32)
    for n in range(3):
        m.smo[2 + n : 3 + n, :shared] = aff[n]

    def mixing(j):
        def value(s):
            rows = pl.ds(s * (length // pieces), length // pieces)
            return cross(m.dz[rows, :], m.wsf[at(j, channels), :]) + cross(
                m.drp[rows, :], m.wag[at(j, channels), :]
            )

        return value

    m.need(m.y)
    for s in range(2):
        piece = pl.ds(s * half, half)
        m.out[piece, :] = (fed.take(s, m.dxn[piece, :]) + m.y[piece, :]).astype(bf16)
    m.flush(m.out)
    fed.close()
    m.need(m.mx, m.xn)
    transposed_product(m.mx, m.drp, m.r, 2 * LANES)
    turns.tick()
    transposed_product(m.xn, m.dvp, m.os, 2 * LANES)
    begin(outer, (m.gao, "gaot"), (m.r, "gagt"), (m.os, "gvt"))
    dm.put_diag(mixing(g.diag))
    turns.tick()
    dm.put_opp(mixing(g.opp))
    turns.tick()
    dm.put_sib(mixing(g.sib))
    turns.tick()
    m.need(m.wv)
    xv = Scatter(m, g, "xv", 2)
    spread = lambda j: pieces_of(cross(m.dvp[at(j, block), :], m.wv[...]), 2)
    split = lambda j: (lambda s: inner(m.mx[:, at(j, channels)], m.dz[...]))

    def spreading():
        xv.put_diag(spread(g.diag))
        xv.put_opp(spread(g.opp))
        turns.tick()
        xv.put_sib(spread(g.sib))
        m.dxn[...] = cross(m.dvp[at(g.me, block), :], m.wv[...])
        turns.tick()
        sh.put_diag(split(g.diag))
        sh.put_opp(split(g.opp))
        turns.tick()
        sh.put_sib(split(g.sib))
        m.shp[...] = split(g.me)(0)
        turns.tick()

    m.need(m.se, m.st, m.xl, m.kf, m.tab, m.om)
    half_states = m.acc.shape[0] // 4
    m.acc[...] = jnp.zeros(m.acc.shape, f32)
    m.go[...] = jnp.zeros(m.go.shape, f32)
    gamma = tuple(jnp.zeros((SUB, LANES), f32) for _ in range(2 * half_states))
    per = length // SPAN // pieces
    own_mix = mixing(g.me)
    for s in range(pieces - 1, -1, -1):
        rows = pl.ds(s * (length // pieces), length // pieces)
        d_e = dm.take(s, own_mix(s)) * m.se[rows, :].astype(f32)
        for l in range(sides):
            m.dq[l, rows, :] = d_e[:, LANES * l : LANES * l + LANES]
        for n in range(per - 1, -1, -1):
            gamma = filter_backward(m, s * per + n, 1, gamma)
            turns.tick()
        for k, dev in enumerate(others):

            @pl.when(dev == s)
            def _():
                parts[k].start()

        if s == pieces - 1:
            spreading()
    filter_gradients(m)
    base_row = m.pk.shape[0] - PACK_TAIL
    m.pk[base_row:, :] = jnp.zeros((PACK_TAIL, channels), f32)
    m.pk[base_row : base_row + 1, :] = m.go[...]
    m.gs[...] = sh.take(0, m.shp[...]).astype(bf16)
    turns.tick()
    m.need(m.tok, m.so, m.gain, m.dy, m.gr, m.segb, m.segr)
    for s in range(2):
        piece = pl.ds(s * half, half)
        m.dxn[piece, :] = xv.take(s, m.dxn[piece, :])
    own_columns = at(g.me, channels)
    m.dxn[:, own_columns] = m.dxn[:, own_columns] + m.dxb[at(g.me, block), :].astype(f32)
    for k, dev in enumerate(others):
        parts[k].wait_recv()
        columns = at(dev, channels)
        m.dxn[:, columns] = m.dxn[:, columns] + m.dxr[k].astype(f32)
    gain_sum = jnp.zeros((1, width), f32)
    lane = lax.broadcasted_iota(jnp.int32, (half, LANES), 1)
    for s in range(2):
        piece = pl.ds(s * half, half)
        mean, rstd, total = (m.so[n, piece, :][:, :1] for n in range(3))
        centred = m.tok[piece, :].astype(f32) - mean
        d_xn = m.dxn[piece, :]
        gain_sum = gain_sum + jnp.sum(d_xn * (centred * rstd), axis=0, keepdims=True)
        d_hat = d_xn * m.gain[...]
        d_var = -0.5 * rstd * rstd * rstd * jnp.sum(d_hat * centred, axis=1, keepdims=True)
        one = (-rstd * jnp.sum(d_hat, axis=1, keepdims=True) - 2.0 * mean * d_var) / total
        two = d_var / total
        m.dxn[piece, :] = d_hat * rstd + m.dy[piece, :]
        m.aw[piece, :] = jnp.where(lane == 0, one, jnp.where(lane == 1, two, 0.0))
    m.smo[0:1, :] = gain_sum
    m.smo[1:2, :] = m.gr[...]
    turned = m.aw[...].T
    for n in range(2):
        rest = turned[n : n + 1, :]
        for k in range(3):
            top = rest.astype(bf16).astype(f32)
            m.art[3 * n + k : 3 * n + k + 1, :] = top
            rest = rest - top
    m.art[6:8, :] = jnp.zeros((2, block), f32)
    m.art[8:16, :] = jnp.zeros((8, block), f32)
    m.aro[...] = m.art[...].astype(bf16)
    for copy in tails + small:
        copy.start()
    m.ar[:, at(g.me, block)] = m.aro[...]
    m.sm[g.me] = m.smo[...]
    reach = -(-MAX_DOC // block)
    keys = min((reach + 1) * block, length)
    first_key = pl.multiple_of(jnp.minimum(g.me * block, length - keys), LANES)
    first_row = pl.multiple_of(g.me * block, LANES)
    here = m.segb[pl.ds(pl.multiple_of(first_row + SUB, SUB), block), :][:, :1]
    same = here == m.segr[:, pl.ds(first_key, keys)].astype(f32)
    row = first_row + lax.broadcasted_iota(jnp.int32, (block, keys), 0)
    key = first_key + lax.broadcasted_iota(jnp.int32, (block, keys), 1)
    seen = (same & (row <= key)).astype(bf16)
    for copy in tails:
        copy.wait_recv()
    pulled = cross(seen, m.ar[:, pl.ds(first_key, keys)])
    b_one = pulled[:, 0:1] + pulled[:, 1:2] + pulled[:, 2:3]
    b_two = pulled[:, 3:4] + pulled[:, 4:5] + pulled[:, 5:6]
    for s in range(2):
        piece = pl.ds(s * half, half)
        rows = slice(s * half, (s + 1) * half)
        x = m.tok[piece, :].astype(f32)
        m.gt[piece, :] = (m.dxn[piece, :] + b_one[rows] + 2.0 * x * b_two[rows]).astype(bf16)
    m.flush(m.gt)
    turns.tick()
    for copy in small:
        copy.wait_recv()
    total = m.sm[0]
    for j in range(1, m.sm.shape[0]):
        total = total + m.sm[j]
    per = width // channels
    for n in range(2):
        for k in range(per):
            row = base_row + 1 + n * per + k
            m.pk[row : row + 1, :] = total[n : n + 1, k * channels : (k + 1) * channels]
    for n in range(3):
        row = base_row + 1 + 2 * per + n
        m.pk[row : row + 1, :shared] = total[2 + n : 3 + n, :shared]
    begin(tail, (m.gs, "gst"), (m.pk, "pkt"))
    turns.close()
    for moved in (dm, xv, sh, back):
        moved.close()
    for copy in parts + small + tails:
        copy.wait_send()
    m.close()


def run_c(arrays, sizes, count):
    length, width, block, channels, shared, values = sizes
    units = arrays.act.shape[1]
    sides = channels // LANES
    dims = arrays.tab.shape[1]
    half_states = sides * (dims // SUB)
    late = dict(
        gao=((values, width), bf16),
        gag=((width, values), bf16),
        gv=((width, values), bf16),
        gs=((channels, shared), bf16),
        pk=((6 * dims + PACK_TAIL, channels), f32),
    )
    summed = dict(
        gd=((units, width), bf16),
        gg=((width, units), bf16),
        gu=((width, units), bf16),
        **late,
    )
    if not ring_fits(summed.values(), count):
        count = 0
    outs = dict(
        gt=((block, width), bf16),
        out=((block, width), bf16),
    )
    scratch = dict(
        dyf=((length, width), bf16),
        dk=((length, shared), f32),
        dv=((length, values), f32),
        dq=((max(sides, shared // LANES), length, LANES), f32),
        drp=((length, values), bf16),
        dz=((length, shared), bf16),
        dvp=((length, values), bf16),
        dxn=((block, width), f32),
        shp=((channels, shared), f32),
        go=((1, channels), f32),
        acc=((4 * half_states, SUB, LANES), f32),
        kept=((SPAN, 2 * half_states, SUB, LANES), f32),
        part=((sides, SPAN * SUB, LANES), f32),
        dxb=((length, channels), bf16),
        dxr=((3, block, channels), bf16),
        aw=((block, LANES), f32),
        art=((16, block), f32),
        aro=((16, block), bf16),
        ar=((16, length), bf16),
        smo=((SUB, width), f32),
        sm=((length // block, SUB, width), f32),
        **{name: late[name] for name in ("gao", "gs", "pk")},
        **scatter_buffers("dm", length, channels),
        **scatter_buffers("xv", block, width),
        **scatter_buffers("sh", channels, shared),
    )
    sems = [42, 42]
    if count:
        for name, (shape, kind) in summed.items():
            small = name in ("gs", "pk")
            scratch[name + "b"] = (direct_box if small else ring_box)(shape, kind, count)
        scratch.update(gss=summed["gs"], pks=summed["pk"])
        sems = [42 + 12 + 4 * (count - 1), 42 + 12 * count + 4 * (count - 1)]
    bare = {name + "t": entry for name, entry in summed.items()}
    done = run_stage(
        functools.partial(body_c, count), arrays, outs, scratch, sems, 3, bare.items()
    )
    done.dims = dims
    done.summed = bool(count)
    return done


def body_f(dims, shared, m):
    wide = ((m.gd, m.gdt), (m.gg, m.ggt), (m.gu, m.gut), (m.gao, m.gaot), (m.gag, m.gagt))
    wide += ((m.gv, m.gvt), (m.gs, m.gst))
    m.load(m.out, m.gt, m.gd, m.gg, m.gu, m.gao, m.gag, m.gv, m.gs, m.pk)
    for source, target in ((m.out, m.outt), (m.gt, m.gtt)):
        m.need(source)
        target[...] = source[...]
        m.flush(target)
    for source, target in wide:
        m.need(source)
        rows = source.shape[0] // 2
        for n in range(2):

            def part(i, _):
                piece = pl.ds(pl.multiple_of(n * rows + i * 16, 16), 16)
                target[piece, :] = source[piece, :].astype(f32)
                return 0

            lax.fori_loop(0, rows // 16, part, 0, unroll=4)
        m.flush(target)
    m.need(m.pk)
    for k, out in enumerate((m.e0, m.e1, m.e2, m.e3, m.e4, m.e5)):
        out[...] = m.pk[k * dims : (k + 1) * dims, :]
    top = 6 * dims
    channels = m.pk.shape[1]
    m.om[...] = m.pk[top : top + 1, :]
    per = m.norm.shape[1] // channels
    for n, out in enumerate((m.norm, m.rms)):
        for k in range(per):
            row = top + 1 + n * per + k
            out[:, k * channels : (k + 1) * channels] = m.pk[row : row + 1, :]
    for n, out in enumerate((m.qg, m.qb, m.kg)):
        row = top + 1 + 2 * per + n
        out[...] = m.pk[row : row + 1, :shared]
    m.flush(m.e0, m.e1, m.e2, m.e3, m.e4, m.e5, m.om, m.norm, m.rms, m.qg, m.qb, m.kg)
    m.close()


def finish(c, shared):
    sums = dict(gd=c.gdt, gg=c.ggt, gu=c.gut, gao=c.gaot, gag=c.gagt, gv=c.gvt, gs=c.gst, pk=c.pkt)
    if not c.summed:
        total = lax.psum([value.astype(f32) for value in sums.values()], "dp")
        sums = {name: v.astype(old.dtype) for (name, old), v in zip(sums.items(), total)}
    channels, width = sums["pk"].shape[1], sums["gd"].shape[1]
    outs = dict(
        e0=((c.dims, channels), f32),
        e1=((c.dims, channels), f32),
        e2=((c.dims, channels), f32),
        e3=((c.dims, channels), f32),
        e4=((c.dims, channels), f32),
        e5=((c.dims, channels), f32),
        om=((1, channels), f32),
        norm=((1, width), f32),
        rms=((1, width), f32),
        qg=((1, shared), f32),
        qb=((1, shared), f32),
        kg=((1, shared), f32),
    )
    for name, value in sums.items():
        if value is not sums["pk"]:
            outs[name + "t"] = (value.shape, f32)
    outs.update(outt=(c.out.shape, bf16), gtt=(c.gt.shape, bf16))
    f = run_stage(
        functools.partial(body_f, c.dims, shared),
        types.SimpleNamespace(out=c.out, gt=c.gt, **sums), outs, {}, (0, 0), None,
    )
    tables = [table.T for table in (f.e0, f.e1, f.e2, f.e3, f.e4, f.e5)]
    return (
        f.outt, f.gtt, f.norm[0], *tables, f.om[0], f.gst,
        f.qg[0], f.qb[0], f.kg[0], f.gagt, f.gvt, f.gaot, f.rms[0], f.ggt, f.gut, f.gdt,
    )


def on_device(
    tokens,
    segments,
    cotangent,
    timestep_norm_gain,
    ema_alpha,
    ema_delta,
    ema_theta,
    ema_beta,
    eta_real,
    eta_imag,
    ema_omega,
    w_shared,
    q_gain,
    q_bias,
    k_gain,
    w_attgate,
    w_value,
    w_attout,
    rms_gain,
    w_gate,
    w_up,
    w_down,
):
    block, width = tokens.shape
    length = segments.shape[1]
    channels, dims = ema_alpha.shape
    shared = w_shared.shape[1]
    values = w_value.shape[1]
    units = w_gate.shape[1]
    om = ema_omega[None]
    gain, rg = timestep_norm_gain[None], rms_gain[None]
    qg, qb, kg = q_gain[None], q_bias[None], k_gain[None]
    segr = segments
    a = run_a(
        types.SimpleNamespace(
            tok=tokens, cot=cotangent, wsh=w_shared, segr=segr, gain=gain,
            p0=ema_alpha.T, p1=ema_delta.T, p2=ema_theta.T,
            p3=ema_beta.T, p4=eta_real.T, p5=eta_imag.T, om=om, qg=qg, qb=qb, kg=kg, wag=w_attgate, wv=w_value, wo=w_attout, rg=rg,
        ),
        (length, width, block, channels, shared, values),
    )
    b = run_b(
        types.SimpleNamespace(
            yn=a.yn, wg=w_gate, wu=w_up, wd=w_down, cotf=a.cotf, y=a.y, rs=a.rs,
            cot=cotangent, rg=rg,
        ),
        (length, width, block, units),
    )
    c = run_c(
        types.SimpleNamespace(
            dyo=b.dyo, gd=b.gd, gg=b.gg, gu=b.gu, act=b.act, wd=w_down, y=a.y,
            wo=w_attout, r=a.r, os=a.os, v=a.v, p=a.p, k=a.k,
            q=a.q, z=a.z, qg=qg, kg=kg, sv=a.sv, wsf=a.wsf, wag=w_attgate,
            wv=w_value, w=a.w, mx=a.mx, xn=a.xn, se=a.se, st=a.st, xl=a.xl,
            kf=a.kf, tab=a.tab, om=om, tok=tokens, so=a.so, gain=gain, dy=b.dy, gr=b.gr,
            segb=a.segb, segr=segr,
        ),
        (length, width, block, channels, shared, values),
        lax.axis_size("dp"),
    )
    return finish(c, shared)


def solution(mesh):
    placed = (
        P(("dp", "tensor"), None),
        P("dp", None),
        P(("dp", "tensor"), None),
        P(),
        P("tensor", None),
        P("tensor", None),
        P("tensor", None),
        P("tensor", None),
        P("tensor", None),
        P("tensor", None),
        P("tensor"),
        P("tensor", None),
        P(),
        P(),
        P(),
        P(None, "tensor"),
        P(None, "tensor"),
        P("tensor", None),
        P(),
        P(None, "tensor"),
        P(None, "tensor"),
        P("tensor", None),
    )
    return jax.shard_map(
        on_device,
        mesh=mesh,
        in_specs=placed,
        out_specs=(
            P(("dp", "tensor"), None),
            P(("dp", "tensor"), None),
            P(),
            P("tensor", None),
            P("tensor", None),
            P("tensor", None),
            P("tensor", None),
            P("tensor", None),
            P("tensor", None),
            P("tensor"),
            P("tensor", None),
            P(),
            P(),
            P(),
            P(None, "tensor"),
            P(None, "tensor"),
            P("tensor", None),
            P(),
            P(None, "tensor"),
            P(None, "tensor"),
            P("tensor", None),
        ),
        check_vma=False,
    )
```

```python
import functools
import math
import types

import jax
import jax.numpy as jnp
from jax import lax
from jax.experimental import pallas as pl
from jax.experimental.pallas import tpu as pltpu
from jax.sharding import PartitionSpec as P

epsilon = 1e-05
masked_score = -1000000000.0
f32 = jnp.float32
bf16 = jnp.bfloat16
MESH = pl.DeviceIdType.MESH
LANES = 128
SUB = 8
SPAN = 64
MAX_DOC = 512
PACK_TAIL = 32
VMEM_BYTES = 62 * 2**20


def plain(left, right):
    return jnp.dot(left, right, preferred_element_type=f32)


def cross(left, right):
    return lax.dot_general(
        left, right, (((1,), (1,)), ((), ())), preferred_element_type=f32
    )


def inner(left, right):
    return lax.dot_general(
        left, right, (((0,), (0,)), ((), ())), preferred_element_type=f32
    )


def sigmoid(value):
    return 1.0 / (1.0 + jnp.exp(-value))


def at(index, size):
    return pl.ds(pl.multiple_of(index * size, size), size)


class Stage:
    def __init__(self, ins, outs, bare, scratch, alias, refs):
        self.pending = {}
        self.flushed = []
        count = len(ins)
        self.hbm_in = dict(zip(ins, refs[:count]))
        total = len(outs) + len(bare)
        self.hbm_out = dict(zip(list(outs) + list(bare), refs[count : count + total]))
        rest = refs[count + total :]
        names = list(ins) + list(outs) + list(scratch)
        self.refs = dict(zip(names, rest[: len(names)]))
        self.load_sem, self.flush_sem, self.send_sem, self.recv_sem = rest[len(names) :]
        self.order = {name: k for k, name in enumerate(ins)}
        self.out_order = {name: k for k, name in enumerate(self.hbm_out)}
        self.sends = self.receipts = 0
        self.names = {id(ref): name for name, ref in self.refs.items()}
        for name, other in alias:
            self.refs[name] = self.refs[other]

    def __getitem__(self, name):
        return self.refs[name]

    def __getattr__(self, name):
        return self.refs[name]

    def load(self, *refs):
        for name in [self.names[id(ref)] for ref in refs]:
            copy = pltpu.make_async_copy(
                self.hbm_in[name], self.refs[name], self.load_sem.at[self.order[name]]
            )
            copy.start()
            self.pending[name] = copy

    def need(self, *refs):
        for name in [self.names[id(ref)] for ref in refs]:
            copy = self.pending.pop(name, None)
            if copy is not None:
                copy.wait()

    def flush(self, *refs):
        for name in [self.names[id(ref)] for ref in refs]:
            if name in self.hbm_out:
                self.store(self.refs[name], name)

    def store(self, source, name):
        copy = pltpu.make_async_copy(
            source, self.hbm_out[name], self.flush_sem.at[self.out_order[name]]
        )
        copy.start()
        self.flushed.append(copy)

    def close(self):
        assert self.sends <= self.send_sem.shape[0]
        assert self.receipts <= self.recv_sem.shape[0]
        for copy in self.flushed:
            copy.wait()


    def sems(self, count, sends=None):
        first = self.sends, self.receipts
        self.sends += count if sends is None else sends
        self.receipts += count
        return first

    def remote(self, source, target_ref, base, index, device, sent=None):
        return pltpu.make_async_remote_copy(
            src_ref=source,
            dst_ref=target_ref,
            send_sem=self.send_sem.at[base[0] + (index if sent is None else sent)],
            recv_sem=self.recv_sem.at[base[1] + index],
            device_id=device,
            device_id_type=MESH,
        )


def run_stage(body, ins, outs, scratch, sems, collective, bare=(), alias=()):
    ins = vars(ins)
    written = {**outs, **dict(bare)}

    def kernel(*refs):
        body(Stage(list(ins), list(outs), list(dict(bare)), list(scratch), alias, refs))

    buffers = [pltpu.VMEM(array.shape, array.dtype) for array in ins.values()]
    buffers += [pltpu.VMEM(shape, kind) for shape, kind in outs.values()]
    buffers += [pltpu.VMEM(shape, kind) for shape, kind in scratch.values()]
    results = pl.pallas_call(
        kernel,
        out_shape=tuple(jax.ShapeDtypeStruct(shape, kind) for shape, kind in written.values()),
        in_specs=[pl.BlockSpec(memory_space=pl.ANY)] * len(ins),
        out_specs=tuple(pl.BlockSpec(memory_space=pl.ANY) for _ in written),
        scratch_shapes=buffers
        + [
            pltpu.SemaphoreType.DMA((len(ins),)),
            pltpu.SemaphoreType.DMA((len(written),)),
            pltpu.SemaphoreType.DMA((max(sems[0], 1),)),
            pltpu.SemaphoreType.DMA((max(sems[1], 1),)),
        ],
        compiler_params=pltpu.CompilerParams(
            collective_id=collective,
            has_side_effects=collective is not None,
            vmem_limit_bytes=VMEM_BYTES,
        ),
    )(*ins.values())
    return types.SimpleNamespace(**dict(zip(written, results)))


class Group:
    def __init__(self):
        self.me = lax.axis_index("tensor")
        chip = self.me // 2
        core = self.me % 2
        self.sib = chip * 2 + (1 - core)
        self.opp = (1 - chip) * 2 + core
        self.diag = (1 - chip) * 2 + (1 - core)

    def greet(self, more=()):
        barrier = pltpu.get_barrier_semaphore()
        for device in more:
            pl.semaphore_signal(barrier, inc=1, device_id={"dp": device}, device_id_type=MESH)
        for device in (self.sib, self.opp, self.diag):
            pl.semaphore_signal(barrier, inc=1, device_id={"tensor": device}, device_id_type=MESH)
        pl.semaphore_wait(barrier, 3 + len(more))


class Gather:
    def __init__(self, stage, group, source, place, pieces):
        self.g = group
        self.pieces = pieces
        base = stage.sems(3 * pieces)
        opp = {"tensor": group.opp}
        sib = {"tensor": group.sib}
        self.to_opp = [
            stage.remote(source(s), place(group.me, s), base, s, opp) for s in range(pieces)
        ]
        self.to_sib = [
            stage.remote(source(s), place(group.me, s), base, pieces + s, sib)
            for s in range(pieces)
        ]
        self.passed = [
            stage.remote(place(group.opp, s), place(group.opp, s), base, 2 * pieces + s, sib)
            for s in range(pieces)
        ]

    def send(self, s):
        self.to_opp[s].start()
        self.to_sib[s].start()

    def forward(self, s):
        self.to_opp[s].wait_recv()
        self.passed[s].start()

    def near(self):
        for s in range(self.pieces):
            self.to_sib[s].wait_recv()

    def far(self):
        for s in range(self.pieces):
            self.passed[s].wait_recv()

    def close(self):
        for copy in self.to_opp + self.to_sib + self.passed:
            copy.wait_send()


class Scatter:
    def __init__(self, stage, group, name, pieces, order=None):
        self.order = list(order or range(pieces))
        self.out_diag = stage[name + "_od"]
        self.out_sib = stage[name + "_os"]
        self.out_opp = stage[name + "_oo"]
        self.in_opp = stage[name + "_io"]
        self.in_own = stage[name + "_iw"]
        self.in_far = stage[name + "_if"]
        self.rows = self.out_diag.shape[0] // pieces
        base = stage.sems(3 * pieces)

        def copies(source, target, first, device):
            return [
                stage.remote(
                    source.at[self.part(s)], target.at[self.part(s)], base, first + s, {"tensor": device}
                )
                for s in range(pieces)
            ]

        self.first = copies(self.out_diag, self.in_opp, 0, group.sib)
        self.second = copies(self.out_sib, self.in_own, pieces, group.sib)
        self.across = copies(self.out_opp, self.in_far, 2 * pieces, group.opp)

    def part(self, s):
        return pl.ds(s * self.rows, self.rows)

    def put_diag(self, value):
        for s in self.order:
            self.out_diag[self.part(s), :] = value(s).astype(bf16)
            self.first[s].start()

    def put_opp(self, value):
        for s in self.order:
            mine = value(s)
            self.first[s].wait_recv()
            total = mine + self.in_opp[self.part(s), :].astype(f32)
            self.out_opp[self.part(s), :] = total.astype(bf16)
            self.across[s].start()

    def put_sib(self, value):
        self.fill_sib(value)
        self.send_sib()

    def fill_sib(self, value):
        for s in self.order:
            self.out_sib[self.part(s), :] = value(s).astype(bf16)

    def send_sib(self):
        for s in self.order:
            self.second[s].start()

    def take(self, s, own):
        self.second[s].wait_recv()
        near = own + self.in_own[self.part(s), :].astype(f32)
        self.across[s].wait_recv()
        return near + self.in_far[self.part(s), :].astype(f32)

    def close(self):
        for copy in self.first + self.second + self.across:
            copy.wait_send()


def pieces_of(value, count):
    rows = value.shape[0] // count
    return lambda s: value[s * rows : (s + 1) * rows]


def scatter_buffers(name, rows, width):
    return {
        name + tail: ((rows, width), bf16) for tail in ("_od", "_os", "_oo", "_io", "_iw", "_if")
    }


def ring_seats(count):
    index = lax.axis_index("dp")
    place = jnp.where(index % 2 == 0, index // 2, count - 1 - index // 2)

    def seat(p):
        p = lax.rem(p + 2 * count, count)
        return jnp.where(2 * p < count, 2 * p, 2 * (count - 1 - p) + 1)

    return place, seat


def ring_rows(shape, kind, count):
    tile = 16 if kind == bf16 else SUB
    if shape[0] % (2 * count * tile) == 0:
        return shape[0] // (2 * count), shape[1]
    if shape[0] % (count * tile) == 0 and shape[1] % (2 * LANES) == 0:
        return shape[0] // count, shape[1] // 2
    return None


class Ring:
    def __init__(self, m, count, items):
        self.m = m
        self.count = count
        self.items = items
        self.place, self.seat = ring_seats(count)
        self.steps = 2 * (count - 1)
        self.base = m.sems(len(items) * 2 * count, len(items) * 2)
        self.step = 0

    def view(self, ref, chunk, way):
        shape = ref.shape
        rows, columns = ring_rows(shape, ref.dtype, self.count)
        chunk = lax.rem(chunk + 2 * self.count, self.count)
        if columns == shape[1]:
            return ref.at[pl.ds(pl.multiple_of((2 * chunk + way) * rows, rows), rows), :]
        return ref.at[
            pl.ds(pl.multiple_of(chunk * rows, rows), rows), pl.ds(way * columns, columns)
        ]

    def slot(self, item, way, step):
        own, box, _ = self.items[item]
        if len(box.shape) == 4:
            return box.at[way, step]
        rows, columns = ring_rows(own.shape, own.dtype, self.count)
        first = (way * (self.count - 1) + step) * rows
        return box.at[pl.ds(first, rows), pl.ds(0, columns)]

    def copy(self, item, way, step):
        own = self.items[item][0]
        sign = 1 - 2 * way
        last = self.count - 1
        place = 2 * item + way
        index = place * self.count + step % self.count
        if step < last:
            source = self.view(own, self.place, way) if step == 0 else self.slot(item, way, step - 1)
            target = self.slot(item, way, step)
        else:
            source = self.view(own, self.place + sign - sign * (step - last), way)
            target = source
        device = {"dp": self.seat(self.place + sign)}
        return self.m.remote(source, target, self.base, index, device, place)

    def start(self, item, way, step):
        self.copy(item, way, step).start()

    def begin(self):
        for item in range(len(self.items)):
            for way in range(2):
                self.start(item, way, 0)

    def tick(self):
        last = self.count - 1
        step = self.step
        self.step = step + 1
        for item, (own, _, name) in enumerate(self.items):
            for way in range(2):
                sign = 1 - 2 * way
                self.copy(item, way, step).wait_recv()
                self.copy(item, way, step).wait_send()
                if step < last:
                    chunk = self.view(own, self.place - sign * (step + 1), way)
                    box = self.slot(item, way, step)
                    value = box[...].astype(f32) + chunk[...].astype(f32)
                    if step < last - 1:
                        box[...] = value.astype(own.dtype)
                    else:
                        chunk[...] = value.astype(own.dtype)
                if step + 1 < self.steps:
                    self.start(item, way, step + 1)
                if step >= last - 1:
                    self.keep(own, name, self.place + sign - sign * (step + 1 - last), way)
        return step + 1 == self.steps

    def keep(self, own, name, chunk, way):
        out = self.m.hbm_out[name]
        sem = self.m.flush_sem.at[self.m.out_order[name]]
        pltpu.make_async_copy(self.view(own, chunk, way), self.view(out, chunk, way), sem).start()

    def close(self):
        for own, _, name in self.items:
            sem = self.m.flush_sem.at[self.m.out_order[name]]
            pltpu.make_async_copy(own, self.m.hbm_out[name], sem).wait()


class Direct:
    def __init__(self, m, count, items):
        self.m = m
        self.count = count
        self.items = items
        self.me = lax.axis_index("dp")
        self.base = m.sems(2 * len(items) * (count - 1))
        self.step = 0
        self.steps = 2

    def share(self, ref, index):
        return ref.at[at(index, ref.shape[0] // self.count), :]

    def copies(self, step):
        made = []
        for item, (own, box, total, _) in enumerate(self.items):
            for r in range(1, self.count):
                there = lax.rem(self.me + r, self.count)
                index = (2 * item + step) * (self.count - 1) + r - 1
                if step == 0:
                    source, target = self.share(own, there), box.at[r - 1]
                else:
                    source = target = self.share(total, self.me)
                made.append(self.m.remote(source, target, self.base, index, {"dp": there}))
        return made

    def begin(self):
        for copy in self.copies(0):
            copy.start()

    def tick(self):
        for copy in self.copies(self.step):
            copy.wait_recv()
        if self.step == 0:
            for own, box, total, _ in self.items:
                value = self.share(own, self.me)[...].astype(f32)
                for r in range(self.count - 1):
                    value = value + box[r].astype(f32)
                self.share(total, self.me)[...] = value.astype(total.dtype)
            for copy in self.copies(1):
                copy.start()
        self.step += 1
        return self.step == 2

    def close(self):
        for copy in self.copies(0) + self.copies(1):
            copy.wait_send()
        for _, _, total, name in self.items:
            self.m.store(total, name)


class Turns:
    def __init__(self):
        self.waiting = []
        self.rings = []
        self.last = None

    def begin(self, ring):
        ring.begin()
        self.waiting.append(ring)
        self.rings.append(ring)

    def tick(self):
        if self.waiting:
            others = [ring for ring in self.waiting if ring is not self.last] or self.waiting
            ring = max(others, key=lambda one: one.steps - one.step)
            self.last = ring
            if ring.tick():
                self.waiting.remove(ring)

    def close(self):
        while self.waiting:
            self.tick()
        for ring in self.rings:
            ring.close()


def ring_box(shape, kind, count):
    rows, columns = ring_rows(shape, kind, count)
    return ((2, count - 1, rows, columns), kind)


def direct_box(shape, kind, count):
    return ((count - 1, shape[0] // count, shape[1]), kind)


def ring_fits(shapes, count):
    return (
        count > 1
        and count % 2 == 0
        and all(ring_rows(shape, kind, count) for shape, kind in shapes)
    )


def groups(array):
    halves = array.shape[0] // SUB
    sides = array.shape[1] // LANES
    return [
        array[SUB * s : SUB * s + SUB, LANES * l : LANES * l + LANES]
        for s in range(halves)
        for l in range(sides)
    ]


def spread_row(ref, index):
    return jnp.broadcast_to(ref[index], (SUB, LANES))


def advance(state, coefs, keep, signals, sides):
    root_real, root_imag = coefs
    half = len(state) // 2
    kept = [value * keep for value in state]
    fresh = [None] * len(state)
    for g in range(half):
        a_real, a_imag = kept[g], kept[half + g]
        fresh[g] = (root_real[g] * a_real - root_imag[g] * a_imag) + signals[g % sides]
        fresh[half + g] = root_real[g] * a_imag + root_imag[g] * a_real
    return kept, fresh


def filter_forward(m, first, count, state):
    sides = m.xl.shape[0]
    tables = m.tab
    root_real, root_imag = groups(tables[0]), groups(tables[1])
    out_real, out_imag = groups(tables[2]), groups(tables[3])
    half = len(root_real)
    unroll = 16

    def chunk(ch, state):
        for g in range(2 * half):
            m.st[ch, g] = state[g]

        def steps(i, state):
            state = list(state)
            for j in range(unroll):
                t = ch * SPAN + i * unroll + j
                keep = spread_row(m.kf, (pl.ds(t, 1), slice(None)))
                signals = [
                    spread_row(m.xl, (l, pl.ds(t, 1), slice(None))) for l in range(sides)
                ]
                _, state = advance(state, (root_real, root_imag), keep, signals, sides)
                for l in range(sides):
                    total = None
                    for g in range(l, half, sides):
                        term = out_real[g] * state[g] - out_imag[g] * state[half + g]
                        total = term if total is None else total + term
                    m.part[l, pl.ds(pl.multiple_of((i * unroll + j) * SUB, SUB), SUB), :] = total
            return tuple(state)

        state = lax.fori_loop(0, SPAN // unroll, steps, state)
        rows = at(ch, SPAN)
        for l in range(sides):
            lanes = slice(LANES * l, LANES * l + LANES)
            value = m.om[:, lanes] * m.xl[l, rows, :]
            for s in range(SUB):
                value = value + m.part[l, pl.ds(s, SPAN, stride=SUB), :]
            gate = sigmoid(value)
            m.mxl[rows, lanes] = (value * gate).astype(bf16)
            m.se[rows, lanes] = (gate * (1.0 + value * (1.0 - gate))).astype(bf16)
        return state

    return lax.fori_loop(first, first + count, chunk, state)


def window_mask(m, first_row, rows, first_key, keys):
    here = m.segb[pl.ds(pl.multiple_of(first_row + SUB, SUB), rows), :][:, :1]
    same = here == m.segr[:, pl.ds(pl.multiple_of(first_key, LANES), keys)].astype(f32)
    row = first_row + lax.broadcasted_iota(jnp.int32, (rows, keys), 0)
    key = first_key + lax.broadcasted_iota(jnp.int32, (rows, keys), 1)
    return same & (row >= key)


def window_of(index, block, length):
    back = -(-MAX_DOC // block)
    keys = min((back + 1) * block, length)
    first = jnp.maximum(index - back, 0) * block
    first = jnp.minimum(first, length - keys)
    return pl.multiple_of(first, LANES), keys


def keeping(m):
    length = m.segr.shape[1]
    m.segb[:SUB, :] = jnp.full((SUB, LANES), -1.0, f32)
    for k in range(length // LANES):
        row = m.segr[:, k * LANES : (k + 1) * LANES].astype(f32)
        m.segb[SUB + k * LANES : SUB + (k + 1) * LANES, :] = jnp.broadcast_to(row, (LANES, LANES)).T
    for k in range(length // LANES):
        now = m.segb[SUB + k * LANES : SUB + (k + 1) * LANES, :]
        before = m.segb[SUB - 1 + k * LANES : SUB - 1 + (k + 1) * LANES, :]
        m.kf[k * LANES : (k + 1) * LANES, :] = jnp.where(now == before, 1.0, 0.0)
    m.kf[length:, :] = jnp.zeros((SUB, LANES), f32)


def filter_tables(m):
    alpha, delta, theta, beta, e_re, e_im = (
        ref[...] for ref in (m.p0, m.p1, m.p2, m.p3, m.p4, m.p5)
    )
    magnitude = 1.0 - alpha * delta
    cosine, sine = jnp.cos(theta), jnp.sin(theta)
    scaled = alpha * beta
    entries = (
        magnitude * cosine, magnitude * sine, scaled * e_re, scaled * e_im,
        cosine, sine, alpha, delta, beta, e_re, e_im,
    )
    for k, entry in enumerate(entries):
        m.tab[k] = entry


def forward_attention(m, g):
    length, width = m.xt.shape
    block = m.tok.shape[0]
    blocks = length // block
    channels = m.mxl.shape[1]
    sides = channels // LANES
    own = at(g.me, block)
    half = block // 2
    tokens = Gather(
        m, g,
        lambda s: m.tok.at[pl.ds(s * half, half), :],
        lambda j, s: m.xt.at[pl.ds(pl.multiple_of(j * block + s * half, half), half), :],
        2,
    )
    shared = Gather(m, g, lambda s: m.wsh, lambda j, s: m.wsf.at[at(j, channels), :], 1)
    pieces = 8
    rows_piece = length // pieces
    mixed = Gather(
        m, g,
        lambda s: m.mxl.at[pl.ds(s * rows_piece, rows_piece), :],
        lambda j, s: m.mx.at[pl.ds(s * rows_piece, rows_piece), at(j, channels)],
        pieces,
    )
    cots = Gather(
        m, g,
        lambda s: m.cot.at[pl.ds(s * half, half), :],
        lambda j, s: m.cotf.at[pl.ds(pl.multiple_of(j * block + s * half, half), half), :],
        2,
    )
    normed = Gather(
        m, g,
        lambda s: m.yno.at[pl.ds(s * half, half), :],
        lambda j, s: m.yn.at[pl.ds(pl.multiple_of(j * block + s * half, half), half), :],
        2,
    )
    branch = Scatter(m, g, "xv", 2)

    m.need(m.tok, m.wsh)
    tokens.send(0)
    tokens.send(1)
    shared.send(0)
    m.need(m.cot)
    cots.send(0)
    m.xt[own, :] = m.tok[...]
    m.wsf[at(g.me, channels), :] = m.wsh[...]
    m.need(m.segr, m.p0, m.p1, m.p2, m.p3, m.p4, m.p5, m.gain, m.om)
    keeping(m)
    filter_tables(m)

    lane = lax.broadcasted_iota(jnp.int32, (SPAN, LANES), 1)

    def sums(j):
        def part(i, _):
            rows = pl.ds(pl.multiple_of(j * block + i * SPAN, SPAN), SPAN)
            one = jnp.zeros((SPAN, LANES), f32)
            two = jnp.zeros((SPAN, LANES), f32)
            for l in range(width // LANES):
                x = m.xt[rows, LANES * l : LANES * l + LANES].astype(f32)
                one = one + x
                two = two + x * x
            picked = jnp.where(lane == 6, 1.0, 0.0)
            for k, total in ((0, one), (3, two)):
                rest = jnp.sum(total, axis=1, keepdims=True)
                for n in range(3):
                    top = rest.astype(bf16).astype(f32)
                    picked = jnp.where(lane == k + n, top, picked)
                    rest = rest - top
            m.sums[rows, :] = picked.astype(bf16)
            return 0

        lax.fori_loop(0, block // SPAN, part, 0)

    sums(g.me)
    tokens.near()
    sums(g.sib)
    tokens.forward(0)
    tokens.forward(1)
    sums(g.opp)
    tokens.far()
    sums(g.diag)

    lane_wide = lax.broadcasted_iota(jnp.int32, (block, LANES), 1)

    def statistics(i, _):
        first, keys = window_of(i, block, length)
        seen = window_mask(m, i * block, block, first, keys).astype(bf16)
        got = plain(seen, m.sums[pl.ds(first, keys), :])
        pick = lambda low, high: jnp.sum(
            jnp.where((lane_wide >= low) & (lane_wide < high), got, 0.0), axis=1, keepdims=True
        )
        total = pick(6, 7) * width
        mean = pick(0, 3) / total
        var = pick(3, 6) / total - mean * mean
        rows = at(i, block)
        m.mean[rows, :] = jnp.broadcast_to(mean, (block, LANES))
        m.rstd[rows, :] = jnp.broadcast_to(lax.rsqrt(var + epsilon), (block, LANES))

        @pl.when(i == g.me)
        def _():
            m.so[0] = m.mean[rows, :]
            m.so[1] = m.rstd[rows, :]
            m.so[2] = jnp.broadcast_to(total, (block, LANES))

        return 0

    lax.fori_loop(0, blocks, statistics, 0)

    def normalise(i, _):
        rows = at(i, SPAN)
        mean, rstd = m.mean[rows, :], m.rstd[rows, :]
        for l in range(width // LANES):
            lanes = slice(LANES * l, LANES * l + LANES)
            x = m.xt[rows, lanes].astype(f32)
            m.xn[rows, lanes] = ((x - mean) * rstd * m.gain[:, lanes]).astype(bf16)
        for l in range(sides):
            lanes = pl.ds(pl.multiple_of(g.me * channels + LANES * l, LANES), LANES)
            x = m.xt[rows, lanes].astype(f32)
            m.xl[l, rows, :] = (x - mean) * rstd * m.gain[:, lanes]
        return 0

    lax.fori_loop(0, length // SPAN, normalise, 0)
    tokens.close()

    zero = jnp.zeros((SUB, LANES), f32)
    state = tuple(zero for _ in range(m.st.shape[1]))
    per = length // SPAN // pieces
    for p in range(pieces):
        state = filter_forward(m, p * per, per, state)
        mixed.send(p)
        if p >= 2:
            mixed.forward(p - 2)
    cots.send(1)
    for i in range(pieces):
        m.mx[pl.ds(i * rows_piece, rows_piece), at(g.me, channels)] = m.mxl[
            pl.ds(i * rows_piece, rows_piece), :
        ]
    m.cotf[own, :] = m.cot[...]
    m.need(m.wv)

    def values(i, _):
        rows = at(i, block)
        pre = plain(m.xn[rows, :], m.wv[...])
        gate = sigmoid(pre)
        m.v[rows, :] = (pre * gate).astype(bf16)
        m.sv[rows, :] = (gate * (1.0 + pre * (1.0 - gate))).astype(bf16)
        return 0

    lax.fori_loop(0, blocks, values, 0)
    for p in range(max(pieces - 2, 0), pieces):
        mixed.forward(p)
    shared.forward(0)
    shared.near()
    shared.far()
    mixed.near()
    mixed.far()
    m.need(m.qg, m.qb, m.kg, m.wag, m.wo, m.rg)

    def project(i, _):
        rows = at(i, block)
        z = plain(m.mx[rows, :], m.wsf[...])
        m.z[rows, :] = z.astype(bf16)
        m.q[rows, :] = (z * m.qg[...] + m.qb[...]).astype(bf16)
        m.k[rows, :] = (z * m.kg[...]).astype(bf16)
        return 0

    lax.fori_loop(0, blocks, project, 0)
    scale = 1.0 / math.sqrt(m.q.shape[1])

    def attend(i):
        rows = at(i, block)
        first, keys = window_of(i, block, length)
        window = pl.ds(first, keys)
        scores = cross(m.q[rows, :], m.k[window, :]) * scale
        scores = jnp.where(window_mask(m, i * block, block, first, keys), scores, masked_score)
        expo = jnp.exp(scores - jnp.max(scores, axis=1, keepdims=True))
        prob = (expo / jnp.sum(expo, axis=1, keepdims=True)).astype(bf16)
        m.p[i] = prob
        attended = plain(prob, m.v[window, :])
        pre = plain(m.mx[rows, :], m.wag[...])
        gate = sigmoid(pre)
        swish = pre * gate
        m.r[rows, :] = swish.astype(bf16)
        m.os[rows, :] = (attended * (gate * (1.0 + pre * (1.0 - gate)))).astype(bf16)
        m.w[rows, :] = (attended * swish).astype(bf16)
        return plain(m.w[rows, :], m.wo[...])

    branch.put_diag(pieces_of(attend(g.diag), 2))
    branch.put_opp(pieces_of(attend(g.opp), 2))
    cots.forward(0)
    branch.put_sib(pieces_of(attend(g.sib), 2))
    cots.forward(1)
    m.bp[...] = attend(g.me)
    for s in range(2):
        piece = pl.ds(s * half, half)
        y = branch.take(s, m.bp[piece, :]) + m.tok[piece, :].astype(f32)
        m.y[piece, :] = y
        rms = lax.rsqrt(jnp.mean(y * y, axis=1, keepdims=True) + epsilon)
        m.rs[piece, :] = jnp.broadcast_to(rms, (half, LANES))
        m.yno[piece, :] = (y * rms * m.rg[...]).astype(bf16)
        normed.send(s)
    m.yn[own, :] = m.yno[...]
    for moved in (shared, mixed, branch):
        moved.close()
    return cots, normed


def transposed_product(left, right, out, step):
    def part(i, _):
        columns = at(i, step)
        out[columns, :] = inner(left[:, columns], right[...]).astype(bf16)
        return 0

    lax.fori_loop(0, left.shape[1] // step, part, 0)


def feed_forward(m, g, cots, normed, turns, begin):
    length, width = m.yn.shape
    block = m.y.shape[0]
    half = block // 2
    grads = Scatter(m, g, "xv", 2)
    back = Gather(
        m, g,
        lambda s: m.dyo.at[pl.ds(s * half, half), :],
        lambda j, s: m.dyf.at[pl.ds(pl.multiple_of(j * block + s * half, half), half), :],
        2,
    )
    m.need(m.wg, m.wu, m.wd)

    def lead(j):
        rows = at(j, block)
        m.dg[rows, :] = cross(m.cotf[rows, :], m.wd[...]).astype(bf16)

    def feed(j):
        rows = at(j, block)
        low = m.yn[rows, :]
        gate = plain(low, m.wg[...])
        up = plain(low, m.wu[...])
        d_act = m.dg[rows, :].astype(f32)
        sig = sigmoid(gate)
        swish = gate * sig
        m.act[rows, :] = (swish * up).astype(bf16)
        m.dg[rows, :] = (d_act * up * (sig * (1.0 + gate * (1.0 - sig)))).astype(bf16)
        m.du[rows, :] = (d_act * swish).astype(bf16)
        return cross(m.dg[rows, :], m.wg[...]) + cross(m.du[rows, :], m.wu[...])

    lead(g.me)
    m.bp[...] = feed(g.me)
    cots.near()
    normed.near()
    lead(g.sib)
    grads.fill_sib(pieces_of(feed(g.sib), 2))
    normed.forward(0)
    cots.far()
    cots.close()
    lead(g.diag)
    lead(g.opp)
    normed.forward(1)
    normed.far()
    grads.put_diag(pieces_of(feed(g.diag), 2))
    m.dy[...] = feed(g.opp)
    transposed_product(m.act, m.cotf, m.gd, LANES)
    begin(0)
    grads.send_sib()
    grads.put_opp(lambda s: m.dy[pl.ds(s * half, half), :])
    transposed_product(m.yn, m.dg, m.gg, 2 * LANES)
    turns.tick()
    transposed_product(m.yn, m.du, m.gu, 2 * LANES)
    begin(1)
    turns.tick()
    turns.tick()
    normed.close()
    m.need(m.y, m.rs, m.cot, m.rg)
    gain_sum = jnp.zeros((1, width), f32)
    for s in range(2):
        piece = pl.ds(s * half, half)
        d_yn = grads.take(s, m.bp[piece, :])
        rms = m.rs[piece, :][:, :1]
        hat = m.y[piece, :] * rms
        gain_sum = gain_sum + jnp.sum(d_yn * hat, axis=0, keepdims=True)
        d_hat = d_yn * m.rg[...]
        pull = d_hat - hat * jnp.mean(d_hat * hat, axis=1, keepdims=True)
        dy = m.cot[piece, :].astype(f32) + rms * pull
        m.dy[piece, :] = dy
        m.dyo[piece, :] = dy.astype(bf16)
        back.send(s)
    m.gr[...] = gain_sum
    m.dyf[at(g.me, block), :] = m.dyo[...]
    grads.close()
    return back


def filter_backward(m, last, count, gamma):
    sides = m.xl.shape[0]
    tables = m.tab
    root_real, root_imag = groups(tables[0]), groups(tables[1])
    out_real, out_imag = groups(tables[2]), groups(tables[3])
    half = len(root_real)
    unroll = 8

    def chunk(step, gamma):
        ch = last - step

        def again(i, state):
            state = list(state)
            for j in range(unroll):
                local = i * unroll + j
                t = ch * SPAN + local
                keep = spread_row(m.kf, (pl.ds(t, 1), slice(None)))
                signals = [
                    spread_row(m.xl, (l, pl.ds(t, 1), slice(None))) for l in range(sides)
                ]
                kept, state = advance(state, (root_real, root_imag), keep, signals, sides)
                for g in range(2 * half):
                    m.kept[local, g] = kept[g]
            return tuple(state)

        lax.fori_loop(0, SPAN // unroll, again, tuple(m.st[ch, g] for g in range(2 * half)))

        def reverse(i, carry):
            gamma, sums = list(carry[: 2 * half]), list(carry[2 * half :])
            for j in range(unroll):
                local = SPAN - 1 - (i * unroll + j)
                t = ch * SPAN + local
                keep = spread_row(m.kf, (pl.ds(t + 1, 1), slice(None)))
                signals = [
                    spread_row(m.dq, (l, pl.ds(t, 1), slice(None))) for l in range(sides)
                ]
                _, gamma = advance(gamma, (root_real, root_imag), keep, signals, sides)
                for l in range(sides):
                    total = None
                    for g in range(l, half, sides):
                        g_real, g_imag = gamma[g], gamma[half + g]
                        a_real, a_imag = m.kept[local, g], m.kept[local, half + g]
                        term = out_real[g] * g_real - out_imag[g] * g_imag
                        total = term if total is None else total + term
                        sums[g] = sums[g] + (g_real * a_real - g_imag * a_imag)
                        sums[half + g] = sums[half + g] + (g_real * a_imag + g_imag * a_real)
                        sums[2 * half + g] = sums[2 * half + g] + signals[l] * a_real
                        sums[3 * half + g] = sums[3 * half + g] + signals[l] * a_imag
                    m.part[l, pl.ds(pl.multiple_of(local * SUB, SUB), SUB), :] = total
            return tuple(gamma) + tuple(sums)

        start = tuple(gamma) + tuple(m.acc[g] for g in range(4 * half))
        done = lax.fori_loop(0, SPAN // unroll, reverse, start)
        for g in range(4 * half):
            m.acc[g] = done[2 * half + g]
        rows = at(ch, SPAN)
        for l in range(sides):
            lanes = slice(LANES * l, LANES * l + LANES)
            signal = m.dq[l, rows, :]
            value = m.om[:, lanes] * signal
            for s in range(SUB):
                value = value + m.part[l, pl.ds(s, SPAN, stride=SUB), :]
            m.dxb[rows, lanes] = value.astype(bf16)
            m.go[:, lanes] = m.go[:, lanes] + jnp.sum(
                signal * m.xl[l, rows, :], axis=0, keepdims=True
            )
        return done[: 2 * half]

    return lax.fori_loop(0, count, chunk, gamma)


def filter_gradients(m):
    sides = m.xl.shape[0]
    half = m.acc.shape[0] // 4
    dims = m.tab.shape[1]
    for g in range(half):
        s, l = g // sides, g % sides
        rows = slice(SUB * s, SUB * s + SUB)
        lanes = slice(LANES * l, LANES * l + LANES)
        q_re, q_im, c_re, c_im, cosine, sine, alpha, delta, beta, e_re, e_im = (
            m.tab[k, rows, lanes] for k in range(11)
        )
        lag_re, lag_im, sum_re, sum_im = (m.acc[k * half + g] for k in range(4))
        f_re = q_re * sum_re - q_im * sum_im + m.go[:, lanes]
        f_im = q_re * sum_im + q_im * sum_re
        scaled = alpha * beta
        d_scaled = e_re * f_re - e_im * f_im
        w_re = c_re * lag_re - c_im * lag_im
        w_im = c_re * lag_im + c_im * lag_re
        d_mag = w_re * cosine - w_im * sine
        m.pk[0 * dims + SUB * s : 0 * dims + SUB * s + SUB, lanes] = beta * d_scaled - delta * d_mag
        m.pk[1 * dims + SUB * s : 1 * dims + SUB * s + SUB, lanes] = -alpha * d_mag
        m.pk[2 * dims + SUB * s : 2 * dims + SUB * s + SUB, lanes] = -(w_re * q_im + w_im * q_re)
        m.pk[3 * dims + SUB * s : 3 * dims + SUB * s + SUB, lanes] = alpha * d_scaled
        m.pk[4 * dims + SUB * s : 4 * dims + SUB * s + SUB, lanes] = scaled * f_re
        m.pk[5 * dims + SUB * s : 5 * dims + SUB * s + SUB, lanes] = -scaled * f_im


def backward_attention(m, g, back, turns, begin):
    length, width = m.mx.shape
    block = m.tok.shape[0]
    blocks = length // block
    half = block // 2
    channels = m.se.shape[1]
    shared = m.q.shape[1]
    sides = channels // LANES
    fed = Scatter(m, g, "xv", 2)
    pieces = 4
    dm = Scatter(m, g, "dm", pieces, range(pieces - 1, -1, -1))
    sh = Scatter(m, g, "sh", 1)
    others = (g.sib, g.opp, g.diag)
    base = m.sems(9)
    parts = [
        m.remote(m.dxb.at[at(dev, block), :], m.dxr.at[k], base, k, {"tensor": dev})
        for k, dev in enumerate(others)
    ]
    small = [
        m.remote(m.smo, m.sm.at[g.me], base, 3 + k, {"tensor": dev})
        for k, dev in enumerate(others)
    ]
    tails = [
        m.remote(m.aro, m.ar.at[:, at(g.me, block)], base, 6 + k, {"tensor": dev})
        for k, dev in enumerate(others)
    ]

    scale = 1.0 / math.sqrt(shared)
    m.dk[...] = jnp.zeros(m.dk.shape, f32)
    m.dv[...] = jnp.zeros(m.dv.shape, f32)
    turns.tick()
    turns.tick()
    back.forward(0)
    turns.tick()
    back.forward(1)
    turns.tick()
    back.near()
    back.far()
    share = lambda j: plain(m.act[at(j, block), :], m.wd[...])
    fed.put_diag(pieces_of(share(g.diag), 2))
    fed.put_opp(pieces_of(share(g.opp), 2))
    turns.tick()
    fed.put_sib(pieces_of(share(g.sib), 2))
    m.bp[...] = share(g.me)
    m.need(m.w, m.wo, m.r, m.os, m.v, m.p, m.k, m.q)
    transposed_product(m.w, m.dyf, m.gao, 2 * LANES)
    turns.tick()

    def attend(i, _):
        rows = at(i, block)
        first, keys = window_of(i, block, length)
        window = pl.ds(first, keys)
        d_w = cross(m.dyf[rows, :], m.wo[...])
        d_o = (d_w * m.r[rows, :].astype(f32)).astype(bf16)
        m.drp[rows, :] = (d_w * m.os[rows, :].astype(f32)).astype(bf16)
        prob_low = m.p[i]
        prob = prob_low.astype(f32)
        weighed = prob * cross(d_o, m.v[window, :])
        d_s = (weighed - prob * jnp.sum(weighed, axis=1, keepdims=True)) * scale
        d_s = d_s.astype(bf16)
        d_q = plain(d_s, m.k[window, :])
        for l in range(shared // LANES):
            m.dq[l, rows, :] = d_q[:, LANES * l : LANES * l + LANES]
        m.dk[window, :] = m.dk[window, :] + inner(d_s, m.q[rows, :])
        m.dv[window, :] = m.dv[window, :] + inner(prob_low, d_o)
        return 0

    for n in range(blocks):
        attend(n, 0)
        turns.tick()
    m.need(m.z, m.qg, m.kg, m.sv, m.wsf, m.wag)

    def affine(i, sums):
        rows = at(i, block)
        d_q = jnp.concatenate([m.dq[l, rows, :] for l in range(shared // LANES)], axis=1)
        d_k, z = m.dk[rows, :], m.z[rows, :].astype(f32)
        m.dz[rows, :] = (d_q * m.qg[...] + d_k * m.kg[...]).astype(bf16)
        m.dvp[rows, :] = (m.dv[rows, :] * m.sv[rows, :].astype(f32)).astype(bf16)
        new = (d_q * z, d_q, d_k * z)
        return tuple(s + jnp.sum(n, axis=0, keepdims=True) for s, n in zip(sums, new))

    aff = lax.fori_loop(0, blocks, affine, tuple(jnp.zeros((1, shared), f32) for _ in range(3)))
    m.smo[...] = jnp.zeros(m.smo.shape, f32)
    for n in range(3):
        m.smo[2 + n : 3 + n, :shared] = aff[n]

    def mixing(j):
        def value(s):
            rows = pl.ds(s * (length // pieces), length // pieces)
            return cross(m.dz[rows, :], m.wsf[at(j, channels), :]) + cross(
                m.drp[rows, :], m.wag[at(j, channels), :]
            )

        return value

    m.need(m.y)
    for s in range(2):
        piece = pl.ds(s * half, half)
        m.out[piece, :] = (fed.take(s, m.bp[piece, :]) + m.y[piece, :]).astype(bf16)
    m.flush(m.out)
    fed.close()
    m.need(m.mx, m.xn)
    transposed_product(m.mx, m.drp, m.r, 2 * LANES)
    turns.tick()
    transposed_product(m.xn, m.dvp, m.os, 2 * LANES)
    begin(2)
    dm.put_diag(mixing(g.diag))
    turns.tick()
    dm.put_opp(mixing(g.opp))
    turns.tick()
    dm.put_sib(mixing(g.sib))
    turns.tick()
    m.need(m.wv)
    xv = Scatter(m, g, "xv", 2)
    spread = lambda j: pieces_of(cross(m.dvp[at(j, block), :], m.wv[...]), 2)
    split = lambda j: (lambda s: inner(m.mx[:, at(j, channels)], m.dz[...]))

    def spreading():
        xv.put_diag(spread(g.diag))
        xv.put_opp(spread(g.opp))
        turns.tick()
        xv.put_sib(spread(g.sib))
        m.bp[...] = cross(m.dvp[at(g.me, block), :], m.wv[...])
        turns.tick()
        sh.put_diag(split(g.diag))
        sh.put_opp(split(g.opp))
        turns.tick()
        sh.put_sib(split(g.sib))
        m.shp[...] = split(g.me)(0)
        turns.tick()

    m.need(m.se, m.st, m.xl, m.kf, m.tab, m.om)
    half_states = m.acc.shape[0] // 4
    m.acc[...] = jnp.zeros(m.acc.shape, f32)
    m.go[...] = jnp.zeros(m.go.shape, f32)
    gamma = tuple(jnp.zeros((SUB, LANES), f32) for _ in range(2 * half_states))
    per = length // SPAN // pieces
    own_mix = mixing(g.me)
    for s in range(pieces - 1, -1, -1):
        rows = pl.ds(s * (length // pieces), length // pieces)
        d_e = dm.take(s, own_mix(s)) * m.se[rows, :].astype(f32)
        for l in range(sides):
            m.dq[l, rows, :] = d_e[:, LANES * l : LANES * l + LANES]
        for n in range(per - 1, -1, -2):
            gamma = filter_backward(m, s * per + n, 2, gamma)
            turns.tick()
            turns.tick()
        for k, dev in enumerate(others):

            @pl.when(dev == s)
            def _():
                parts[k].start()

        if s == pieces - 1:
            spreading()
    filter_gradients(m)
    base_row = m.pk.shape[0] - PACK_TAIL
    m.pk[base_row:, :] = jnp.zeros((PACK_TAIL, channels), f32)
    m.pk[base_row : base_row + 1, :] = m.go[...]
    m.gs[...] = sh.take(0, m.shp[...]).astype(bf16)
    turns.tick()
    m.need(m.tok, m.so, m.gain, m.dy, m.gr, m.segb, m.segr)
    for s in range(2):
        piece = pl.ds(s * half, half)
        m.bp[piece, :] = xv.take(s, m.bp[piece, :])
    own_columns = at(g.me, channels)
    m.bp[:, own_columns] = m.bp[:, own_columns] + m.dxb[at(g.me, block), :].astype(f32)
    for k, dev in enumerate(others):
        parts[k].wait_recv()
        columns = at(dev, channels)
        m.bp[:, columns] = m.bp[:, columns] + m.dxr[k].astype(f32)
    gain_sum = jnp.zeros((1, width), f32)
    lane = lax.broadcasted_iota(jnp.int32, (half, LANES), 1)
    for s in range(2):
        piece = pl.ds(s * half, half)
        mean, rstd, total = (m.so[n, piece, :][:, :1] for n in range(3))
        centred = m.tok[piece, :].astype(f32) - mean
        d_xn = m.bp[piece, :]
        gain_sum = gain_sum + jnp.sum(d_xn * (centred * rstd), axis=0, keepdims=True)
        d_hat = d_xn * m.gain[...]
        d_var = -0.5 * rstd * rstd * rstd * jnp.sum(d_hat * centred, axis=1, keepdims=True)
        one = (-rstd * jnp.sum(d_hat, axis=1, keepdims=True) - 2.0 * mean * d_var) / total
        two = d_var / total
        m.bp[piece, :] = d_hat * rstd + m.dy[piece, :]
        m.aw[piece, :] = jnp.where(lane == 0, one, jnp.where(lane == 1, two, 0.0))
    m.smo[0:1, :] = gain_sum
    m.smo[1:2, :] = m.gr[...]
    turned = m.aw[...].T
    for n in range(2):
        rest = turned[n : n + 1, :]
        for k in range(3):
            top = rest.astype(bf16).astype(f32)
            m.art[3 * n + k : 3 * n + k + 1, :] = top
            rest = rest - top
    m.art[6:8, :] = jnp.zeros((2, block), f32)
    m.art[8:16, :] = jnp.zeros((8, block), f32)
    m.aro[...] = m.art[...].astype(bf16)
    for copy in tails + small:
        copy.start()
    m.ar[:, at(g.me, block)] = m.aro[...]
    m.sm[g.me] = m.smo[...]
    reach = -(-MAX_DOC // block)
    keys = min((reach + 1) * block, length)
    first_key = pl.multiple_of(jnp.minimum(g.me * block, length - keys), LANES)
    first_row = pl.multiple_of(g.me * block, LANES)
    here = m.segb[pl.ds(pl.multiple_of(first_row + SUB, SUB), block), :][:, :1]
    same = here == m.segr[:, pl.ds(first_key, keys)].astype(f32)
    row = first_row + lax.broadcasted_iota(jnp.int32, (block, keys), 0)
    key = first_key + lax.broadcasted_iota(jnp.int32, (block, keys), 1)
    seen = (same & (row <= key)).astype(bf16)
    for copy in tails:
        copy.wait_recv()
    pulled = cross(seen, m.ar[:, pl.ds(first_key, keys)])
    b_one = pulled[:, 0:1] + pulled[:, 1:2] + pulled[:, 2:3]
    b_two = pulled[:, 3:4] + pulled[:, 4:5] + pulled[:, 5:6]
    for s in range(2):
        piece = pl.ds(s * half, half)
        rows = slice(s * half, (s + 1) * half)
        x = m.tok[piece, :].astype(f32)
        m.gt[piece, :] = (m.bp[piece, :] + b_one[rows] + 2.0 * x * b_two[rows]).astype(bf16)
    m.flush(m.gt)
    turns.tick()
    for copy in small:
        copy.wait_recv()
    total = m.sm[0]
    for j in range(1, m.sm.shape[0]):
        total = total + m.sm[j]
    per = width // channels
    for n in range(2):
        for k in range(per):
            row = base_row + 1 + n * per + k
            m.pk[row : row + 1, :] = total[n : n + 1, k * channels : (k + 1) * channels]
    for n in range(3):
        row = base_row + 1 + 2 * per + n
        m.pk[row : row + 1, :shared] = total[2 + n : 3 + n, :shared]
    begin(3)
    turns.close()
    for moved in (dm, xv, sh, back):
        moved.close()
    for copy in parts + small + tails:
        copy.wait_send()


def body(count, m):
    g = Group()
    m.load(m.tok, m.wsh, m.cot, m.segr, m.p0, m.p1, m.p2, m.p3, m.p4, m.p5)
    m.load(m.gain, m.om, m.wv, m.wag, m.qg, m.qb, m.kg, m.wo, m.rg, m.wg, m.wu, m.wd)
    m.refs.update(mean=m.dq.at[0], rstd=m.dq.at[1])
    turns = Turns()
    plans = (
        ((m.gd, "gdt"),),
        ((m.gg, "ggt"), (m.gu, "gut")),
        ((m.gao, "gaot"), (m.r, "gagt"), (m.os, "gvt")),
        ((m.gs, "gst"), (m.pk, "pkt")),
    )
    rings = None
    if count:
        rings = (
            Ring(m, count, [(m.gd, m.gdb, "gdt")]),
            Ring(m, count, [(m.gg, m.ggb, "ggt"), (m.gu, m.gub, "gut")]),
            Ring(m, count, [(m.gao, m.gaob, "gaot"), (m.r, m.gagb, "gagt"), (m.os, m.gvb, "gvt")]),
            Direct(m, count, [(m.gs, m.gsb, m.gss, "gst"), (m.pk, m.pkb, m.pks, "pkt")]),
        )
        here = lax.axis_index("dp")
        g.greet([lax.rem(here + r, count) for r in range(1, count)])
    else:
        g.greet()

    def begin(n):
        if rings:
            turns.begin(rings[n])
        else:
            for ref, name in plans[n]:
                m.store(ref, name)

    cots, normed = forward_attention(m, g)
    back = feed_forward(m, g, cots, normed, turns, begin)
    backward_attention(m, g, back, turns, begin)
    m.close()


def run(arrays, sizes, count):
    length, width, block, channels, shared, values, units = sizes
    blocks = length // block
    keys = min((-(-MAX_DOC // block) + 1) * block, length)
    sides = channels // LANES
    dims = arrays.p0.shape[0]
    half_states = sides * (dims // SUB)
    late = dict(
        gao=((values, width), bf16),
        gag=((width, values), bf16),
        gv=((width, values), bf16),
        gs=((channels, shared), bf16),
        pk=((6 * dims + PACK_TAIL, channels), f32),
    )
    summed = dict(
        gd=((units, width), bf16),
        gg=((width, units), bf16),
        gu=((width, units), bf16),
        **late,
    )
    if not ring_fits(summed.values(), count):
        count = 0
    outs = dict(
        gt=((block, width), bf16),
        out=((block, width), bf16),
    )
    scratch = dict(
        xt=((length, width), bf16),
        cotf=((length, width), bf16),
        xn=((length, width), bf16),
        mx=((length, width), bf16),
        xl=((sides, length, LANES), f32),
        tab=((11, dims, channels), f32),
        kf=((length + SUB, LANES), f32),
        segb=((length + SUB, LANES), f32),
        so=((3, block, LANES), f32),
        sums=((length, LANES), bf16),
        se=((length, channels), bf16),
        st=((length // SPAN, 2 * half_states, SUB, LANES), f32),
        v=((length, values), bf16),
        sv=((length, values), bf16),
        z=((length, shared), bf16),
        q=((length, shared), bf16),
        k=((length, shared), bf16),
        wsf=((width, shared), bf16),
        p=((blocks, block, keys), bf16),
        r=((length, values), bf16),
        os=((length, values), bf16),
        w=((length, values), bf16),
        y=((block, width), f32),
        rs=((block, LANES), f32),
        yno=((block, width), bf16),
        bp=((block, width), f32),
        act=((length, units), bf16),
        dg=((length, units), bf16),
        du=((length, units), bf16),
        gd=summed["gd"],
        dy=((block, width), f32),
        gr=((1, width), f32),
        dk=((length, shared), f32),
        dv=((length, values), f32),
        dq=((max(sides, shared // LANES), length, LANES), f32),
        shp=((channels, shared), f32),
        go=((1, channels), f32),
        acc=((4 * half_states, SUB, LANES), f32),
        kept=((SPAN, 2 * half_states, SUB, LANES), f32),
        part=((sides, SPAN * SUB, LANES), f32),
        dxr=((3, block, channels), bf16),
        art=((16, block), f32),
        aro=((16, block), bf16),
        ar=((16, length), bf16),
        smo=((SUB, width), f32),
        sm=((length // block, SUB, width), f32),
        gao=late["gao"],
        gs=late["gs"],
        pk=late["pk"],
        **scatter_buffers("dm", length, channels),
        **scatter_buffers("xv", block, width),
        **scatter_buffers("sh", channels, shared),
    )
    alias = dict(yn="xt", dyf="cotf", gg="wg", gu="wu", dyo="yno", dvp="v", aw="rs")
    alias.update(dz="q", dxb="k", drp="w", mxl="dm_os")
    shared_boxes = dict(gag="dg", gv="du")
    sems = [99, 99]
    if count:
        for name, (shape, kind) in summed.items():
            small = name in ("gs", "pk")
            used = count - 1, *(ring_rows(shape, kind, count) or ())
            if name in shared_boxes and 2 * used[0] * used[1] <= length and used[2] <= units:
                alias[name + "b"] = shared_boxes[name]
                continue
            scratch[name + "b"] = (direct_box if small else ring_box)(shape, kind, count)
        scratch.update(gss=summed["gs"], pks=summed["pk"])
        sems = [99 + 12 + 4 * (count - 1), 99 + 12 * count + 4 * (count - 1)]
    bare = {name + "t": entry for name, entry in summed.items()}
    done = run_stage(
        functools.partial(body, count), arrays, outs, scratch, sems, 1, bare.items(), alias.items()
    )
    done.dims = dims
    done.summed = bool(count)
    return done


def body_f(dims, shared, m):
    wide = ((m.gd, m.gdt), (m.gg, m.ggt), (m.gu, m.gut), (m.gao, m.gaot), (m.gag, m.gagt))
    wide += ((m.gv, m.gvt), (m.gs, m.gst))
    m.load(m.out, m.gt, m.gd, m.gg, m.gu, m.gao, m.gag, m.gv, m.gs, m.pk)
    for source, target in ((m.out, m.outt), (m.gt, m.gtt)):
        m.need(source)
        target[...] = source[...]
        m.flush(target)
    for source, target in wide:
        m.need(source)
        rows = source.shape[0] // 2
        for n in range(2):

            def part(i, _):
                piece = pl.ds(pl.multiple_of(n * rows + i * 16, 16), 16)
                target[piece, :] = source[piece, :].astype(f32)
                return 0

            lax.fori_loop(0, rows // 16, part, 0, unroll=4)
        m.flush(target)
    m.need(m.pk)
    for k, out in enumerate((m.e0, m.e1, m.e2, m.e3, m.e4, m.e5)):
        out[...] = m.pk[k * dims : (k + 1) * dims, :]
    top = 6 * dims
    channels = m.pk.shape[1]
    m.om[...] = m.pk[top : top + 1, :]
    per = m.norm.shape[1] // channels
    for n, out in enumerate((m.norm, m.rms)):
        for k in range(per):
            row = top + 1 + n * per + k
            out[:, k * channels : (k + 1) * channels] = m.pk[row : row + 1, :]
    for n, out in enumerate((m.qg, m.qb, m.kg)):
        row = top + 1 + 2 * per + n
        out[...] = m.pk[row : row + 1, :shared]
    m.flush(m.e0, m.e1, m.e2, m.e3, m.e4, m.e5, m.om, m.norm, m.rms, m.qg, m.qb, m.kg)
    m.close()


def finish(c, shared):
    sums = dict(gd=c.gdt, gg=c.ggt, gu=c.gut, gao=c.gaot, gag=c.gagt, gv=c.gvt, gs=c.gst, pk=c.pkt)
    if not c.summed:
        total = lax.psum([value.astype(f32) for value in sums.values()], "dp")
        sums = {name: v.astype(old.dtype) for (name, old), v in zip(sums.items(), total)}
    channels, width = sums["pk"].shape[1], sums["gd"].shape[1]
    outs = dict(
        e0=((c.dims, channels), f32),
        e1=((c.dims, channels), f32),
        e2=((c.dims, channels), f32),
        e3=((c.dims, channels), f32),
        e4=((c.dims, channels), f32),
        e5=((c.dims, channels), f32),
        om=((1, channels), f32),
        norm=((1, width), f32),
        rms=((1, width), f32),
        qg=((1, shared), f32),
        qb=((1, shared), f32),
        kg=((1, shared), f32),
    )
    for name, value in sums.items():
        if value is not sums["pk"]:
            outs[name + "t"] = (value.shape, f32)
    outs.update(outt=(c.out.shape, bf16), gtt=(c.gt.shape, bf16))
    f = run_stage(
        functools.partial(body_f, c.dims, shared),
        types.SimpleNamespace(out=c.out, gt=c.gt, **sums), outs, {}, (0, 0), None,
    )
    tables = [table.T for table in (f.e0, f.e1, f.e2, f.e3, f.e4, f.e5)]
    return (
        f.outt, f.gtt, f.norm[0], *tables, f.om[0], f.gst,
        f.qg[0], f.qb[0], f.kg[0], f.gagt, f.gvt, f.gaot, f.rms[0], f.ggt, f.gut, f.gdt,
    )


def on_device(
    tokens,
    segments,
    cotangent,
    timestep_norm_gain,
    ema_alpha,
    ema_delta,
    ema_theta,
    ema_beta,
    eta_real,
    eta_imag,
    ema_omega,
    w_shared,
    q_gain,
    q_bias,
    k_gain,
    w_attgate,
    w_value,
    w_attout,
    rms_gain,
    w_gate,
    w_up,
    w_down,
):
    block, width = tokens.shape
    length = segments.shape[1]
    channels, dims = ema_alpha.shape
    shared = w_shared.shape[1]
    values = w_value.shape[1]
    units = w_gate.shape[1]
    om = ema_omega[None]
    gain, rg = timestep_norm_gain[None], rms_gain[None]
    qg, qb, kg = q_gain[None], q_bias[None], k_gain[None]
    segr = segments
    done = run(
        types.SimpleNamespace(
            tok=tokens, cot=cotangent, wsh=w_shared, segr=segr, gain=gain,
            p0=ema_alpha.T, p1=ema_delta.T, p2=ema_theta.T,
            p3=ema_beta.T, p4=eta_real.T, p5=eta_imag.T, om=om, qg=qg, qb=qb, kg=kg,
            wag=w_attgate, wv=w_value, wo=w_attout, rg=rg, wg=w_gate, wu=w_up, wd=w_down,
        ),
        (length, width, block, channels, shared, values, units),
        lax.axis_size("dp"),
    )
    return finish(done, shared)


def solution(mesh):
    placed = (
        P(("dp", "tensor"), None),
        P("dp", None),
        P(("dp", "tensor"), None),
        P(),
        P("tensor", None),
        P("tensor", None),
        P("tensor", None),
        P("tensor", None),
        P("tensor", None),
        P("tensor", None),
        P("tensor"),
        P("tensor", None),
        P(),
        P(),
        P(),
        P(None, "tensor"),
        P(None, "tensor"),
        P("tensor", None),
        P(),
        P(None, "tensor"),
        P(None, "tensor"),
        P("tensor", None),
    )
    return jax.shard_map(
        on_device,
        mesh=mesh,
        in_specs=placed,
        out_specs=(
            P(("dp", "tensor"), None),
            P(("dp", "tensor"), None),
            P(),
            P("tensor", None),
            P("tensor", None),
            P("tensor", None),
            P("tensor", None),
            P("tensor", None),
            P("tensor", None),
            P("tensor"),
            P("tensor", None),
            P(),
            P(),
            P(),
            P(None, "tensor"),
            P(None, "tensor"),
            P("tensor", None),
            P(),
            P(None, "tensor"),
            P(None, "tensor"),
            P("tensor", None),
        ),
        check_vma=False,
    )
```

```python
import functools
import math
import types

import jax
import jax.numpy as jnp
from jax import lax
from jax.experimental import pallas as pl
from jax.experimental.pallas import tpu as pltpu
from jax.sharding import PartitionSpec as P

epsilon = 1e-05
masked_score = -1000000000.0
f32 = jnp.float32
bf16 = jnp.bfloat16
MESH = pl.DeviceIdType.MESH
LANES = 128
SUB = 8
SPAN = 64
MAX_DOC = 512
PACK_TAIL = 32
VMEM_BYTES = 62 * 2**20


def plain(left, right):
    return jnp.dot(left, right, preferred_element_type=f32)


def cross(left, right):
    return lax.dot_general(
        left, right, (((1,), (1,)), ((), ())), preferred_element_type=f32
    )


def inner(left, right):
    return lax.dot_general(
        left, right, (((0,), (0,)), ((), ())), preferred_element_type=f32
    )


def sigmoid(value):
    return 1.0 / (1.0 + jnp.exp(-value))


def at(index, size):
    return pl.ds(pl.multiple_of(index * size, size), size)


class Stage:
    def __init__(self, ins, outs, bare, scratch, alias, refs):
        self.pending = {}
        self.flushed = []
        count = len(ins)
        self.hbm_in = dict(zip(ins, refs[:count]))
        total = len(outs) + len(bare)
        self.hbm_out = dict(zip(list(outs) + list(bare), refs[count : count + total]))
        rest = refs[count + total :]
        names = list(ins) + list(outs) + list(scratch)
        self.refs = dict(zip(names, rest[: len(names)]))
        self.load_sem, self.flush_sem, self.send_sem, self.recv_sem = rest[len(names) :]
        self.order = {name: k for k, name in enumerate(ins)}
        self.out_order = {name: k for k, name in enumerate(self.hbm_out)}
        self.sends = self.receipts = 0
        self.sets = {}
        self.names = {id(ref): name for name, ref in self.refs.items()}
        for name, other in alias:
            self.refs[name] = self.refs[other]

    def __getitem__(self, name):
        return self.refs[name]

    def __getattr__(self, name):
        return self.refs[name]

    def load(self, *refs):
        for name in [self.names[id(ref)] for ref in refs]:
            copy = pltpu.make_async_copy(
                self.hbm_in[name], self.refs[name], self.load_sem.at[self.order[name]]
            )
            copy.start()
            self.pending[name] = copy

    def need(self, *refs):
        for name in [self.names[id(ref)] for ref in refs]:
            copy = self.pending.pop(name, None)
            if copy is not None:
                copy.wait()

    def flush(self, *refs):
        for name in [self.names[id(ref)] for ref in refs]:
            if name in self.hbm_out:
                self.store(self.refs[name], name)

    def store(self, source, name):
        copy = pltpu.make_async_copy(
            source, self.hbm_out[name], self.flush_sem.at[self.out_order[name]]
        )
        copy.start()
        self.flushed.append(copy)

    def close(self):
        assert self.sends <= self.send_sem.shape[0]
        assert self.receipts <= self.recv_sem.shape[0]
        for copy in self.flushed:
            copy.wait()


    def sems(self, count, sends=None, key=None):
        if key in self.sets:
            return self.sets[key]
        first = self.sends, self.receipts
        self.sends += count if sends is None else sends
        self.receipts += count
        if key:
            self.sets[key] = first
        return first

    def remote(self, source, target_ref, base, index, device, sent=None):
        return pltpu.make_async_remote_copy(
            src_ref=source,
            dst_ref=target_ref,
            send_sem=self.send_sem.at[base[0] + (index if sent is None else sent)],
            recv_sem=self.recv_sem.at[base[1] + index],
            device_id=device,
            device_id_type=MESH,
        )


def run_stage(body, ins, outs, scratch, sems, collective, bare=(), alias=()):
    ins = vars(ins)
    written = {**outs, **dict(bare)}

    def kernel(*refs):
        body(Stage(list(ins), list(outs), list(dict(bare)), list(scratch), alias, refs))

    buffers = [pltpu.VMEM(array.shape, array.dtype) for array in ins.values()]
    buffers += [pltpu.VMEM(shape, kind) for shape, kind in outs.values()]
    buffers += [pltpu.VMEM(shape, kind) for shape, kind in scratch.values()]
    results = pl.pallas_call(
        kernel,
        out_shape=tuple(jax.ShapeDtypeStruct(shape, kind) for shape, kind in written.values()),
        in_specs=[pl.BlockSpec(memory_space=pl.ANY)] * len(ins),
        out_specs=tuple(pl.BlockSpec(memory_space=pl.ANY) for _ in written),
        scratch_shapes=buffers
        + [
            pltpu.SemaphoreType.DMA((len(ins),)),
            pltpu.SemaphoreType.DMA((len(written),)),
            pltpu.SemaphoreType.DMA((max(sems[0], 1),)),
            pltpu.SemaphoreType.DMA((max(sems[1], 1),)),
        ],
        compiler_params=pltpu.CompilerParams(
            collective_id=collective,
            has_side_effects=collective is not None,
            vmem_limit_bytes=VMEM_BYTES,
        ),
    )(*ins.values())
    return types.SimpleNamespace(**dict(zip(written, results)))


class Group:
    def __init__(self):
        self.me = lax.axis_index("tensor")
        chip = self.me // 2
        core = self.me % 2
        self.sib = chip * 2 + (1 - core)
        self.opp = (1 - chip) * 2 + core
        self.diag = (1 - chip) * 2 + (1 - core)

    def greet(self, more=()):
        barrier = pltpu.get_barrier_semaphore()
        for device in more:
            pl.semaphore_signal(barrier, inc=1, device_id={"dp": device}, device_id_type=MESH)
        for device in (self.sib, self.opp, self.diag):
            pl.semaphore_signal(barrier, inc=1, device_id={"tensor": device}, device_id_type=MESH)
        pl.semaphore_wait(barrier, 3 + len(more))


class Gather:
    def __init__(self, stage, group, source, place, pieces, key=None):
        self.g = group
        self.pieces = pieces
        base = stage.sems(3 * pieces, key=key)
        opp = {"tensor": group.opp}
        sib = {"tensor": group.sib}
        self.to_opp = [
            stage.remote(source(s), place(group.me, s), base, s, opp) for s in range(pieces)
        ]
        self.to_sib = [
            stage.remote(source(s), place(group.me, s), base, pieces + s, sib)
            for s in range(pieces)
        ]
        self.passed = [
            stage.remote(place(group.opp, s), place(group.opp, s), base, 2 * pieces + s, sib)
            for s in range(pieces)
        ]

    def send(self, s):
        self.to_opp[s].start()
        self.to_sib[s].start()

    def forward(self, s):
        self.to_opp[s].wait_recv()
        self.passed[s].start()

    def near(self):
        for s in range(self.pieces):
            self.to_sib[s].wait_recv()

    def far(self):
        for s in range(self.pieces):
            self.passed[s].wait_recv()

    def close(self):
        for copy in self.to_opp + self.to_sib + self.passed:
            copy.wait_send()


class Scatter:
    def __init__(self, stage, group, name, pieces, order=None):
        self.order = list(order or range(pieces))
        self.out_diag = stage[name + "_od"]
        self.out_sib = stage[name + "_os"]
        self.out_opp = stage[name + "_oo"]
        self.in_opp = stage[name + "_io"]
        self.in_own = stage[name + "_iw"]
        self.in_far = stage[name + "_if"]
        self.rows = self.out_diag.shape[0] // pieces
        base = stage.sems(3 * pieces, key=name)

        def copies(source, target, first, device):
            return [
                stage.remote(
                    source.at[self.part(s)], target.at[self.part(s)], base, first + s, {"tensor": device}
                )
                for s in range(pieces)
            ]

        self.first = copies(self.out_diag, self.in_opp, 0, group.sib)
        self.second = copies(self.out_sib, self.in_own, pieces, group.sib)
        self.across = copies(self.out_opp, self.in_far, 2 * pieces, group.opp)

    def part(self, s):
        return pl.ds(s * self.rows, self.rows)

    def put_diag(self, value, only=None):
        for s in self.order if only is None else [only]:
            self.out_diag[self.part(s), :] = value(s).astype(bf16)
            self.first[s].start()

    def put_opp(self, value, only=None):
        for s in self.order if only is None else [only]:
            mine = value(s)
            self.first[s].wait_recv()
            total = mine + self.in_opp[self.part(s), :].astype(f32)
            self.out_opp[self.part(s), :] = total.astype(bf16)
            self.across[s].start()

    def put_sib(self, value):
        self.fill_sib(value)
        self.send_sib()

    def fill_sib(self, value):
        for s in self.order:
            self.out_sib[self.part(s), :] = value(s).astype(bf16)

    def send_sib(self):
        for s in self.order:
            self.second[s].start()

    def take(self, s, own):
        self.second[s].wait_recv()
        near = own + self.in_own[self.part(s), :].astype(f32)
        self.across[s].wait_recv()
        return near + self.in_far[self.part(s), :].astype(f32)

    def close(self):
        for copy in self.first + self.second + self.across:
            copy.wait_send()


def pieces_of(value, count):
    rows = value.shape[0] // count
    return lambda s: value[s * rows : (s + 1) * rows]


def scatter_buffers(name, rows, width):
    return {
        name + tail: ((rows, width), bf16) for tail in ("_od", "_os", "_oo", "_io", "_iw", "_if")
    }


def ring_seats(count):
    index = lax.axis_index("dp")
    place = jnp.where(index % 2 == 0, index // 2, count - 1 - index // 2)

    def seat(p):
        p = lax.rem(p + 2 * count, count)
        return jnp.where(2 * p < count, 2 * p, 2 * (count - 1 - p) + 1)

    return place, seat


def ring_rows(shape, kind, count):
    tile = 16 if kind == bf16 else SUB
    if shape[0] % (2 * count * tile) == 0:
        return shape[0] // (2 * count), shape[1]
    if shape[0] % (count * tile) == 0 and shape[1] % (2 * LANES) == 0:
        return shape[0] // count, shape[1] // 2
    return None


class Ring:
    def __init__(self, m, count, items):
        self.m = m
        self.count = count
        self.items = items
        self.place, self.seat = ring_seats(count)
        self.steps = 2 * (count - 1)
        self.ahead = 0
        self.base = m.sems(len(items) * 2 * count, len(items) * 2)
        self.step = 0

    def neighbours(self):
        return self.seat(self.place - 1), self.seat(self.place + 1)

    def view(self, ref, chunk, way):
        shape = ref.shape
        rows, columns = ring_rows(shape, ref.dtype, self.count)
        chunk = lax.rem(chunk + 2 * self.count, self.count)
        if columns == shape[1]:
            return ref.at[pl.ds(pl.multiple_of((2 * chunk + way) * rows, rows), rows), :]
        return ref.at[
            pl.ds(pl.multiple_of(chunk * rows, rows), rows), pl.ds(way * columns, columns)
        ]

    def slot(self, item, way, step):
        own, box, _ = self.items[item]
        if len(box.shape) == 4:
            return box.at[way, step]
        rows, columns = ring_rows(own.shape, own.dtype, self.count)
        first = (way * (self.count - 1) + step) * rows
        return box.at[pl.ds(first, rows), pl.ds(0, columns)]

    def copy(self, item, way, step):
        own = self.items[item][0]
        sign = 1 - 2 * way
        last = self.count - 1
        place = 2 * item + way
        index = place * self.count + step % self.count
        if step < last:
            source = self.view(own, self.place, way) if step == 0 else self.slot(item, way, step - 1)
            target = self.slot(item, way, step)
        else:
            source = self.view(own, self.place + sign - sign * (step - last), way)
            target = source
        device = {"dp": self.seat(self.place + sign)}
        return self.m.remote(source, target, self.base, index, device, place)

    def start(self, item, way, step):
        self.copy(item, way, step).start()

    def begin(self):
        for item in range(len(self.items)):
            for way in range(2):
                self.start(item, way, 0)

    def tick(self):
        last = self.count - 1
        step = self.step
        self.step = step + 1
        for item, (own, _, name) in enumerate(self.items):
            for way in range(2):
                sign = 1 - 2 * way
                self.copy(item, way, step).wait_recv()
                self.copy(item, way, step).wait_send()
                if step < last:
                    chunk = self.view(own, self.place - sign * (step + 1), way)
                    box = self.slot(item, way, step)
                    value = box[...].astype(f32) + chunk[...].astype(f32)
                    if step < last - 1:
                        box[...] = value.astype(own.dtype)
                    else:
                        chunk[...] = value.astype(own.dtype)
                if step + 1 < self.steps:
                    self.start(item, way, step + 1)
                if step >= last - 1:
                    self.keep(own, name, self.place + sign - sign * (step + 1 - last), way)
        return step + 1 == self.steps

    def keep(self, own, name, chunk, way):
        out = self.m.hbm_out[name]
        sem = self.m.flush_sem.at[self.m.out_order[name]]
        pltpu.make_async_copy(self.view(own, chunk, way), self.view(out, chunk, way), sem).start()

    def close(self):
        for own, _, name in self.items:
            sem = self.m.flush_sem.at[self.m.out_order[name]]
            pltpu.make_async_copy(own, self.m.hbm_out[name], sem).wait()


class Direct:
    def __init__(self, m, count, items):
        self.m = m
        self.count = count
        self.items = items
        self.me = lax.axis_index("dp")
        self.base = m.sems(2 * len(items) * (count - 1))
        self.step = 0
        self.steps = 2
        self.ahead = 2 * count

    def share(self, ref, index):
        return ref.at[at(index, ref.shape[0] // self.count), :]

    def copies(self, step):
        made = []
        for item, (own, box, total, _) in enumerate(self.items):
            for r in range(1, self.count):
                there = lax.rem(self.me + r, self.count)
                index = (2 * item + step) * (self.count - 1) + r - 1
                if step == 0:
                    source, target = self.share(own, there), box.at[r - 1]
                else:
                    source = target = self.share(total, self.me)
                made.append(self.m.remote(source, target, self.base, index, {"dp": there}))
        return made

    def begin(self):
        for copy in self.copies(0):
            copy.start()

    def tick(self):
        for copy in self.copies(self.step):
            copy.wait_recv()
        if self.step == 0:
            for own, box, total, _ in self.items:
                value = self.share(own, self.me)[...].astype(f32)
                for r in range(self.count - 1):
                    value = value + box[r].astype(f32)
                self.share(total, self.me)[...] = value.astype(total.dtype)
            for copy in self.copies(1):
                copy.start()
        self.step += 1
        return self.step == 2

    def close(self):
        for copy in self.copies(0) + self.copies(1):
            copy.wait_send()
        for _, _, total, name in self.items:
            self.m.store(total, name)


class Turns:
    def __init__(self):
        self.waiting = []
        self.rings = []
        self.recent = []

    def begin(self, ring):
        ring.begin()
        self.waiting.append(ring)
        self.rings.append(ring)
        self.recent.append(ring)

    def tick(self, times=1):
        for _ in range(times):
            if self.waiting:
                recent = self.recent[-1:] if len(self.waiting) > 1 else []
                others = [ring for ring in self.waiting if ring not in recent]
                ring = max(others, key=lambda one: one.ahead + one.steps - one.step)
                self.recent.append(ring)
                if ring.tick():
                    self.waiting.remove(ring)

    def close(self):
        while self.waiting:
            self.tick()
        for ring in self.rings:
            ring.close()


def ring_box(shape, kind, count):
    rows, columns = ring_rows(shape, kind, count)
    return ((2, count - 1, rows, columns), kind)


def direct_box(shape, kind, count):
    return ((count - 1, shape[0] // count, shape[1]), kind)


def ring_fits(shapes, count):
    return (
        count > 1
        and count % 2 == 0
        and all(ring_rows(shape, kind, count) for shape, kind in shapes)
    )


def groups(array):
    halves = array.shape[0] // SUB
    sides = array.shape[1] // LANES
    return [
        array[SUB * s : SUB * s + SUB, LANES * l : LANES * l + LANES]
        for s in range(halves)
        for l in range(sides)
    ]


def spread_row(ref, index):
    return jnp.broadcast_to(ref[index], (SUB, LANES))


def advance(state, coefs, keep, signals, sides):
    root_real, root_imag = coefs
    half = len(state) // 2
    kept = [value * keep for value in state]
    fresh = [None] * len(state)
    for g in range(half):
        a_real, a_imag = kept[g], kept[half + g]
        fresh[g] = (root_real[g] * a_real - root_imag[g] * a_imag) + signals[g % sides]
        fresh[half + g] = root_real[g] * a_imag + root_imag[g] * a_real
    return kept, fresh


def filter_forward(m, first, count, state):
    sides = m.xl.shape[0]
    tables = m.tab
    root_real, root_imag = groups(tables[0]), groups(tables[1])
    out_real, out_imag = groups(tables[2]), groups(tables[3])
    half = len(root_real)
    unroll = 16

    def chunk(ch, state):
        for g in range(2 * half):
            m.st[ch, g] = state[g]

        def steps(i, state):
            state = list(state)
            for j in range(unroll):
                t = ch * SPAN + i * unroll + j
                keep = spread_row(m.kf, (pl.ds(t, 1), slice(None)))
                signals = [
                    spread_row(m.xl, (l, pl.ds(t, 1), slice(None))) for l in range(sides)
                ]
                _, state = advance(state, (root_real, root_imag), keep, signals, sides)
                for l in range(sides):
                    total = None
                    for g in range(l, half, sides):
                        term = out_real[g] * state[g] - out_imag[g] * state[half + g]
                        total = term if total is None else total + term
                    m.part[l, pl.ds(pl.multiple_of((i * unroll + j) * SUB, SUB), SUB), :] = total
            return tuple(state)

        state = lax.fori_loop(0, SPAN // unroll, steps, state)
        rows = at(ch, SPAN)
        for l in range(sides):
            lanes = slice(LANES * l, LANES * l + LANES)
            value = m.om[:, lanes] * m.xl[l, rows, :]
            for s in range(SUB):
                value = value + m.part[l, pl.ds(s, SPAN, stride=SUB), :]
            gate = sigmoid(value)
            m.mxl[rows, lanes] = (value * gate).astype(bf16)
            m.se[rows, lanes] = (gate * (1.0 + value * (1.0 - gate))).astype(bf16)
        return state

    return lax.fori_loop(first, first + count, chunk, state)


def window_mask(m, first_row, rows, first_key, keys):
    here = m.segb[pl.ds(pl.multiple_of(first_row + SUB, SUB), rows), :][:, :1]
    same = here == m.segr[:, pl.ds(pl.multiple_of(first_key, LANES), keys)].astype(f32)
    row = first_row + lax.broadcasted_iota(jnp.int32, (rows, keys), 0)
    key = first_key + lax.broadcasted_iota(jnp.int32, (rows, keys), 1)
    return same & (row >= key)


def window_of(index, block, length):
    back = -(-MAX_DOC // block)
    keys = min((back + 1) * block, length)
    first = jnp.maximum(index - back, 0) * block
    first = jnp.minimum(first, length - keys)
    return pl.multiple_of(first, LANES), keys


def keeping(m):
    length = m.segr.shape[1]
    m.segb[:SUB, :] = jnp.full((SUB, LANES), -1.0, f32)
    for k in range(length // LANES):
        row = m.segr[:, k * LANES : (k + 1) * LANES].astype(f32)
        m.segb[SUB + k * LANES : SUB + (k + 1) * LANES, :] = jnp.broadcast_to(row, (LANES, LANES)).T
    for k in range(length // LANES):
        now = m.segb[SUB + k * LANES : SUB + (k + 1) * LANES, :]
        before = m.segb[SUB - 1 + k * LANES : SUB - 1 + (k + 1) * LANES, :]
        m.kf[k * LANES : (k + 1) * LANES, :] = jnp.where(now == before, 1.0, 0.0)
    m.kf[length:, :] = jnp.zeros((SUB, LANES), f32)


def filter_tables(m):
    alpha, delta, theta, beta, e_re, e_im = (
        ref[...] for ref in (m.p0, m.p1, m.p2, m.p3, m.p4, m.p5)
    )
    magnitude = 1.0 - alpha * delta
    cosine, sine = jnp.cos(theta), jnp.sin(theta)
    scaled = alpha * beta
    entries = (
        magnitude * cosine, magnitude * sine, scaled * e_re, scaled * e_im,
        cosine, sine, alpha, delta, beta, e_re, e_im,
    )
    for k, entry in enumerate(entries):
        m.tab[k] = entry


def forward_attention(m, g):
    length, width = m.xt.shape
    block = m.tok.shape[0]
    blocks = length // block
    channels = m.mxl.shape[1]
    sides = channels // LANES
    own = at(g.me, block)
    half = block // 2
    tokens = Gather(
        m, g,
        lambda s: m.tok.at[pl.ds(s * half, half), :],
        lambda j, s: m.xt.at[pl.ds(pl.multiple_of(j * block + s * half, half), half), :],
        2, "rows",
    )
    shared = Gather(m, g, lambda s: m.wsh, lambda j, s: m.wsf.at[at(j, channels), :], 1)
    pieces = 8
    rows_piece = length // pieces
    mixed = Gather(
        m, g,
        lambda s: m.mxl.at[pl.ds(s * rows_piece, rows_piece), :],
        lambda j, s: m.mx.at[pl.ds(s * rows_piece, rows_piece), at(j, channels)],
        pieces,
    )
    cots = Gather(
        m, g,
        lambda s: m.cot.at[pl.ds(s * half, half), :],
        lambda j, s: m.cotf.at[pl.ds(pl.multiple_of(j * block + s * half, half), half), :],
        2,
    )
    normed = Gather(
        m, g,
        lambda s: m.yno.at[pl.ds(s * half, half), :],
        lambda j, s: m.yn.at[pl.ds(pl.multiple_of(j * block + s * half, half), half), :],
        2, "rows",
    )
    branch = Scatter(m, g, "xv", 2)

    m.need(m.tok, m.wsh)
    tokens.send(0)
    tokens.send(1)
    shared.send(0)
    m.need(m.cot)
    cots.send(0)
    m.xt[own, :] = m.tok[...]
    m.wsf[at(g.me, channels), :] = m.wsh[...]
    m.need(m.segr, m.p0, m.p1, m.p2, m.p3, m.p4, m.p5, m.gain, m.om)
    keeping(m)
    filter_tables(m)

    lane = lax.broadcasted_iota(jnp.int32, (SPAN, LANES), 1)

    def sums(j):
        def part(i, _):
            rows = pl.ds(pl.multiple_of(j * block + i * SPAN, SPAN), SPAN)
            one = jnp.zeros((SPAN, LANES), f32)
            two = jnp.zeros((SPAN, LANES), f32)
            for l in range(width // LANES):
                x = m.xt[rows, LANES * l : LANES * l + LANES].astype(f32)
                one = one + x
                two = two + x * x
            picked = jnp.where(lane == 6, 1.0, 0.0)
            for k, total in ((0, one), (3, two)):
                rest = jnp.sum(total, axis=1, keepdims=True)
                for n in range(3):
                    top = rest.astype(bf16).astype(f32)
                    picked = jnp.where(lane == k + n, top, picked)
                    rest = rest - top
            m.sums[rows, :] = picked.astype(bf16)
            return 0

        lax.fori_loop(0, block // SPAN, part, 0)

    sums(g.me)
    tokens.near()
    sums(g.sib)
    tokens.forward(0)
    tokens.forward(1)
    sums(g.opp)
    tokens.far()
    sums(g.diag)

    lane_wide = lax.broadcasted_iota(jnp.int32, (block, LANES), 1)

    def statistics(i, _):
        first, keys = window_of(i, block, length)
        seen = window_mask(m, i * block, block, first, keys).astype(bf16)
        got = plain(seen, m.sums[pl.ds(first, keys), :])
        pick = lambda low, high: jnp.sum(
            jnp.where((lane_wide >= low) & (lane_wide < high), got, 0.0), axis=1, keepdims=True
        )
        total = pick(6, 7) * width
        mean = pick(0, 3) / total
        var = pick(3, 6) / total - mean * mean
        rows = at(i, block)
        m.mean[rows, :] = jnp.broadcast_to(mean, (block, LANES))
        m.rstd[rows, :] = jnp.broadcast_to(lax.rsqrt(var + epsilon), (block, LANES))

        @pl.when(i == g.me)
        def _():
            m.so[0] = m.mean[rows, :]
            m.so[1] = m.rstd[rows, :]
            m.so[2] = jnp.broadcast_to(total, (block, LANES))

        return 0

    lax.fori_loop(0, blocks, statistics, 0)

    def normalise(i, _):
        rows = at(i, SPAN)
        mean, rstd = m.mean[rows, :], m.rstd[rows, :]
        for l in range(width // LANES):
            lanes = slice(LANES * l, LANES * l + LANES)
            x = m.xt[rows, lanes].astype(f32)
            m.xn[rows, lanes] = ((x - mean) * rstd * m.gain[:, lanes]).astype(bf16)
        for l in range(sides):
            lanes = pl.ds(pl.multiple_of(g.me * channels + LANES * l, LANES), LANES)
            x = m.xt[rows, lanes].astype(f32)
            m.xl[l, rows, :] = (x - mean) * rstd * m.gain[:, lanes]
        return 0

    lax.fori_loop(0, length // SPAN, normalise, 0)
    tokens.close()

    zero = jnp.zeros((SUB, LANES), f32)
    state = tuple(zero for _ in range(m.st.shape[1]))
    per = length // SPAN // pieces
    for p in range(pieces):
        state = filter_forward(m, p * per, per, state)
        mixed.send(p)
        if p >= 2:
            mixed.forward(p - 2)
    cots.send(1)
    for i in range(pieces):
        m.mx[pl.ds(i * rows_piece, rows_piece), at(g.me, channels)] = m.mxl[
            pl.ds(i * rows_piece, rows_piece), :
        ]
    m.cotf[own, :] = m.cot[...]
    m.need(m.wv)

    def values(i, _):
        rows = at(i, block)
        pre = plain(m.xn[rows, :], m.wv[...])
        gate = sigmoid(pre)
        m.v[rows, :] = (pre * gate).astype(bf16)
        m.sv[rows, :] = (gate * (1.0 + pre * (1.0 - gate))).astype(bf16)
        return 0

    lax.fori_loop(0, blocks, values, 0)
    for p in range(max(pieces - 2, 0), pieces):
        mixed.forward(p)
    shared.forward(0)
    shared.near()
    shared.far()
    mixed.near()
    mixed.far()
    m.need(m.qg, m.qb, m.kg, m.wag, m.wo, m.rg)

    def project(i, _):
        rows = at(i, block)
        z = plain(m.mx[rows, :], m.wsf[...])
        m.z[rows, :] = z.astype(bf16)
        m.q[rows, :] = (z * m.qg[...] + m.qb[...]).astype(bf16)
        m.k[rows, :] = (z * m.kg[...]).astype(bf16)
        return 0

    lax.fori_loop(0, blocks, project, 0)
    scale = 1.0 / math.sqrt(m.q.shape[1])

    def attend(i, part, count):
        size = block // count
        start = pl.multiple_of(i * block + part * size, size)
        rows = pl.ds(start, size)
        first, keys = window_of(i, block, length)
        window = pl.ds(first, keys)
        scores = cross(m.q[rows, :], m.k[window, :]) * scale
        scores = jnp.where(window_mask(m, start, size, first, keys), scores, masked_score)
        expo = jnp.exp(scores - jnp.max(scores, axis=1, keepdims=True))
        prob = (expo / jnp.sum(expo, axis=1, keepdims=True)).astype(bf16)
        m.p[i, pl.ds(part * size, size), :] = prob
        attended = plain(prob, m.v[window, :])
        pre = plain(m.mx[rows, :], m.wag[...])
        gate = sigmoid(pre)
        swish = pre * gate
        m.r[rows, :] = swish.astype(bf16)
        m.os[rows, :] = (attended * (gate * (1.0 + pre * (1.0 - gate)))).astype(bf16)
        m.w[rows, :] = (attended * swish).astype(bf16)
        return plain(m.w[rows, :], m.wo[...])

    for n in range(2):
        branch.put_diag(lambda s: attend(g.diag, s, 2), n)
        branch.put_opp(lambda s: attend(g.opp, s, 2), n)
    cots.forward(0)
    branch.put_sib(pieces_of(attend(g.sib, 0, 1), 2))
    cots.forward(1)
    m.bp[...] = attend(g.me, 0, 1)
    for s in range(2):
        piece = pl.ds(s * half, half)
        y = branch.take(s, m.bp[piece, :]) + m.tok[piece, :].astype(f32)
        m.y[piece, :] = y
        rms = lax.rsqrt(jnp.mean(y * y, axis=1, keepdims=True) + epsilon)
        m.rs[piece, :] = jnp.broadcast_to(rms, (half, LANES))
        m.yno[piece, :] = (y * rms * m.rg[...]).astype(bf16)
        normed.send(s)
    m.yn[own, :] = m.yno[...]
    for moved in (shared, mixed, branch):
        moved.close()
    return cots, normed


def transposed_product(left, right, out, step):
    def part(i, _):
        columns = at(i, step)
        out[columns, :] = inner(left[:, columns], right[...]).astype(bf16)
        return 0

    lax.fori_loop(0, left.shape[1] // step, part, 0)


def half_product(left, right, tokens, step, keep, done=None):
    def part(i, _):
        rows = at(i, step)
        value = inner(left[tokens, rows], right[tokens, :])
        keep(rows, value if done is None else value + done(rows))
        return 0

    lax.fori_loop(0, left.shape[1] // step, part, 0)


def strips(refs, width):
    size = refs[0].shape[1]
    spans = [(k * size, min((k + 1) * size, width)) for k in range(-(-width // size))]

    def store(rows, value):
        for ref, (low, high) in zip(refs, spans):
            ref[rows, : high - low] = value[:, low:high].astype(bf16)

    def load(rows):
        parts = [ref[rows, : high - low].astype(f32) for ref, (low, high) in zip(refs, spans)]
        return jnp.concatenate(parts, axis=1)

    return store, load


def feed_forward(m, g, cots, normed, turns, begin):
    length, width = m.yn.shape
    block = m.y.shape[0]
    half = block // 2
    grads = Scatter(m, g, "xv", 2)
    back = Gather(
        m, g,
        lambda s: m.dyo.at[pl.ds(s * half, half), :],
        lambda j, s: m.dyf.at[pl.ds(pl.multiple_of(j * block + s * half, half), half), :],
        2, "rows",
    )
    m.need(m.wg, m.wu, m.wd)

    def lead(j):
        rows = at(j, block)
        m.dg[rows, :] = cross(m.cotf[rows, :], m.wd[...]).astype(bf16)

    def feed(j):
        rows = at(j, block)
        low = m.yn[rows, :]
        gate = plain(low, m.wg[...])
        up = plain(low, m.wu[...])
        d_act = m.dg[rows, :].astype(f32)
        sig = sigmoid(gate)
        swish = gate * sig
        m.act[rows, :] = (swish * up).astype(bf16)
        m.dg[rows, :] = (d_act * up * (sig * (1.0 + gate * (1.0 - sig)))).astype(bf16)
        m.du[rows, :] = (d_act * swish).astype(bf16)
        return cross(m.dg[rows, :], m.wg[...]) + cross(m.du[rows, :], m.wu[...])

    lead(g.me)
    m.bp[...] = feed(g.me)
    cots.near()
    normed.near()
    lead(g.sib)
    grads.fill_sib(pieces_of(feed(g.sib), 2))
    normed.forward(0)
    cots.far()
    cots.close()
    lead(g.diag)
    lead(g.opp)
    chip = 2 * block
    near = at(g.me // 2, chip)
    far = at(1 - g.me // 2, chip)
    units = m.act.shape[1]

    def keep(ref):
        def store(rows, value):
            ref[rows, :] = value.astype(bf16)

        return store

    gate_store, gate_load = strips((m.dm_od, m.dm_os, m.dm_oo), units)
    up_store, up_load = strips((m.dm_io, m.dm_iw, m.dm_if), units)
    half_product(m.yn, m.dg, near, 2 * LANES, gate_store)
    half_product(m.yn, m.du, near, 2 * LANES, up_store)
    half_product(m.act, m.cotf, near, LANES, keep(m.gd))
    normed.forward(1)
    normed.far()
    grads.put_diag(pieces_of(feed(g.diag), 2))
    m.dy[...] = feed(g.opp)
    half_product(m.act, m.cotf, far, LANES, keep(m.gd), lambda rows: m.gd[rows, :].astype(f32))
    begin(0)
    grads.send_sib()
    grads.put_opp(lambda s: m.dy[pl.ds(s * half, half), :])
    half_product(m.yn, m.dg, far, 2 * LANES, keep(m.gg), gate_load)
    half_product(m.yn, m.du, far, 2 * LANES, keep(m.gu), up_load)
    begin(1)
    turns.tick(3)
    normed.close()
    m.need(m.y, m.rs, m.cot, m.rg)
    gain_sum = jnp.zeros((1, width), f32)
    for s in range(2):
        piece = pl.ds(s * half, half)
        d_yn = grads.take(s, m.bp[piece, :])
        rms = m.rs[piece, :][:, :1]
        hat = m.y[piece, :] * rms
        gain_sum = gain_sum + jnp.sum(d_yn * hat, axis=0, keepdims=True)
        d_hat = d_yn * m.rg[...]
        pull = d_hat - hat * jnp.mean(d_hat * hat, axis=1, keepdims=True)
        dy = m.cot[piece, :].astype(f32) + rms * pull
        m.dy[piece, :] = dy
        m.dyo[piece, :] = dy.astype(bf16)
        back.send(s)
    m.gr[...] = gain_sum
    m.dyf[at(g.me, block), :] = m.dyo[...]
    grads.close()
    return back


def filter_backward(m, last, count, gamma):
    sides = m.xl.shape[0]
    tables = m.tab
    root_real, root_imag = groups(tables[0]), groups(tables[1])
    out_real, out_imag = groups(tables[2]), groups(tables[3])
    half = len(root_real)
    unroll = 8

    def chunk(step, gamma):
        ch = last - step

        def again(i, state):
            state = list(state)
            for j in range(unroll):
                local = i * unroll + j
                t = ch * SPAN + local
                keep = spread_row(m.kf, (pl.ds(t, 1), slice(None)))
                signals = [
                    spread_row(m.xl, (l, pl.ds(t, 1), slice(None))) for l in range(sides)
                ]
                kept, state = advance(state, (root_real, root_imag), keep, signals, sides)
                for g in range(2 * half):
                    m.kept[local, g] = kept[g]
            return tuple(state)

        lax.fori_loop(0, SPAN // unroll, again, tuple(m.st[ch, g] for g in range(2 * half)))

        def reverse(i, carry):
            gamma, sums = list(carry[: 2 * half]), list(carry[2 * half :])
            for j in range(unroll):
                local = SPAN - 1 - (i * unroll + j)
                t = ch * SPAN + local
                keep = spread_row(m.kf, (pl.ds(t + 1, 1), slice(None)))
                signals = [
                    spread_row(m.dq, (l, pl.ds(t, 1), slice(None))) for l in range(sides)
                ]
                _, gamma = advance(gamma, (root_real, root_imag), keep, signals, sides)
                for l in range(sides):
                    total = None
                    for g in range(l, half, sides):
                        g_real, g_imag = gamma[g], gamma[half + g]
                        a_real, a_imag = m.kept[local, g], m.kept[local, half + g]
                        term = out_real[g] * g_real - out_imag[g] * g_imag
                        total = term if total is None else total + term
                        sums[g] = sums[g] + (g_real * a_real - g_imag * a_imag)
                        sums[half + g] = sums[half + g] + (g_real * a_imag + g_imag * a_real)
                        sums[2 * half + g] = sums[2 * half + g] + signals[l] * a_real
                        sums[3 * half + g] = sums[3 * half + g] + signals[l] * a_imag
                    m.part[l, pl.ds(pl.multiple_of(local * SUB, SUB), SUB), :] = total
            return tuple(gamma) + tuple(sums)

        start = tuple(gamma) + tuple(m.acc[g] for g in range(4 * half))
        done = lax.fori_loop(0, SPAN // unroll, reverse, start)
        for g in range(4 * half):
            m.acc[g] = done[2 * half + g]
        rows = at(ch, SPAN)
        for l in range(sides):
            lanes = slice(LANES * l, LANES * l + LANES)
            signal = m.dq[l, rows, :]
            value = m.om[:, lanes] * signal
            for s in range(SUB):
                value = value + m.part[l, pl.ds(s, SPAN, stride=SUB), :]
            m.dxb[rows, lanes] = value.astype(bf16)
            m.go[:, lanes] = m.go[:, lanes] + jnp.sum(
                signal * m.xl[l, rows, :], axis=0, keepdims=True
            )
        return done[: 2 * half]

    return lax.fori_loop(0, count, chunk, gamma)


def filter_gradients(m):
    sides = m.xl.shape[0]
    half = m.acc.shape[0] // 4
    dims = m.tab.shape[1]
    for g in range(half):
        s, l = g // sides, g % sides
        rows = slice(SUB * s, SUB * s + SUB)
        lanes = slice(LANES * l, LANES * l + LANES)
        q_re, q_im, c_re, c_im, cosine, sine, alpha, delta, beta, e_re, e_im = (
            m.tab[k, rows, lanes] for k in range(11)
        )
        lag_re, lag_im, sum_re, sum_im = (m.acc[k * half + g] for k in range(4))
        f_re = q_re * sum_re - q_im * sum_im + m.go[:, lanes]
        f_im = q_re * sum_im + q_im * sum_re
        scaled = alpha * beta
        d_scaled = e_re * f_re - e_im * f_im
        w_re = c_re * lag_re - c_im * lag_im
        w_im = c_re * lag_im + c_im * lag_re
        d_mag = w_re * cosine - w_im * sine
        m.pk[0 * dims + SUB * s : 0 * dims + SUB * s + SUB, lanes] = beta * d_scaled - delta * d_mag
        m.pk[1 * dims + SUB * s : 1 * dims + SUB * s + SUB, lanes] = -alpha * d_mag
        m.pk[2 * dims + SUB * s : 2 * dims + SUB * s + SUB, lanes] = -(w_re * q_im + w_im * q_re)
        m.pk[3 * dims + SUB * s : 3 * dims + SUB * s + SUB, lanes] = alpha * d_scaled
        m.pk[4 * dims + SUB * s : 4 * dims + SUB * s + SUB, lanes] = scaled * f_re
        m.pk[5 * dims + SUB * s : 5 * dims + SUB * s + SUB, lanes] = -scaled * f_im


def backward_attention(m, g, back, turns, begin):
    length, width = m.mx.shape
    block = m.tok.shape[0]
    blocks = length // block
    half = block // 2
    channels = m.se.shape[1]
    shared = m.q.shape[1]
    sides = channels // LANES
    fed = Scatter(m, g, "xv", 2)
    pieces = 4
    dm = Scatter(m, g, "dm", pieces, range(pieces - 1, -1, -1))
    sh = Scatter(m, g, "sh", 1)
    others = (g.sib, g.opp, g.diag)
    base = m.sems(9)
    parts = [
        m.remote(m.dxb.at[at(dev, block), :], m.dxr.at[k], base, k, {"tensor": dev})
        for k, dev in enumerate(others)
    ]
    small = [
        m.remote(m.smo, m.sm.at[g.me], base, 3 + k, {"tensor": dev})
        for k, dev in enumerate(others)
    ]
    tails = [
        m.remote(m.aro, m.ar.at[:, at(g.me, block)], base, 6 + k, {"tensor": dev})
        for k, dev in enumerate(others)
    ]

    scale = 1.0 / math.sqrt(shared)
    m.dk[...] = jnp.zeros(m.dk.shape, f32)
    m.dv[...] = jnp.zeros(m.dv.shape, f32)
    turns.tick(2)
    back.forward(0)
    turns.tick(2)
    back.forward(1)
    back.near()
    back.far()
    share = lambda j: plain(m.act[at(j, block), :], m.wd[...])
    fed.put_diag(pieces_of(share(g.diag), 2))
    turns.tick()
    fed.put_opp(pieces_of(share(g.opp), 2))
    turns.tick()
    fed.put_sib(pieces_of(share(g.sib), 2))
    m.bp[...] = share(g.me)
    m.need(m.w, m.wo, m.r, m.os, m.v, m.p, m.k, m.q)
    transposed_product(m.w, m.dyf, m.gao, 2 * LANES)
    turns.tick()

    def attend(i, _):
        rows = at(i, block)
        first, keys = window_of(i, block, length)
        window = pl.ds(first, keys)
        d_w = cross(m.dyf[rows, :], m.wo[...])
        d_o = (d_w * m.r[rows, :].astype(f32)).astype(bf16)
        m.drp[rows, :] = (d_w * m.os[rows, :].astype(f32)).astype(bf16)
        prob_low = m.p[i]
        prob = prob_low.astype(f32)
        weighed = prob * cross(d_o, m.v[window, :])
        d_s = (weighed - prob * jnp.sum(weighed, axis=1, keepdims=True)) * scale
        d_s = d_s.astype(bf16)
        d_q = plain(d_s, m.k[window, :])
        for l in range(shared // LANES):
            m.dq[l, rows, :] = d_q[:, LANES * l : LANES * l + LANES]
        m.dk[window, :] = m.dk[window, :] + inner(d_s, m.q[rows, :])
        m.dv[window, :] = m.dv[window, :] + inner(prob_low, d_o)
        return 0

    for n in range(blocks):
        attend(n, 0)
        turns.tick()
    m.need(m.z, m.qg, m.kg, m.sv, m.wsf, m.wag)

    def affine(i, sums):
        rows = at(i, block)
        d_q = jnp.concatenate([m.dq[l, rows, :] for l in range(shared // LANES)], axis=1)
        d_k, z = m.dk[rows, :], m.z[rows, :].astype(f32)
        m.dz[rows, :] = (d_q * m.qg[...] + d_k * m.kg[...]).astype(bf16)
        m.dvp[rows, :] = (m.dv[rows, :] * m.sv[rows, :].astype(f32)).astype(bf16)
        new = (d_q * z, d_q, d_k * z)
        return tuple(s + jnp.sum(n, axis=0, keepdims=True) for s, n in zip(sums, new))

    aff = lax.fori_loop(0, blocks, affine, tuple(jnp.zeros((1, shared), f32) for _ in range(3)))
    m.smo[...] = jnp.zeros(m.smo.shape, f32)
    for n in range(3):
        m.smo[2 + n : 3 + n, :shared] = aff[n]

    def mixing(j):
        def value(s):
            rows = pl.ds(s * (length // pieces), length // pieces)
            return cross(m.dz[rows, :], m.wsf[at(j, channels), :]) + cross(
                m.drp[rows, :], m.wag[at(j, channels), :]
            )

        return value

    m.need(m.y)
    for s in range(2):
        piece = pl.ds(s * half, half)
        m.out[piece, :] = (fed.take(s, m.bp[piece, :]) + m.y[piece, :]).astype(bf16)
    m.flush(m.out)
    fed.close()
    turns.tick()
    m.need(m.mx, m.xn)
    transposed_product(m.mx, m.drp, m.r, 2 * LANES)
    turns.tick()
    transposed_product(m.xn, m.dvp, m.os, 2 * LANES)
    begin(2)
    dm.put_diag(mixing(g.diag))
    turns.tick()
    dm.put_opp(mixing(g.opp))
    turns.tick()
    dm.put_sib(mixing(g.sib))
    turns.tick()
    m.need(m.wv)
    xv = Scatter(m, g, "xv", 2)
    spread = lambda j: pieces_of(cross(m.dvp[at(j, block), :], m.wv[...]), 2)
    split = lambda j: (lambda s: inner(m.mx[:, at(j, channels)], m.dz[...]))

    def spreading():
        xv.put_diag(spread(g.diag))
        xv.put_opp(spread(g.opp))
        turns.tick()
        xv.put_sib(spread(g.sib))
        m.bp[...] = cross(m.dvp[at(g.me, block), :], m.wv[...])
        turns.tick()
        sh.put_diag(split(g.diag))
        sh.put_opp(split(g.opp))
        turns.tick()
        sh.put_sib(split(g.sib))
        m.shp[...] = split(g.me)(0)
        turns.tick()

    m.need(m.se, m.st, m.xl, m.kf, m.tab, m.om)
    half_states = m.acc.shape[0] // 4
    m.acc[...] = jnp.zeros(m.acc.shape, f32)
    m.go[...] = jnp.zeros(m.go.shape, f32)
    gamma = tuple(jnp.zeros((SUB, LANES), f32) for _ in range(2 * half_states))
    per = length // SPAN // pieces
    own_mix = mixing(g.me)
    for s in range(pieces - 1, -1, -1):
        rows = pl.ds(s * (length // pieces), length // pieces)
        d_e = dm.take(s, own_mix(s)) * m.se[rows, :].astype(f32)
        for l in range(sides):
            m.dq[l, rows, :] = d_e[:, LANES * l : LANES * l + LANES]
        for n in range(per - 1, -1, -2):
            gamma = filter_backward(m, s * per + n, 2, gamma)
            turns.tick(2)
        for k, dev in enumerate(others):

            @pl.when(dev == s)
            def _():
                parts[k].start()

        if s == pieces - 1:
            spreading()
    filter_gradients(m)
    base_row = m.pk.shape[0] - PACK_TAIL
    m.pk[base_row:, :] = jnp.zeros((PACK_TAIL, channels), f32)
    m.pk[base_row : base_row + 1, :] = m.go[...]
    m.gs[...] = sh.take(0, m.shp[...]).astype(bf16)
    turns.tick()
    m.need(m.tok, m.so, m.gain, m.dy, m.gr, m.segb, m.segr)
    for s in range(2):
        piece = pl.ds(s * half, half)
        m.bp[piece, :] = xv.take(s, m.bp[piece, :])
    own_columns = at(g.me, channels)
    m.bp[:, own_columns] = m.bp[:, own_columns] + m.dxb[at(g.me, block), :].astype(f32)
    for k, dev in enumerate(others):
        parts[k].wait_recv()
        columns = at(dev, channels)
        m.bp[:, columns] = m.bp[:, columns] + m.dxr[k].astype(f32)
    gain_sum = jnp.zeros((1, width), f32)
    lane = lax.broadcasted_iota(jnp.int32, (half, LANES), 1)
    for s in range(2):
        piece = pl.ds(s * half, half)
        mean, rstd, total = (m.so[n, piece, :][:, :1] for n in range(3))
        centred = m.tok[piece, :].astype(f32) - mean
        d_xn = m.bp[piece, :]
        gain_sum = gain_sum + jnp.sum(d_xn * (centred * rstd), axis=0, keepdims=True)
        d_hat = d_xn * m.gain[...]
        d_var = -0.5 * rstd * rstd * rstd * jnp.sum(d_hat * centred, axis=1, keepdims=True)
        one = (-rstd * jnp.sum(d_hat, axis=1, keepdims=True) - 2.0 * mean * d_var) / total
        two = d_var / total
        m.bp[piece, :] = d_hat * rstd + m.dy[piece, :]
        m.aw[piece, :] = jnp.where(lane == 0, one, jnp.where(lane == 1, two, 0.0))
    m.smo[0:1, :] = gain_sum
    m.smo[1:2, :] = m.gr[...]
    turned = m.aw[...].T
    for n in range(2):
        rest = turned[n : n + 1, :]
        for k in range(3):
            top = rest.astype(bf16).astype(f32)
            m.art[3 * n + k : 3 * n + k + 1, :] = top
            rest = rest - top
    m.art[6:8, :] = jnp.zeros((2, block), f32)
    m.art[8:16, :] = jnp.zeros((8, block), f32)
    m.aro[...] = m.art[...].astype(bf16)
    for copy in tails + small:
        copy.start()
    m.ar[:, at(g.me, block)] = m.aro[...]
    m.sm[g.me] = m.smo[...]
    reach = -(-MAX_DOC // block)
    keys = min((reach + 1) * block, length)
    first_key = pl.multiple_of(jnp.minimum(g.me * block, length - keys), LANES)
    first_row = pl.multiple_of(g.me * block, LANES)
    here = m.segb[pl.ds(pl.multiple_of(first_row + SUB, SUB), block), :][:, :1]
    same = here == m.segr[:, pl.ds(first_key, keys)].astype(f32)
    row = first_row + lax.broadcasted_iota(jnp.int32, (block, keys), 0)
    key = first_key + lax.broadcasted_iota(jnp.int32, (block, keys), 1)
    seen = (same & (row <= key)).astype(bf16)
    for copy in tails:
        copy.wait_recv()
    pulled = cross(seen, m.ar[:, pl.ds(first_key, keys)])
    b_one = pulled[:, 0:1] + pulled[:, 1:2] + pulled[:, 2:3]
    b_two = pulled[:, 3:4] + pulled[:, 4:5] + pulled[:, 5:6]
    for s in range(2):
        piece = pl.ds(s * half, half)
        rows = slice(s * half, (s + 1) * half)
        x = m.tok[piece, :].astype(f32)
        m.gt[piece, :] = (m.bp[piece, :] + b_one[rows] + 2.0 * x * b_two[rows]).astype(bf16)
    m.flush(m.gt)
    turns.tick()
    for copy in small:
        copy.wait_recv()
    total = m.sm[0]
    for j in range(1, m.sm.shape[0]):
        total = total + m.sm[j]
    per = width // channels
    for n in range(2):
        for k in range(per):
            row = base_row + 1 + n * per + k
            m.pk[row : row + 1, :] = total[n : n + 1, k * channels : (k + 1) * channels]
    for n in range(3):
        row = base_row + 1 + 2 * per + n
        m.pk[row : row + 1, :shared] = total[2 + n : 3 + n, :shared]
    begin(3)
    turns.close()
    for moved in (dm, xv, sh, back):
        moved.close()
    for copy in parts + small + tails:
        copy.wait_send()


def body(count, m):
    g = Group()
    m.load(m.tok, m.wsh, m.cot, m.segr, m.p0, m.p1, m.p2, m.p3, m.p4, m.p5)
    m.load(m.gain, m.om, m.wv, m.wag, m.qg, m.qb, m.kg, m.wo, m.rg, m.wg, m.wu, m.wd)
    m.refs.update(mean=m.dq.at[0], rstd=m.dq.at[1])
    turns = Turns()
    plans = (
        [(m.gd, m.gdb, "gdt")],
        [(m.gg, m.ggb, "ggt"), (m.gu, m.gub, "gut")],
        [(m.gao, m.gaob, "gaot"), (m.r, m.gagb, "gagt"), (m.os, m.gvb, "gvt")],
    ) if count else ()
    rings = [Ring(m, count, plan) for plan in plans]
    if count:
        rings.append(Direct(m, count, [(m.gs, m.gsb, m.gss, "gst"), (m.pk, m.pkb, m.pks, "pkt")]))
        g.greet(rings[0].neighbours())
    else:
        g.greet()

    alone = (
        ((m.gd, "gdt"),),
        ((m.gg, "ggt"), (m.gu, "gut")),
        ((m.gao, "gaot"), (m.r, "gagt"), (m.os, "gvt")),
        ((m.gs, "gst"), (m.pk, "pkt")),
    )

    def begin(n):
        if rings:
            turns.begin(rings[n])
        else:
            for ref, name in alone[n]:
                m.store(ref, name)

    cots, normed = forward_attention(m, g)
    back = feed_forward(m, g, cots, normed, turns, begin)
    backward_attention(m, g, back, turns, begin)
    m.close()


def run(arrays, sizes, count):
    length, width, block, channels, shared, values, units = sizes
    blocks = length // block
    keys = min((-(-MAX_DOC // block) + 1) * block, length)
    sides = channels // LANES
    dims = arrays.p0.shape[0]
    half_states = sides * (dims // SUB)
    late = dict(
        gao=((values, width), bf16),
        gag=((width, values), bf16),
        gv=((width, values), bf16),
        gs=((channels, shared), bf16),
        pk=((6 * dims + PACK_TAIL, channels), f32),
    )
    summed = dict(
        gd=((units, width), bf16),
        gg=((width, units), bf16),
        gu=((width, units), bf16),
        **late,
    )
    if not ring_fits(summed.values(), count):
        count = 0
    outs = dict(
        gt=((block, width), bf16),
        out=((block, width), bf16),
    )
    scratch = dict(
        xt=((length, width), bf16),
        cotf=((length, width), bf16),
        xn=((length, width), bf16),
        mx=((length, width), bf16),
        xl=((sides, length, LANES), f32),
        tab=((11, dims, channels), f32),
        kf=((length + SUB, LANES), f32),
        segb=((length + SUB, LANES), f32),
        so=((3, block, LANES), f32),
        sums=((length, LANES), bf16),
        se=((length, channels), bf16),
        st=((length // SPAN, 2 * half_states, SUB, LANES), f32),
        v=((length, values), bf16),
        sv=((length, values), bf16),
        z=((length, shared), bf16),
        q=((length, shared), bf16),
        k=((length, shared), bf16),
        wsf=((width, shared), bf16),
        p=((blocks, block, keys), bf16),
        r=((length, values), bf16),
        os=((length, values), bf16),
        w=((length, values), bf16),
        y=((block, width), f32),
        rs=((block, LANES), f32),
        yno=((block, width), bf16),
        bp=((block, width), f32),
        act=((length, units), bf16),
        dg=((length, units), bf16),
        du=((length, units), bf16),
        gd=summed["gd"],
        dy=((block, width), f32),
        gr=((1, width), f32),
        dk=((length, shared), f32),
        dv=((length, values), f32),
        dq=((max(sides, shared // LANES), length, LANES), f32),
        shp=((channels, shared), f32),
        go=((1, channels), f32),
        acc=((4 * half_states, SUB, LANES), f32),
        kept=((SPAN, 2 * half_states, SUB, LANES), f32),
        part=((sides, SPAN * SUB, LANES), f32),
        dxr=((3, block, channels), bf16),
        art=((16, block), f32),
        aro=((16, block), bf16),
        ar=((16, length), bf16),
        smo=((SUB, width), f32),
        sm=((length // block, SUB, width), f32),
        gao=late["gao"],
        gs=late["gs"],
        pk=late["pk"],
        **scatter_buffers("dm", length, channels),
        **scatter_buffers("xv", block, width),
        **scatter_buffers("sh", channels, shared),
    )
    alias = dict(yn="xt", dyf="cotf", gg="wg", gu="wu", dyo="yno", dvp="v", aw="rs")
    alias.update(dz="q", dxb="k", drp="w", mxl="dm_os")
    shared_boxes = dict(gag="dg", gv="du")
    sems = [69, 69]
    if count:
        for name, (shape, kind) in summed.items():
            small = name in ("gs", "pk")
            used = count - 1, *(ring_rows(shape, kind, count) or ())
            if name in shared_boxes and 2 * used[0] * used[1] <= length and used[2] <= units:
                alias[name + "b"] = shared_boxes[name]
                continue
            scratch[name + "b"] = (direct_box if small else ring_box)(shape, kind, count)
        scratch.update(gss=summed["gs"], pks=summed["pk"])
        sems = [69 + 12 + 4 * (count - 1), 69 + 12 * count + 4 * (count - 1)]
    bare = {name + "t": entry for name, entry in summed.items()}
    done = run_stage(
        functools.partial(body, count), arrays, outs, scratch, sems, 1, bare.items(), alias.items()
    )
    done.dims = dims
    done.summed = bool(count)
    return done


def body_f(dims, shared, m):
    wide = ((m.gd, m.gdt), (m.gg, m.ggt), (m.gu, m.gut), (m.gao, m.gaot), (m.gag, m.gagt))
    wide += ((m.gv, m.gvt), (m.gs, m.gst))
    m.load(m.out, m.gt, m.gd, m.gg, m.gu, m.gao, m.gag, m.gv, m.gs, m.pk)
    for source, target in ((m.out, m.outt), (m.gt, m.gtt)):
        m.need(source)
        target[...] = source[...]
        m.flush(target)
    for source, target in wide:
        m.need(source)
        rows = source.shape[0] // 2
        for n in range(2):

            def part(i, _):
                piece = pl.ds(pl.multiple_of(n * rows + i * 16, 16), 16)
                target[piece, :] = source[piece, :].astype(f32)
                return 0

            lax.fori_loop(0, rows // 16, part, 0, unroll=4)
        m.flush(target)
    m.need(m.pk)
    for k, out in enumerate((m.e0, m.e1, m.e2, m.e3, m.e4, m.e5)):
        out[...] = m.pk[k * dims : (k + 1) * dims, :]
    top = 6 * dims
    channels = m.pk.shape[1]
    m.om[...] = m.pk[top : top + 1, :]
    per = m.norm.shape[1] // channels
    for n, out in enumerate((m.norm, m.rms)):
        for k in range(per):
            row = top + 1 + n * per + k
            out[:, k * channels : (k + 1) * channels] = m.pk[row : row + 1, :]
    for n, out in enumerate((m.qg, m.qb, m.kg)):
        row = top + 1 + 2 * per + n
        out[...] = m.pk[row : row + 1, :shared]
    m.flush(m.e0, m.e1, m.e2, m.e3, m.e4, m.e5, m.om, m.norm, m.rms, m.qg, m.qb, m.kg)
    m.close()


def finish(c, shared):
    sums = dict(gd=c.gdt, gg=c.ggt, gu=c.gut, gao=c.gaot, gag=c.gagt, gv=c.gvt, gs=c.gst, pk=c.pkt)
    if not c.summed:
        total = lax.psum([value.astype(f32) for value in sums.values()], "dp")
        sums = {name: v.astype(old.dtype) for (name, old), v in zip(sums.items(), total)}
    channels, width = sums["pk"].shape[1], sums["gd"].shape[1]
    outs = dict(
        e0=((c.dims, channels), f32),
        e1=((c.dims, channels), f32),
        e2=((c.dims, channels), f32),
        e3=((c.dims, channels), f32),
        e4=((c.dims, channels), f32),
        e5=((c.dims, channels), f32),
        om=((1, channels), f32),
        norm=((1, width), f32),
        rms=((1, width), f32),
        qg=((1, shared), f32),
        qb=((1, shared), f32),
        kg=((1, shared), f32),
    )
    for name, value in sums.items():
        if value is not sums["pk"]:
            outs[name + "t"] = (value.shape, f32)
    outs.update(outt=(c.out.shape, bf16), gtt=(c.gt.shape, bf16))
    f = run_stage(
        functools.partial(body_f, c.dims, shared),
        types.SimpleNamespace(out=c.out, gt=c.gt, **sums), outs, {}, (0, 0), None,
    )
    tables = [table.T for table in (f.e0, f.e1, f.e2, f.e3, f.e4, f.e5)]
    return (
        f.outt, f.gtt, f.norm[0], *tables, f.om[0], f.gst,
        f.qg[0], f.qb[0], f.kg[0], f.gagt, f.gvt, f.gaot, f.rms[0], f.ggt, f.gut, f.gdt,
    )


def on_device(
    tokens,
    segments,
    cotangent,
    timestep_norm_gain,
    ema_alpha,
    ema_delta,
    ema_theta,
    ema_beta,
    eta_real,
    eta_imag,
    ema_omega,
    w_shared,
    q_gain,
    q_bias,
    k_gain,
    w_attgate,
    w_value,
    w_attout,
    rms_gain,
    w_gate,
    w_up,
    w_down,
):
    block, width = tokens.shape
    length = segments.shape[1]
    channels, dims = ema_alpha.shape
    shared = w_shared.shape[1]
    values = w_value.shape[1]
    units = w_gate.shape[1]
    om = ema_omega[None]
    gain, rg = timestep_norm_gain[None], rms_gain[None]
    qg, qb, kg = q_gain[None], q_bias[None], k_gain[None]
    segr = segments
    done = run(
        types.SimpleNamespace(
            tok=tokens, cot=cotangent, wsh=w_shared, segr=segr, gain=gain,
            p0=ema_alpha.T, p1=ema_delta.T, p2=ema_theta.T,
            p3=ema_beta.T, p4=eta_real.T, p5=eta_imag.T, om=om, qg=qg, qb=qb, kg=kg,
            wag=w_attgate, wv=w_value, wo=w_attout, rg=rg, wg=w_gate, wu=w_up, wd=w_down,
        ),
        (length, width, block, channels, shared, values, units),
        lax.axis_size("dp"),
    )
    return finish(done, shared)


def solution(mesh):
    placed = (
        P(("dp", "tensor"), None),
        P("dp", None),
        P(("dp", "tensor"), None),
        P(),
        P("tensor", None),
        P("tensor", None),
        P("tensor", None),
        P("tensor", None),
        P("tensor", None),
        P("tensor", None),
        P("tensor"),
        P("tensor", None),
        P(),
        P(),
        P(),
        P(None, "tensor"),
        P(None, "tensor"),
        P("tensor", None),
        P(),
        P(None, "tensor"),
        P(None, "tensor"),
        P("tensor", None),
    )
    return jax.shard_map(
        on_device,
        mesh=mesh,
        in_specs=placed,
        out_specs=(
            P(("dp", "tensor"), None),
            P(("dp", "tensor"), None),
            P(),
            P("tensor", None),
            P("tensor", None),
            P("tensor", None),
            P("tensor", None),
            P("tensor", None),
            P("tensor", None),
            P("tensor"),
            P("tensor", None),
            P(),
            P(),
            P(),
            P(None, "tensor"),
            P(None, "tensor"),
            P("tensor", None),
            P(),
            P(None, "tensor"),
            P(None, "tensor"),
            P("tensor", None),
        ),
        check_vma=False,
    )
```

```python
import functools
import math
import types

import jax
import jax.numpy as jnp
from jax import lax
from jax.experimental import pallas as pl
from jax.experimental.pallas import tpu as pltpu
from jax.sharding import PartitionSpec as P

epsilon = 1e-05
masked_score = -1000000000.0
f32 = jnp.float32
bf16 = jnp.bfloat16
MESH = pl.DeviceIdType.MESH
LANES = 128
SUB = 8
SPAN = 64
MAX_DOC = 512
PACK_TAIL = 32
VMEM_BYTES = 62 * 2**20


def plain(left, right):
    return jnp.dot(left, right, preferred_element_type=f32)


def cross(left, right):
    return lax.dot_general(
        left, right, (((1,), (1,)), ((), ())), preferred_element_type=f32
    )


def inner(left, right):
    return lax.dot_general(
        left, right, (((0,), (0,)), ((), ())), preferred_element_type=f32
    )


def sigmoid(value):
    return 1.0 / (1.0 + jnp.exp(-value))


def at(index, size):
    return pl.ds(pl.multiple_of(index * size, size), size)


class Stage:
    def __init__(self, ins, outs, bare, scratch, alias, refs):
        self.pending = {}
        self.flushed = []
        count = len(ins)
        self.hbm_in = dict(zip(ins, refs[:count]))
        total = len(outs) + len(bare)
        self.hbm_out = dict(zip(list(outs) + list(bare), refs[count : count + total]))
        rest = refs[count + total :]
        names = list(ins) + list(outs) + list(scratch)
        self.refs = dict(zip(names, rest[: len(names)]))
        self.load_sem, self.flush_sem, self.send_sem, self.recv_sem = rest[len(names) :]
        self.order = {name: k for k, name in enumerate(ins)}
        self.out_order = {name: k for k, name in enumerate(self.hbm_out)}
        self.sends = self.receipts = 0
        self.sets = {}
        self.names = {id(ref): name for name, ref in self.refs.items()}
        for name, other in alias:
            self.refs[name] = self.refs[other]

    def __getitem__(self, name):
        return self.refs[name]

    def __getattr__(self, name):
        return self.refs[name]

    def load(self, *refs):
        for name in [self.names[id(ref)] for ref in refs]:
            copy = pltpu.make_async_copy(
                self.hbm_in[name], self.refs[name], self.load_sem.at[self.order[name]]
            )
            copy.start()
            self.pending[name] = copy

    def need(self, *refs):
        for name in [self.names[id(ref)] for ref in refs]:
            copy = self.pending.pop(name, None)
            if copy is not None:
                copy.wait()

    def flush(self, *refs):
        for name in [self.names[id(ref)] for ref in refs]:
            if name in self.hbm_out:
                self.store(self.refs[name], name)

    def store(self, source, name):
        copy = pltpu.make_async_copy(
            source, self.hbm_out[name], self.flush_sem.at[self.out_order[name]]
        )
        copy.start()
        self.flushed.append(copy)

    def close(self):
        assert self.sends <= self.send_sem.shape[0]
        assert self.receipts <= self.recv_sem.shape[0]
        for copy in self.flushed:
            copy.wait()


    def sems(self, count, sends=None, key=None):
        if key in self.sets:
            return self.sets[key]
        first = self.sends, self.receipts
        self.sends += count if sends is None else sends
        self.receipts += count
        if key:
            self.sets[key] = first
        return first

    def remote(self, source, target_ref, base, index, device, sent=None):
        return pltpu.make_async_remote_copy(
            src_ref=source,
            dst_ref=target_ref,
            send_sem=self.send_sem.at[base[0] + (index if sent is None else sent)],
            recv_sem=self.recv_sem.at[base[1] + index],
            device_id=device,
            device_id_type=MESH,
        )


def run_stage(body, ins, outs, scratch, sems, collective, bare=(), alias=()):
    ins = vars(ins)
    written = {**outs, **dict(bare)}

    def kernel(*refs):
        body(Stage(list(ins), list(outs), list(dict(bare)), list(scratch), alias, refs))

    buffers = [pltpu.VMEM(array.shape, array.dtype) for array in ins.values()]
    buffers += [pltpu.VMEM(shape, kind) for shape, kind in outs.values()]
    buffers += [pltpu.VMEM(shape, kind) for shape, kind in scratch.values()]
    results = pl.pallas_call(
        kernel,
        out_shape=tuple(jax.ShapeDtypeStruct(shape, kind) for shape, kind in written.values()),
        in_specs=[pl.BlockSpec(memory_space=pl.ANY)] * len(ins),
        out_specs=tuple(pl.BlockSpec(memory_space=pl.ANY) for _ in written),
        scratch_shapes=buffers
        + [
            pltpu.SemaphoreType.DMA((len(ins),)),
            pltpu.SemaphoreType.DMA((len(written),)),
            pltpu.SemaphoreType.DMA((max(sems[0], 1),)),
            pltpu.SemaphoreType.DMA((max(sems[1], 1),)),
        ],
        compiler_params=pltpu.CompilerParams(
            collective_id=collective,
            has_side_effects=collective is not None,
            vmem_limit_bytes=VMEM_BYTES,
        ),
    )(*ins.values())
    return types.SimpleNamespace(**dict(zip(written, results)))


class Group:
    def __init__(self):
        self.me = lax.axis_index("tensor")
        chip = self.me // 2
        core = self.me % 2
        self.sib = chip * 2 + (1 - core)
        self.opp = (1 - chip) * 2 + core
        self.diag = (1 - chip) * 2 + (1 - core)

    def greet(self, more=()):
        barrier = pltpu.get_barrier_semaphore()
        for device in more:
            pl.semaphore_signal(barrier, inc=1, device_id={"dp": device}, device_id_type=MESH)
        for device in (self.sib, self.opp, self.diag):
            pl.semaphore_signal(barrier, inc=1, device_id={"tensor": device}, device_id_type=MESH)
        pl.semaphore_wait(barrier, 3 + len(more))


class Gather:
    def __init__(self, stage, group, source, place, pieces, key=None):
        self.g = group
        self.pieces = pieces
        base = stage.sems(3 * pieces, key=key)
        opp = {"tensor": group.opp}
        sib = {"tensor": group.sib}
        self.to_opp = [
            stage.remote(source(s), place(group.me, s), base, s, opp) for s in range(pieces)
        ]
        self.to_sib = [
            stage.remote(source(s), place(group.me, s), base, pieces + s, sib)
            for s in range(pieces)
        ]
        self.passed = [
            stage.remote(place(group.opp, s), place(group.opp, s), base, 2 * pieces + s, sib)
            for s in range(pieces)
        ]

    def send(self, s):
        self.to_opp[s].start()
        self.to_sib[s].start()

    def forward(self, s):
        self.to_opp[s].wait_recv()
        self.passed[s].start()

    def near(self):
        for s in range(self.pieces):
            self.to_sib[s].wait_recv()

    def far(self):
        for s in range(self.pieces):
            self.passed[s].wait_recv()

    def close(self):
        for copy in self.to_opp + self.to_sib + self.passed:
            copy.wait_send()


class Scatter:
    def __init__(self, stage, group, name, pieces, order=None):
        self.order = list(order or range(pieces))
        self.out_diag = stage[name + "_od"]
        self.out_sib = stage[name + "_os"]
        self.out_opp = stage[name + "_oo"]
        self.in_opp = stage[name + "_io"]
        self.in_own = stage[name + "_iw"]
        self.in_far = stage[name + "_if"]
        self.rows = self.out_diag.shape[0] // pieces
        base = stage.sems(3 * pieces, key=name)

        def copies(source, target, first, device):
            return [
                stage.remote(
                    source.at[self.part(s)], target.at[self.part(s)], base, first + s, {"tensor": device}
                )
                for s in range(pieces)
            ]

        self.first = copies(self.out_diag, self.in_opp, 0, group.sib)
        self.second = copies(self.out_sib, self.in_own, pieces, group.sib)
        self.across = copies(self.out_opp, self.in_far, 2 * pieces, group.opp)

    def part(self, s):
        return pl.ds(s * self.rows, self.rows)

    def put_diag(self, value, only=None):
        for s in self.order if only is None else [only]:
            self.out_diag[self.part(s), :] = value(s).astype(bf16)
            self.first[s].start()

    def put_opp(self, value, only=None):
        for s in self.order if only is None else [only]:
            mine = value(s)
            self.first[s].wait_recv()
            total = mine + self.in_opp[self.part(s), :].astype(f32)
            self.out_opp[self.part(s), :] = total.astype(bf16)
            self.across[s].start()

    def put_sib(self, value):
        self.fill_sib(value)
        self.send_sib()

    def fill_sib(self, value):
        for s in self.order:
            self.out_sib[self.part(s), :] = value(s).astype(bf16)

    def send_sib(self):
        for s in self.order:
            self.second[s].start()

    def take(self, s, own):
        self.second[s].wait_recv()
        near = own + self.in_own[self.part(s), :].astype(f32)
        self.across[s].wait_recv()
        return near + self.in_far[self.part(s), :].astype(f32)

    def close(self):
        for copy in self.first + self.second + self.across:
            copy.wait_send()


def pieces_of(value, count):
    rows = value.shape[0] // count
    return lambda s: value[s * rows : (s + 1) * rows]


def scatter_buffers(name, rows, width):
    return {
        name + tail: ((rows, width), bf16) for tail in ("_od", "_os", "_oo", "_io", "_iw", "_if")
    }


def ring_seats(count):
    index = lax.axis_index("dp")
    place = jnp.where(index % 2 == 0, index // 2, count - 1 - index // 2)

    def seat(p):
        p = lax.rem(p + 2 * count, count)
        return jnp.where(2 * p < count, 2 * p, 2 * (count - 1 - p) + 1)

    return place, seat


def ring_rows(shape, kind, count):
    tile = 16 if kind == bf16 else SUB
    if shape[0] % (2 * count * tile) == 0:
        return shape[0] // (2 * count), shape[1]
    if shape[0] % (count * tile) == 0 and shape[1] % (2 * LANES) == 0:
        return shape[0] // count, shape[1] // 2
    return None


class Ring:
    def __init__(self, m, count, items):
        self.m = m
        self.count = count
        self.items = items
        self.place, self.seat = ring_seats(count)
        self.steps = 2 * (count - 1)
        self.ahead = self.pause = 0
        self.base = m.sems(len(items) * 2 * count, len(items) * 2)
        self.step = 0

    def neighbours(self):
        return self.seat(self.place - 1), self.seat(self.place + 1)

    def view(self, ref, chunk, way):
        shape = ref.shape
        rows, columns = ring_rows(shape, ref.dtype, self.count)
        chunk = lax.rem(chunk + 2 * self.count, self.count)
        if columns == shape[1]:
            return ref.at[pl.ds(pl.multiple_of((2 * chunk + way) * rows, rows), rows), :]
        return ref.at[
            pl.ds(pl.multiple_of(chunk * rows, rows), rows), pl.ds(way * columns, columns)
        ]

    def slot(self, item, way, step):
        own, box, _ = self.items[item]
        if len(box.shape) == 4:
            return box.at[way, step]
        rows, columns = ring_rows(own.shape, own.dtype, self.count)
        first = (way * (self.count - 1) + step) * rows
        return box.at[pl.ds(first, rows), pl.ds(0, columns)]

    def copy(self, item, way, step):
        own = self.items[item][0]
        sign = 1 - 2 * way
        last = self.count - 1
        place = 2 * item + way
        index = place * self.count + step % self.count
        if step < last:
            source = self.view(own, self.place, way) if step == 0 else self.slot(item, way, step - 1)
            target = self.slot(item, way, step)
        else:
            source = self.view(own, self.place + sign - sign * (step - last), way)
            target = source
        device = {"dp": self.seat(self.place + sign)}
        return self.m.remote(source, target, self.base, index, device, place)

    def start(self, item, way, step):
        self.copy(item, way, step).start()

    def begin(self):
        for item in range(len(self.items)):
            for way in range(2):
                self.start(item, way, 0)

    def tick(self):
        last = self.count - 1
        step = self.step
        self.step = step + 1
        for item, (own, _, name) in enumerate(self.items):
            for way in range(2):
                sign = 1 - 2 * way
                self.copy(item, way, step).wait_recv()
                self.copy(item, way, step).wait_send()
                if step < last:
                    chunk = self.view(own, self.place - sign * (step + 1), way)
                    box = self.slot(item, way, step)
                    value = box[...].astype(f32) + chunk[...].astype(f32)
                    if step < last - 1:
                        box[...] = value.astype(own.dtype)
                    else:
                        chunk[...] = value.astype(own.dtype)
                if step + 1 < self.steps:
                    self.start(item, way, step + 1)
                if step >= last - 1:
                    self.keep(own, name, self.place + sign - sign * (step + 1 - last), way)
        return step + 1 == self.steps

    def keep(self, own, name, chunk, way):
        out = self.m.hbm_out[name]
        sem = self.m.flush_sem.at[self.m.out_order[name]]
        pltpu.make_async_copy(self.view(own, chunk, way), self.view(out, chunk, way), sem).start()

    def close(self):
        for own, _, name in self.items:
            sem = self.m.flush_sem.at[self.m.out_order[name]]
            pltpu.make_async_copy(own, self.m.hbm_out[name], sem).wait()


class Direct:
    def __init__(self, m, count, items):
        self.m = m
        self.count = count
        self.items = items
        self.me = lax.axis_index("dp")
        self.base = m.sems(2 * len(items) * (count - 1))
        self.step = 0
        self.steps = 2
        self.ahead = 2 * count
        self.pause = 3

    def share(self, ref, index):
        return ref.at[at(index, ref.shape[0] // self.count), :]

    def copies(self, step):
        made = []
        for item, (own, box, total, _) in enumerate(self.items):
            for r in range(1, self.count):
                there = lax.rem(self.me + r, self.count)
                index = (2 * item + step) * (self.count - 1) + r - 1
                if step == 0:
                    source, target = self.share(own, there), box.at[r - 1]
                else:
                    source = target = self.share(total, self.me)
                made.append(self.m.remote(source, target, self.base, index, {"dp": there}))
        return made

    def begin(self):
        for copy in self.copies(0):
            copy.start()

    def tick(self):
        for copy in self.copies(self.step):
            copy.wait_recv()
        if self.step == 0:
            for own, box, total, _ in self.items:
                value = self.share(own, self.me)[...].astype(f32)
                for r in range(self.count - 1):
                    value = value + box[r].astype(f32)
                self.share(total, self.me)[...] = value.astype(total.dtype)
            for copy in self.copies(1):
                copy.start()
        self.step += 1
        return self.step == 2

    def close(self):
        for copy in self.copies(0) + self.copies(1):
            copy.wait_send()
        for _, _, total, name in self.items:
            self.m.store(total, name)


class Turns:
    def __init__(self):
        self.waiting = []
        self.rings = []
        self.recent = []

    def begin(self, ring):
        ring.begin()
        self.waiting.append(ring)
        self.rings.append(ring)
        self.recent.append(ring)

    def tick(self, times=1):
        for _ in range(times):
            if self.waiting:
                others = [one for one in self.waiting if one not in self.recent[-1 - one.pause :]]
                others = others or [one for one in self.waiting if not one.pause] or self.waiting
                ring = max(others, key=lambda one: one.ahead + one.steps - one.step)
                self.recent.append(ring)
                if ring.tick():
                    self.waiting.remove(ring)

    def close(self):
        while self.waiting:
            self.tick()
        for ring in self.rings:
            ring.close()


def ring_box(shape, kind, count):
    rows, columns = ring_rows(shape, kind, count)
    return ((2, count - 1, rows, columns), kind)


def direct_box(shape, kind, count):
    return ((count - 1, shape[0] // count, shape[1]), kind)


def ring_fits(shapes, count):
    return (
        count > 1
        and count % 2 == 0
        and all(ring_rows(shape, kind, count) for shape, kind in shapes)
    )


def groups(array):
    halves = array.shape[0] // SUB
    sides = array.shape[1] // LANES
    return [
        array[SUB * s : SUB * s + SUB, LANES * l : LANES * l + LANES]
        for s in range(halves)
        for l in range(sides)
    ]


def spread_row(ref, index):
    return jnp.broadcast_to(ref[index], (SUB, LANES))


def advance(state, coefs, keep, signals, sides):
    root_real, root_imag = coefs
    half = len(state) // 2
    kept = [value * keep for value in state]
    fresh = [None] * len(state)
    for g in range(half):
        a_real, a_imag = kept[g], kept[half + g]
        fresh[g] = (root_real[g] * a_real - root_imag[g] * a_imag) + signals[g % sides]
        fresh[half + g] = root_real[g] * a_imag + root_imag[g] * a_real
    return kept, fresh


def filter_forward(m, first, count, state):
    sides = m.xl.shape[0]
    tables = m.tab
    root_real, root_imag = groups(tables[0]), groups(tables[1])
    out_real, out_imag = groups(tables[2]), groups(tables[3])
    half = len(root_real)
    unroll = 16

    def chunk(ch, state):
        for g in range(2 * half):
            m.st[ch, g] = state[g]

        def steps(i, state):
            state = list(state)
            for j in range(unroll):
                t = ch * SPAN + i * unroll + j
                keep = spread_row(m.kf, (pl.ds(t, 1), slice(None)))
                signals = [
                    spread_row(m.xl, (l, pl.ds(t, 1), slice(None))) for l in range(sides)
                ]
                _, state = advance(state, (root_real, root_imag), keep, signals, sides)
                for l in range(sides):
                    total = None
                    for g in range(l, half, sides):
                        term = out_real[g] * state[g] - out_imag[g] * state[half + g]
                        total = term if total is None else total + term
                    m.part[l, pl.ds(pl.multiple_of((i * unroll + j) * SUB, SUB), SUB), :] = total
            return tuple(state)

        state = lax.fori_loop(0, SPAN // unroll, steps, state)
        rows = at(ch, SPAN)
        for l in range(sides):
            lanes = slice(LANES * l, LANES * l + LANES)
            value = m.om[:, lanes] * m.xl[l, rows, :]
            for s in range(SUB):
                value = value + m.part[l, pl.ds(s, SPAN, stride=SUB), :]
            gate = sigmoid(value)
            m.mxl[rows, lanes] = (value * gate).astype(bf16)
            m.se[rows, lanes] = (gate * (1.0 + value * (1.0 - gate))).astype(bf16)
        return state

    return lax.fori_loop(first, first + count, chunk, state)


def window_mask(m, first_row, rows, first_key, keys):
    here = m.segb[pl.ds(pl.multiple_of(first_row + SUB, SUB), rows), :][:, :1]
    same = here == m.segr[:, pl.ds(pl.multiple_of(first_key, LANES), keys)].astype(f32)
    row = first_row + lax.broadcasted_iota(jnp.int32, (rows, keys), 0)
    key = first_key + lax.broadcasted_iota(jnp.int32, (rows, keys), 1)
    return same & (row >= key)


def window_of(index, block, length):
    back = -(-MAX_DOC // block)
    keys = min((back + 1) * block, length)
    first = jnp.maximum(index - back, 0) * block
    first = jnp.minimum(first, length - keys)
    return pl.multiple_of(first, LANES), keys


def keeping(m):
    length = m.segr.shape[1]
    m.segb[:SUB, :] = jnp.full((SUB, LANES), -1.0, f32)
    for k in range(length // LANES):
        row = m.segr[:, k * LANES : (k + 1) * LANES].astype(f32)
        m.segb[SUB + k * LANES : SUB + (k + 1) * LANES, :] = jnp.broadcast_to(row, (LANES, LANES)).T
    for k in range(length // LANES):
        now = m.segb[SUB + k * LANES : SUB + (k + 1) * LANES, :]
        before = m.segb[SUB - 1 + k * LANES : SUB - 1 + (k + 1) * LANES, :]
        m.kf[k * LANES : (k + 1) * LANES, :] = jnp.where(now == before, 1.0, 0.0)
    m.kf[length:, :] = jnp.zeros((SUB, LANES), f32)


def filter_tables(m):
    alpha, delta, theta, beta, e_re, e_im = (
        ref[...] for ref in (m.p0, m.p1, m.p2, m.p3, m.p4, m.p5)
    )
    magnitude = 1.0 - alpha * delta
    cosine, sine = jnp.cos(theta), jnp.sin(theta)
    scaled = alpha * beta
    entries = (
        magnitude * cosine, magnitude * sine, scaled * e_re, scaled * e_im,
        cosine, sine, alpha, delta, beta, e_re, e_im,
    )
    for k, entry in enumerate(entries):
        m.tab[k] = entry


def forward_attention(m, g):
    length, width = m.xt.shape
    block = m.tok.shape[0]
    blocks = length // block
    channels = m.mxl.shape[1]
    sides = channels // LANES
    own = at(g.me, block)
    half = block // 2
    tokens = Gather(
        m, g,
        lambda s: m.tok.at[pl.ds(s * half, half), :],
        lambda j, s: m.xt.at[pl.ds(pl.multiple_of(j * block + s * half, half), half), :],
        2, "rows",
    )
    shared = Gather(m, g, lambda s: m.wsh, lambda j, s: m.wsf.at[at(j, channels), :], 1)
    pieces = 8
    rows_piece = length // pieces
    mixed = Gather(
        m, g,
        lambda s: m.mxl.at[pl.ds(s * rows_piece, rows_piece), :],
        lambda j, s: m.mx.at[pl.ds(s * rows_piece, rows_piece), at(j, channels)],
        pieces,
    )
    cots = Gather(
        m, g,
        lambda s: m.cot.at[pl.ds(s * half, half), :],
        lambda j, s: m.cotf.at[pl.ds(pl.multiple_of(j * block + s * half, half), half), :],
        2,
    )
    normed = Gather(
        m, g,
        lambda s: m.yno.at[pl.ds(s * half, half), :],
        lambda j, s: m.yn.at[pl.ds(pl.multiple_of(j * block + s * half, half), half), :],
        2, "rows",
    )
    branch = Scatter(m, g, "xv", 2)

    m.need(m.tok, m.wsh)
    tokens.send(0)
    tokens.send(1)
    shared.send(0)
    m.need(m.cot)
    cots.send(0)
    m.xt[own, :] = m.tok[...]
    m.wsf[at(g.me, channels), :] = m.wsh[...]
    m.need(m.segr, m.p0, m.p1, m.p2, m.p3, m.p4, m.p5, m.gain, m.om)
    keeping(m)
    filter_tables(m)

    lane = lax.broadcasted_iota(jnp.int32, (SPAN, LANES), 1)

    def sums(j):
        def part(i, _):
            rows = pl.ds(pl.multiple_of(j * block + i * SPAN, SPAN), SPAN)
            one = jnp.zeros((SPAN, LANES), f32)
            two = jnp.zeros((SPAN, LANES), f32)
            for l in range(width // LANES):
                x = m.xt[rows, LANES * l : LANES * l + LANES].astype(f32)
                one = one + x
                two = two + x * x
            picked = jnp.where(lane == 6, 1.0, 0.0)
            for k, total in ((0, one), (3, two)):
                rest = jnp.sum(total, axis=1, keepdims=True)
                for n in range(3):
                    top = rest.astype(bf16).astype(f32)
                    picked = jnp.where(lane == k + n, top, picked)
                    rest = rest - top
            m.sums[rows, :] = picked.astype(bf16)
            return 0

        lax.fori_loop(0, block // SPAN, part, 0)

    sums(g.me)
    tokens.near()
    sums(g.sib)
    tokens.forward(0)
    tokens.forward(1)
    sums(g.opp)
    tokens.far()
    sums(g.diag)

    lane_wide = lax.broadcasted_iota(jnp.int32, (block, LANES), 1)

    def statistics(i, _):
        first, keys = window_of(i, block, length)
        seen = window_mask(m, i * block, block, first, keys).astype(bf16)
        got = plain(seen, m.sums[pl.ds(first, keys), :])
        pick = lambda low, high: jnp.sum(
            jnp.where((lane_wide >= low) & (lane_wide < high), got, 0.0), axis=1, keepdims=True
        )
        total = pick(6, 7) * width
        mean = pick(0, 3) / total
        var = pick(3, 6) / total - mean * mean
        rows = at(i, block)
        m.mean[rows, :] = jnp.broadcast_to(mean, (block, LANES))
        m.rstd[rows, :] = jnp.broadcast_to(lax.rsqrt(var + epsilon), (block, LANES))

        @pl.when(i == g.me)
        def _():
            m.so[0] = m.mean[rows, :]
            m.so[1] = m.rstd[rows, :]
            m.so[2] = jnp.broadcast_to(total, (block, LANES))

        return 0

    lax.fori_loop(0, blocks, statistics, 0)

    def normalise(i, _):
        rows = at(i, SPAN)
        mean, rstd = m.mean[rows, :], m.rstd[rows, :]
        for l in range(width // LANES):
            lanes = slice(LANES * l, LANES * l + LANES)
            x = m.xt[rows, lanes].astype(f32)
            m.xn[rows, lanes] = ((x - mean) * rstd * m.gain[:, lanes]).astype(bf16)
        for l in range(sides):
            lanes = pl.ds(pl.multiple_of(g.me * channels + LANES * l, LANES), LANES)
            x = m.xt[rows, lanes].astype(f32)
            m.xl[l, rows, :] = (x - mean) * rstd * m.gain[:, lanes]
        return 0

    lax.fori_loop(0, length // SPAN, normalise, 0)
    tokens.close()

    zero = jnp.zeros((SUB, LANES), f32)
    state = tuple(zero for _ in range(m.st.shape[1]))
    per = length // SPAN // pieces
    for p in range(pieces):
        state = filter_forward(m, p * per, per, state)
        mixed.send(p)
        if p >= 2:
            mixed.forward(p - 2)
    cots.send(1)
    for i in range(pieces):
        m.mx[pl.ds(i * rows_piece, rows_piece), at(g.me, channels)] = m.mxl[
            pl.ds(i * rows_piece, rows_piece), :
        ]
    m.cotf[own, :] = m.cot[...]
    m.need(m.wv)

    def values(i, _):
        rows = at(i, block)
        pre = plain(m.xn[rows, :], m.wv[...])
        gate = sigmoid(pre)
        m.v[rows, :] = (pre * gate).astype(bf16)
        m.sv[rows, :] = (gate * (1.0 + pre * (1.0 - gate))).astype(bf16)
        return 0

    lax.fori_loop(0, blocks, values, 0)
    for p in range(max(pieces - 2, 0), pieces):
        mixed.forward(p)
    shared.forward(0)
    shared.near()
    shared.far()
    mixed.near()
    mixed.far()
    m.need(m.qg, m.qb, m.kg, m.wag, m.wo, m.rg)

    def project(i, _):
        rows = at(i, block)
        z = plain(m.mx[rows, :], m.wsf[...])
        m.z[rows, :] = z.astype(bf16)
        m.q[rows, :] = (z * m.qg[...] + m.qb[...]).astype(bf16)
        m.k[rows, :] = (z * m.kg[...]).astype(bf16)
        return 0

    lax.fori_loop(0, blocks, project, 0)
    scale = 1.0 / math.sqrt(m.q.shape[1])

    def attend(i, part, count):
        size = block // count
        start = pl.multiple_of(i * block + part * size, size)
        rows = pl.ds(start, size)
        first, keys = window_of(i, block, length)
        window = pl.ds(first, keys)
        scores = cross(m.q[rows, :], m.k[window, :]) * scale
        scores = jnp.where(window_mask(m, start, size, first, keys), scores, masked_score)
        expo = jnp.exp(scores - jnp.max(scores, axis=1, keepdims=True))
        prob = (expo / jnp.sum(expo, axis=1, keepdims=True)).astype(bf16)
        m.p[i, pl.ds(part * size, size), :] = prob
        attended = plain(prob, m.v[window, :])
        pre = plain(m.mx[rows, :], m.wag[...])
        gate = sigmoid(pre)
        swish = pre * gate
        m.r[rows, :] = swish.astype(bf16)
        m.os[rows, :] = (attended * (gate * (1.0 + pre * (1.0 - gate)))).astype(bf16)
        m.w[rows, :] = (attended * swish).astype(bf16)
        return plain(m.w[rows, :], m.wo[...])

    for n in range(2):
        branch.put_diag(lambda s: attend(g.diag, s, 2), n)
        branch.put_opp(lambda s: attend(g.opp, s, 2), n)
    cots.forward(0)
    branch.put_sib(pieces_of(attend(g.sib, 0, 1), 2))
    cots.forward(1)
    m.bp[...] = attend(g.me, 0, 1)
    for s in range(2):
        piece = pl.ds(s * half, half)
        y = branch.take(s, m.bp[piece, :]) + m.tok[piece, :].astype(f32)
        m.y[piece, :] = y
        rms = lax.rsqrt(jnp.mean(y * y, axis=1, keepdims=True) + epsilon)
        m.rs[piece, :] = jnp.broadcast_to(rms, (half, LANES))
        m.yno[piece, :] = (y * rms * m.rg[...]).astype(bf16)
        normed.send(s)
    m.yn[own, :] = m.yno[...]
    for moved in (shared, mixed, branch):
        moved.close()
    return cots, normed


def transposed_product(left, right, out, step):
    def part(i, _):
        columns = at(i, step)
        out[columns, :] = inner(left[:, columns], right[...]).astype(bf16)
        return 0

    lax.fori_loop(0, left.shape[1] // step, part, 0)


def half_product(left, right, tokens, step, keep, done=None):
    def part(i, _):
        rows = at(i, step)
        value = inner(left[tokens, rows], right[tokens, :])
        keep(rows, value if done is None else value + done(rows))
        return 0

    lax.fori_loop(0, left.shape[1] // step, part, 0)


def strips(refs, width):
    size = refs[0].shape[1]
    spans = [(k * size, min((k + 1) * size, width)) for k in range(-(-width // size))]

    def store(rows, value):
        for ref, (low, high) in zip(refs, spans):
            ref[rows, : high - low] = value[:, low:high].astype(bf16)

    def load(rows):
        parts = [ref[rows, : high - low].astype(f32) for ref, (low, high) in zip(refs, spans)]
        return jnp.concatenate(parts, axis=1)

    return store, load


def feed_forward(m, g, cots, normed, turns, begin):
    length, width = m.yn.shape
    block = m.y.shape[0]
    half = block // 2
    grads = Scatter(m, g, "xv", 2)
    back = Gather(
        m, g,
        lambda s: m.dyo.at[pl.ds(s * half, half), :],
        lambda j, s: m.dyf.at[pl.ds(pl.multiple_of(j * block + s * half, half), half), :],
        2, "rows",
    )
    m.need(m.wg, m.wu, m.wd)

    def lead(j):
        rows = at(j, block)
        m.dg[rows, :] = cross(m.cotf[rows, :], m.wd[...]).astype(bf16)

    def feed(j):
        rows = at(j, block)
        low = m.yn[rows, :]
        gate = plain(low, m.wg[...])
        up = plain(low, m.wu[...])
        d_act = m.dg[rows, :].astype(f32)
        sig = sigmoid(gate)
        swish = gate * sig
        m.act[rows, :] = (swish * up).astype(bf16)
        m.dg[rows, :] = (d_act * up * (sig * (1.0 + gate * (1.0 - sig)))).astype(bf16)
        m.du[rows, :] = (d_act * swish).astype(bf16)
        return cross(m.dg[rows, :], m.wg[...]) + cross(m.du[rows, :], m.wu[...])

    lead(g.me)
    m.bp[...] = feed(g.me)
    cots.near()
    normed.near()
    lead(g.sib)
    grads.fill_sib(pieces_of(feed(g.sib), 2))
    normed.forward(0)
    cots.far()
    cots.close()
    lead(g.diag)
    lead(g.opp)
    chip = 2 * block
    near = at(g.me // 2, chip)
    far = at(1 - g.me // 2, chip)
    units = m.act.shape[1]

    def keep(ref):
        def store(rows, value):
            ref[rows, :] = value.astype(bf16)

        return store

    gate_store, gate_load = strips((m.dm_od, m.dm_os, m.dm_oo), units)
    up_store, up_load = strips((m.dm_io, m.dm_iw, m.dm_if), units)
    half_product(m.yn, m.dg, near, 2 * LANES, gate_store)
    half_product(m.yn, m.du, near, 2 * LANES, up_store)
    half_product(m.act, m.cotf, near, LANES, keep(m.gd))
    normed.forward(1)
    normed.far()
    grads.put_diag(pieces_of(feed(g.diag), 2))
    m.dy[...] = feed(g.opp)
    half_product(m.act, m.cotf, far, LANES, keep(m.gd), lambda rows: m.gd[rows, :].astype(f32))
    begin(0)
    grads.send_sib()
    grads.put_opp(lambda s: m.dy[pl.ds(s * half, half), :])
    half_product(m.yn, m.dg, far, 2 * LANES, keep(m.gg), gate_load)
    half_product(m.yn, m.du, far, 2 * LANES, keep(m.gu), up_load)
    begin(1)
    turns.tick(3)
    normed.close()
    m.need(m.y, m.rs, m.cot, m.rg)
    gain_sum = jnp.zeros((1, width), f32)
    for s in range(2):
        piece = pl.ds(s * half, half)
        d_yn = grads.take(s, m.bp[piece, :])
        rms = m.rs[piece, :][:, :1]
        hat = m.y[piece, :] * rms
        gain_sum = gain_sum + jnp.sum(d_yn * hat, axis=0, keepdims=True)
        d_hat = d_yn * m.rg[...]
        pull = d_hat - hat * jnp.mean(d_hat * hat, axis=1, keepdims=True)
        dy = m.cot[piece, :].astype(f32) + rms * pull
        m.dy[piece, :] = dy
        m.dyo[piece, :] = dy.astype(bf16)
        back.send(s)
    m.gr[...] = gain_sum
    m.dyf[at(g.me, block), :] = m.dyo[...]
    grads.close()
    return back


def filter_backward(m, last, count, gamma):
    sides = m.xl.shape[0]
    tables = m.tab
    root_real, root_imag = groups(tables[0]), groups(tables[1])
    out_real, out_imag = groups(tables[2]), groups(tables[3])
    half = len(root_real)
    unroll = 8

    def chunk(step, gamma):
        ch = last - step

        def again(i, state):
            state = list(state)
            for j in range(unroll):
                local = i * unroll + j
                t = ch * SPAN + local
                keep = spread_row(m.kf, (pl.ds(t, 1), slice(None)))
                signals = [
                    spread_row(m.xl, (l, pl.ds(t, 1), slice(None))) for l in range(sides)
                ]
                kept, state = advance(state, (root_real, root_imag), keep, signals, sides)
                for g in range(2 * half):
                    m.kept[local, g] = kept[g]
            return tuple(state)

        lax.fori_loop(0, SPAN // unroll, again, tuple(m.st[ch, g] for g in range(2 * half)))

        def reverse(i, carry):
            gamma, sums = list(carry[: 2 * half]), list(carry[2 * half :])
            for j in range(unroll):
                local = SPAN - 1 - (i * unroll + j)
                t = ch * SPAN + local
                keep = spread_row(m.kf, (pl.ds(t + 1, 1), slice(None)))
                signals = [
                    spread_row(m.dq, (l, pl.ds(t, 1), slice(None))) for l in range(sides)
                ]
                _, gamma = advance(gamma, (root_real, root_imag), keep, signals, sides)
                for l in range(sides):
                    total = None
                    for g in range(l, half, sides):
                        g_real, g_imag = gamma[g], gamma[half + g]
                        a_real, a_imag = m.kept[local, g], m.kept[local, half + g]
                        term = out_real[g] * g_real - out_imag[g] * g_imag
                        total = term if total is None else total + term
                        sums[g] = sums[g] + (g_real * a_real - g_imag * a_imag)
                        sums[half + g] = sums[half + g] + (g_real * a_imag + g_imag * a_real)
                        sums[2 * half + g] = sums[2 * half + g] + signals[l] * a_real
                        sums[3 * half + g] = sums[3 * half + g] + signals[l] * a_imag
                    m.part[l, pl.ds(pl.multiple_of(local * SUB, SUB), SUB), :] = total
            return tuple(gamma) + tuple(sums)

        start = tuple(gamma) + tuple(m.acc[g] for g in range(4 * half))
        done = lax.fori_loop(0, SPAN // unroll, reverse, start)
        for g in range(4 * half):
            m.acc[g] = done[2 * half + g]
        rows = at(ch, SPAN)
        for l in range(sides):
            lanes = slice(LANES * l, LANES * l + LANES)
            signal = m.dq[l, rows, :]
            value = m.om[:, lanes] * signal
            for s in range(SUB):
                value = value + m.part[l, pl.ds(s, SPAN, stride=SUB), :]
            m.dxb[rows, lanes] = value.astype(bf16)
            m.go[:, lanes] = m.go[:, lanes] + jnp.sum(
                signal * m.xl[l, rows, :], axis=0, keepdims=True
            )
        return done[: 2 * half]

    return lax.fori_loop(0, count, chunk, gamma)


def filter_gradients(m):
    sides = m.xl.shape[0]
    half = m.acc.shape[0] // 4
    dims = m.tab.shape[1]
    for g in range(half):
        s, l = g // sides, g % sides
        rows = slice(SUB * s, SUB * s + SUB)
        lanes = slice(LANES * l, LANES * l + LANES)
        q_re, q_im, c_re, c_im, cosine, sine, alpha, delta, beta, e_re, e_im = (
            m.tab[k, rows, lanes] for k in range(11)
        )
        lag_re, lag_im, sum_re, sum_im = (m.acc[k * half + g] for k in range(4))
        f_re = q_re * sum_re - q_im * sum_im + m.go[:, lanes]
        f_im = q_re * sum_im + q_im * sum_re
        scaled = alpha * beta
        d_scaled = e_re * f_re - e_im * f_im
        w_re = c_re * lag_re - c_im * lag_im
        w_im = c_re * lag_im + c_im * lag_re
        d_mag = w_re * cosine - w_im * sine
        m.pk[0 * dims + SUB * s : 0 * dims + SUB * s + SUB, lanes] = beta * d_scaled - delta * d_mag
        m.pk[1 * dims + SUB * s : 1 * dims + SUB * s + SUB, lanes] = -alpha * d_mag
        m.pk[2 * dims + SUB * s : 2 * dims + SUB * s + SUB, lanes] = -(w_re * q_im + w_im * q_re)
        m.pk[3 * dims + SUB * s : 3 * dims + SUB * s + SUB, lanes] = alpha * d_scaled
        m.pk[4 * dims + SUB * s : 4 * dims + SUB * s + SUB, lanes] = scaled * f_re
        m.pk[5 * dims + SUB * s : 5 * dims + SUB * s + SUB, lanes] = -scaled * f_im


def backward_attention(m, g, back, turns, begin):
    length, width = m.mx.shape
    block = m.tok.shape[0]
    blocks = length // block
    half = block // 2
    channels = m.se.shape[1]
    shared = m.q.shape[1]
    sides = channels // LANES
    fed = Scatter(m, g, "xv", 2)
    pieces = 4
    dm = Scatter(m, g, "dm", pieces, range(pieces - 1, -1, -1))
    sh = Scatter(m, g, "sh", 1)
    others = (g.sib, g.opp, g.diag)
    base = m.sems(9)
    parts = [
        m.remote(m.dxb.at[at(dev, block), :], m.dxr.at[k], base, k, {"tensor": dev})
        for k, dev in enumerate(others)
    ]
    small = [
        m.remote(m.smo, m.sm.at[g.me], base, 3 + k, {"tensor": dev})
        for k, dev in enumerate(others)
    ]
    tails = [
        m.remote(m.aro, m.ar.at[:, at(g.me, block)], base, 6 + k, {"tensor": dev})
        for k, dev in enumerate(others)
    ]

    scale = 1.0 / math.sqrt(shared)
    m.dk[...] = jnp.zeros(m.dk.shape, f32)
    m.dv[...] = jnp.zeros(m.dv.shape, f32)
    turns.tick(2)
    back.forward(0)
    turns.tick(2)
    back.forward(1)
    back.near()
    back.far()
    share = lambda j: plain(m.act[at(j, block), :], m.wd[...])
    fed.put_diag(pieces_of(share(g.diag), 2))
    turns.tick()
    fed.put_opp(pieces_of(share(g.opp), 2))
    turns.tick()
    fed.put_sib(pieces_of(share(g.sib), 2))
    m.bp[...] = share(g.me)
    m.need(m.w, m.wo, m.r, m.os, m.v, m.p, m.k, m.q)
    transposed_product(m.w, m.dyf, m.gao, 2 * LANES)
    turns.tick()

    def attend(i, _):
        rows = at(i, block)
        first, keys = window_of(i, block, length)
        window = pl.ds(first, keys)
        d_w = cross(m.dyf[rows, :], m.wo[...])
        d_o = (d_w * m.r[rows, :].astype(f32)).astype(bf16)
        m.drp[rows, :] = (d_w * m.os[rows, :].astype(f32)).astype(bf16)
        prob_low = m.p[i]
        prob = prob_low.astype(f32)
        weighed = prob * cross(d_o, m.v[window, :])
        d_s = (weighed - prob * jnp.sum(weighed, axis=1, keepdims=True)) * scale
        d_s = d_s.astype(bf16)
        d_q = plain(d_s, m.k[window, :])
        for l in range(shared // LANES):
            m.dq[l, rows, :] = d_q[:, LANES * l : LANES * l + LANES]
        m.dk[window, :] = m.dk[window, :] + inner(d_s, m.q[rows, :])
        m.dv[window, :] = m.dv[window, :] + inner(prob_low, d_o)
        return 0

    for n in range(blocks):
        attend(n, 0)
        turns.tick()
    m.need(m.z, m.qg, m.kg, m.sv, m.wsf, m.wag)

    def affine(i, sums):
        rows = at(i, block)
        d_q = jnp.concatenate([m.dq[l, rows, :] for l in range(shared // LANES)], axis=1)
        d_k, z = m.dk[rows, :], m.z[rows, :].astype(f32)
        m.dz[rows, :] = (d_q * m.qg[...] + d_k * m.kg[...]).astype(bf16)
        m.dvp[rows, :] = (m.dv[rows, :] * m.sv[rows, :].astype(f32)).astype(bf16)
        new = (d_q * z, d_q, d_k * z)
        return tuple(s + jnp.sum(n, axis=0, keepdims=True) for s, n in zip(sums, new))

    aff = lax.fori_loop(0, blocks, affine, tuple(jnp.zeros((1, shared), f32) for _ in range(3)))
    m.smo[...] = jnp.zeros(m.smo.shape, f32)
    for n in range(3):
        m.smo[2 + n : 3 + n, :shared] = aff[n]

    def mixing(j):
        def value(s):
            rows = pl.ds(s * (length // pieces), length // pieces)
            return cross(m.dz[rows, :], m.wsf[at(j, channels), :]) + cross(
                m.drp[rows, :], m.wag[at(j, channels), :]
            )

        return value

    m.need(m.y)
    for s in range(2):
        piece = pl.ds(s * half, half)
        m.out[piece, :] = (fed.take(s, m.bp[piece, :]) + m.y[piece, :]).astype(bf16)
    m.flush(m.out)
    fed.close()
    turns.tick()
    m.need(m.mx, m.xn)
    transposed_product(m.mx, m.drp, m.r, 2 * LANES)
    turns.tick()
    transposed_product(m.xn, m.dvp, m.os, 2 * LANES)
    begin(2)
    dm.put_diag(mixing(g.diag))
    turns.tick()
    dm.put_opp(mixing(g.opp))
    turns.tick()
    dm.put_sib(mixing(g.sib))
    turns.tick()
    m.need(m.wv)
    xv = Scatter(m, g, "xv", 2)
    spread = lambda j: pieces_of(cross(m.dvp[at(j, block), :], m.wv[...]), 2)
    split = lambda j: (lambda s: inner(m.mx[:, at(j, channels)], m.dz[...]))

    def spreading():
        xv.put_diag(spread(g.diag))
        xv.put_opp(spread(g.opp))
        turns.tick()
        xv.put_sib(spread(g.sib))
        m.bp[...] = cross(m.dvp[at(g.me, block), :], m.wv[...])
        turns.tick()
        sh.put_diag(split(g.diag))
        sh.put_opp(split(g.opp))
        turns.tick()
        sh.put_sib(split(g.sib))
        m.shp[...] = split(g.me)(0)
        turns.tick()

    m.need(m.se, m.st, m.xl, m.kf, m.tab, m.om)
    half_states = m.acc.shape[0] // 4
    m.acc[...] = jnp.zeros(m.acc.shape, f32)
    m.go[...] = jnp.zeros(m.go.shape, f32)
    gamma = tuple(jnp.zeros((SUB, LANES), f32) for _ in range(2 * half_states))
    per = length // SPAN // pieces
    own_mix = mixing(g.me)
    for s in range(pieces - 1, -1, -1):
        rows = pl.ds(s * (length // pieces), length // pieces)
        d_e = dm.take(s, own_mix(s)) * m.se[rows, :].astype(f32)
        for l in range(sides):
            m.dq[l, rows, :] = d_e[:, LANES * l : LANES * l + LANES]
        for n in range(per - 1, -1, -2):
            gamma = filter_backward(m, s * per + n, 2, gamma)
            turns.tick()
        for k, dev in enumerate(others):

            @pl.when(dev == s)
            def _():
                parts[k].start()

        if s == pieces - 1:
            spreading()
    filter_gradients(m)
    base_row = m.pk.shape[0] - PACK_TAIL
    m.pk[base_row:, :] = jnp.zeros((PACK_TAIL, channels), f32)
    m.pk[base_row : base_row + 1, :] = m.go[...]
    m.gs[...] = sh.take(0, m.shp[...]).astype(bf16)
    turns.tick()
    m.need(m.tok, m.so, m.gain, m.dy, m.gr, m.segb, m.segr)
    for s in range(2):
        piece = pl.ds(s * half, half)
        m.bp[piece, :] = xv.take(s, m.bp[piece, :])
    own_columns = at(g.me, channels)
    m.bp[:, own_columns] = m.bp[:, own_columns] + m.dxb[at(g.me, block), :].astype(f32)
    for k, dev in enumerate(others):
        parts[k].wait_recv()
        columns = at(dev, channels)
        m.bp[:, columns] = m.bp[:, columns] + m.dxr[k].astype(f32)
    gain_sum = jnp.zeros((1, width), f32)
    lane = lax.broadcasted_iota(jnp.int32, (half, LANES), 1)
    for s in range(2):
        piece = pl.ds(s * half, half)
        mean, rstd, total = (m.so[n, piece, :][:, :1] for n in range(3))
        centred = m.tok[piece, :].astype(f32) - mean
        d_xn = m.bp[piece, :]
        gain_sum = gain_sum + jnp.sum(d_xn * (centred * rstd), axis=0, keepdims=True)
        d_hat = d_xn * m.gain[...]
        d_var = -0.5 * rstd * rstd * rstd * jnp.sum(d_hat * centred, axis=1, keepdims=True)
        one = (-rstd * jnp.sum(d_hat, axis=1, keepdims=True) - 2.0 * mean * d_var) / total
        two = d_var / total
        m.bp[piece, :] = d_hat * rstd + m.dy[piece, :]
        m.aw[piece, :] = jnp.where(lane == 0, one, jnp.where(lane == 1, two, 0.0))
    m.smo[0:1, :] = gain_sum
    m.smo[1:2, :] = m.gr[...]
    turned = m.aw[...].T
    for n in range(2):
        rest = turned[n : n + 1, :]
        for k in range(3):
            top = rest.astype(bf16).astype(f32)
            m.art[3 * n + k : 3 * n + k + 1, :] = top
            rest = rest - top
    m.art[6:8, :] = jnp.zeros((2, block), f32)
    m.art[8:16, :] = jnp.zeros((8, block), f32)
    m.aro[...] = m.art[...].astype(bf16)
    for copy in tails + small:
        copy.start()
    m.ar[:, at(g.me, block)] = m.aro[...]
    m.sm[g.me] = m.smo[...]
    reach = -(-MAX_DOC // block)
    keys = min((reach + 1) * block, length)
    first_key = pl.multiple_of(jnp.minimum(g.me * block, length - keys), LANES)
    first_row = pl.multiple_of(g.me * block, LANES)
    here = m.segb[pl.ds(pl.multiple_of(first_row + SUB, SUB), block), :][:, :1]
    same = here == m.segr[:, pl.ds(first_key, keys)].astype(f32)
    row = first_row + lax.broadcasted_iota(jnp.int32, (block, keys), 0)
    key = first_key + lax.broadcasted_iota(jnp.int32, (block, keys), 1)
    seen = (same & (row <= key)).astype(bf16)
    for copy in tails:
        copy.wait_recv()
    pulled = cross(seen, m.ar[:, pl.ds(first_key, keys)])
    b_one = pulled[:, 0:1] + pulled[:, 1:2] + pulled[:, 2:3]
    b_two = pulled[:, 3:4] + pulled[:, 4:5] + pulled[:, 5:6]
    for s in range(2):
        piece = pl.ds(s * half, half)
        rows = slice(s * half, (s + 1) * half)
        x = m.tok[piece, :].astype(f32)
        m.gt[piece, :] = (m.bp[piece, :] + b_one[rows] + 2.0 * x * b_two[rows]).astype(bf16)
    m.flush(m.gt)
    turns.tick()
    for copy in small:
        copy.wait_recv()
    total = m.sm[0]
    for j in range(1, m.sm.shape[0]):
        total = total + m.sm[j]
    per = width // channels
    for n in range(2):
        for k in range(per):
            row = base_row + 1 + n * per + k
            m.pk[row : row + 1, :] = total[n : n + 1, k * channels : (k + 1) * channels]
    for n in range(3):
        row = base_row + 1 + 2 * per + n
        m.pk[row : row + 1, :shared] = total[2 + n : 3 + n, :shared]
    begin(3)
    turns.close()
    for moved in (dm, xv, sh, back):
        moved.close()
    for copy in parts + small + tails:
        copy.wait_send()


def body(count, m):
    g = Group()
    m.load(m.tok, m.wsh, m.cot, m.segr, m.p0, m.p1, m.p2, m.p3, m.p4, m.p5)
    m.load(m.gain, m.om, m.wv, m.wag, m.qg, m.qb, m.kg, m.wo, m.rg, m.wg, m.wu, m.wd)
    m.refs.update(mean=m.dq.at[0], rstd=m.dq.at[1])
    turns = Turns()
    plans = (
        [(m.gd, m.gdb, "gdt")],
        [(m.gg, m.ggb, "ggt"), (m.gu, m.gub, "gut")],
        [(m.gao, m.gaob, "gaot"), (m.r, m.gagb, "gagt"), (m.os, m.gvb, "gvt")],
    ) if count else ()
    rings = [Ring(m, count, plan) for plan in plans]
    if count:
        rings.append(Direct(m, count, [(m.gs, m.gsb, m.gss, "gst"), (m.pk, m.pkb, m.pks, "pkt")]))
        g.greet(rings[0].neighbours())
    else:
        g.greet()

    alone = (
        ((m.gd, "gdt"),),
        ((m.gg, "ggt"), (m.gu, "gut")),
        ((m.gao, "gaot"), (m.r, "gagt"), (m.os, "gvt")),
        ((m.gs, "gst"), (m.pk, "pkt")),
    )

    def begin(n):
        if rings:
            turns.begin(rings[n])
        else:
            for ref, name in alone[n]:
                m.store(ref, name)

    cots, normed = forward_attention(m, g)
    back = feed_forward(m, g, cots, normed, turns, begin)
    backward_attention(m, g, back, turns, begin)
    m.close()


def run(arrays, sizes, count):
    length, width, block, channels, shared, values, units = sizes
    blocks = length // block
    keys = min((-(-MAX_DOC // block) + 1) * block, length)
    sides = channels // LANES
    dims = arrays.p0.shape[0]
    half_states = sides * (dims // SUB)
    late = dict(
        gao=((values, width), bf16),
        gag=((width, values), bf16),
        gv=((width, values), bf16),
        gs=((channels, shared), bf16),
        pk=((6 * dims + PACK_TAIL, channels), f32),
    )
    summed = dict(
        gd=((units, width), bf16),
        gg=((width, units), bf16),
        gu=((width, units), bf16),
        **late,
    )
    if not ring_fits(summed.values(), count):
        count = 0
    outs = dict(
        gt=((block, width), bf16),
        out=((block, width), bf16),
    )
    scratch = dict(
        xt=((length, width), bf16),
        cotf=((length, width), bf16),
        xn=((length, width), bf16),
        mx=((length, width), bf16),
        xl=((sides, length, LANES), f32),
        tab=((11, dims, channels), f32),
        kf=((length + SUB, LANES), f32),
        segb=((length + SUB, LANES), f32),
        so=((3, block, LANES), f32),
        sums=((length, LANES), bf16),
        se=((length, channels), bf16),
        st=((length // SPAN, 2 * half_states, SUB, LANES), f32),
        v=((length, values), bf16),
        sv=((length, values), bf16),
        z=((length, shared), bf16),
        q=((length, shared), bf16),
        k=((length, shared), bf16),
        wsf=((width, shared), bf16),
        p=((blocks, block, keys), bf16),
        r=((length, values), bf16),
        os=((length, values), bf16),
        w=((length, values), bf16),
        y=((block, width), f32),
        rs=((block, LANES), f32),
        yno=((block, width), bf16),
        bp=((block, width), f32),
        act=((length, units), bf16),
        dg=((length, units), bf16),
        du=((length, units), bf16),
        gd=summed["gd"],
        dy=((block, width), f32),
        gr=((1, width), f32),
        dk=((length, shared), f32),
        dv=((length, values), f32),
        dq=((max(sides, shared // LANES), length, LANES), f32),
        shp=((channels, shared), f32),
        go=((1, channels), f32),
        acc=((4 * half_states, SUB, LANES), f32),
        kept=((SPAN, 2 * half_states, SUB, LANES), f32),
        part=((sides, SPAN * SUB, LANES), f32),
        dxr=((3, block, channels), bf16),
        art=((16, block), f32),
        aro=((16, block), bf16),
        ar=((16, length), bf16),
        smo=((SUB, width), f32),
        sm=((length // block, SUB, width), f32),
        gao=late["gao"],
        gs=late["gs"],
        pk=late["pk"],
        **scatter_buffers("dm", length, channels),
        **scatter_buffers("xv", block, width),
        **scatter_buffers("sh", channels, shared),
    )
    alias = dict(yn="xt", dyf="cotf", gg="wg", gu="wu", dyo="yno", dvp="v", aw="rs")
    alias.update(dz="q", dxb="k", drp="w", mxl="dm_os")
    shared_boxes = dict(gag="dg", gv="du")
    sems = [69, 69]
    if count:
        for name, (shape, kind) in summed.items():
            small = name in ("gs", "pk")
            used = count - 1, *(ring_rows(shape, kind, count) or ())
            if name in shared_boxes and 2 * used[0] * used[1] <= length and used[2] <= units:
                alias[name + "b"] = shared_boxes[name]
                continue
            scratch[name + "b"] = (direct_box if small else ring_box)(shape, kind, count)
        scratch.update(gss=summed["gs"], pks=summed["pk"])
        sems = [69 + 12 + 4 * (count - 1), 69 + 12 * count + 4 * (count - 1)]
    bare = {name + "t": entry for name, entry in summed.items()}
    done = run_stage(
        functools.partial(body, count), arrays, outs, scratch, sems, 1, bare.items(), alias.items()
    )
    done.dims = dims
    done.summed = bool(count)
    return done


def body_f(dims, shared, m):
    wide = ((m.gd, m.gdt), (m.gg, m.ggt), (m.gu, m.gut), (m.gao, m.gaot), (m.gag, m.gagt))
    wide += ((m.gv, m.gvt), (m.gs, m.gst))
    m.load(m.out, m.gt, m.gd, m.gg, m.gu, m.gao, m.gag, m.gv, m.gs, m.pk)
    for source, target in ((m.out, m.outt), (m.gt, m.gtt)):
        m.need(source)
        target[...] = source[...]
        m.flush(target)
    for source, target in wide:
        m.need(source)
        rows = source.shape[0] // 2
        for n in range(2):

            def part(i, _):
                piece = pl.ds(pl.multiple_of(n * rows + i * 16, 16), 16)
                target[piece, :] = source[piece, :].astype(f32)
                return 0

            lax.fori_loop(0, rows // 16, part, 0, unroll=4)
        m.flush(target)
    m.need(m.pk)
    for k, out in enumerate((m.e0, m.e1, m.e2, m.e3, m.e4, m.e5)):
        out[...] = m.pk[k * dims : (k + 1) * dims, :]
    top = 6 * dims
    channels = m.pk.shape[1]
    m.om[...] = m.pk[top : top + 1, :]
    per = m.norm.shape[1] // channels
    for n, out in enumerate((m.norm, m.rms)):
        for k in range(per):
            row = top + 1 + n * per + k
            out[:, k * channels : (k + 1) * channels] = m.pk[row : row + 1, :]
    for n, out in enumerate((m.qg, m.qb, m.kg)):
        row = top + 1 + 2 * per + n
        out[...] = m.pk[row : row + 1, :shared]
    m.flush(m.e0, m.e1, m.e2, m.e3, m.e4, m.e5, m.om, m.norm, m.rms, m.qg, m.qb, m.kg)
    m.close()


def finish(c, shared):
    sums = dict(gd=c.gdt, gg=c.ggt, gu=c.gut, gao=c.gaot, gag=c.gagt, gv=c.gvt, gs=c.gst, pk=c.pkt)
    if not c.summed:
        total = lax.psum([value.astype(f32) for value in sums.values()], "dp")
        sums = {name: v.astype(old.dtype) for (name, old), v in zip(sums.items(), total)}
    channels, width = sums["pk"].shape[1], sums["gd"].shape[1]
    outs = dict(
        e0=((c.dims, channels), f32),
        e1=((c.dims, channels), f32),
        e2=((c.dims, channels), f32),
        e3=((c.dims, channels), f32),
        e4=((c.dims, channels), f32),
        e5=((c.dims, channels), f32),
        om=((1, channels), f32),
        norm=((1, width), f32),
        rms=((1, width), f32),
        qg=((1, shared), f32),
        qb=((1, shared), f32),
        kg=((1, shared), f32),
    )
    for name, value in sums.items():
        if value is not sums["pk"]:
            outs[name + "t"] = (value.shape, f32)
    outs.update(outt=(c.out.shape, bf16), gtt=(c.gt.shape, bf16))
    f = run_stage(
        functools.partial(body_f, c.dims, shared),
        types.SimpleNamespace(out=c.out, gt=c.gt, **sums), outs, {}, (0, 0), None,
    )
    tables = [table.T for table in (f.e0, f.e1, f.e2, f.e3, f.e4, f.e5)]
    return (
        f.outt, f.gtt, f.norm[0], *tables, f.om[0], f.gst,
        f.qg[0], f.qb[0], f.kg[0], f.gagt, f.gvt, f.gaot, f.rms[0], f.ggt, f.gut, f.gdt,
    )


def on_device(
    tokens,
    segments,
    cotangent,
    timestep_norm_gain,
    ema_alpha,
    ema_delta,
    ema_theta,
    ema_beta,
    eta_real,
    eta_imag,
    ema_omega,
    w_shared,
    q_gain,
    q_bias,
    k_gain,
    w_attgate,
    w_value,
    w_attout,
    rms_gain,
    w_gate,
    w_up,
    w_down,
):
    block, width = tokens.shape
    length = segments.shape[1]
    channels, dims = ema_alpha.shape
    shared = w_shared.shape[1]
    values = w_value.shape[1]
    units = w_gate.shape[1]
    om = ema_omega[None]
    gain, rg = timestep_norm_gain[None], rms_gain[None]
    qg, qb, kg = q_gain[None], q_bias[None], k_gain[None]
    segr = segments
    done = run(
        types.SimpleNamespace(
            tok=tokens, cot=cotangent, wsh=w_shared, segr=segr, gain=gain,
            p0=ema_alpha.T, p1=ema_delta.T, p2=ema_theta.T,
            p3=ema_beta.T, p4=eta_real.T, p5=eta_imag.T, om=om, qg=qg, qb=qb, kg=kg,
            wag=w_attgate, wv=w_value, wo=w_attout, rg=rg, wg=w_gate, wu=w_up, wd=w_down,
        ),
        (length, width, block, channels, shared, values, units),
        lax.axis_size("dp"),
    )
    return finish(done, shared)


def solution(mesh):
    placed = (
        P(("dp", "tensor"), None),
        P("dp", None),
        P(("dp", "tensor"), None),
        P(),
        P("tensor", None),
        P("tensor", None),
        P("tensor", None),
        P("tensor", None),
        P("tensor", None),
        P("tensor", None),
        P("tensor"),
        P("tensor", None),
        P(),
        P(),
        P(),
        P(None, "tensor"),
        P(None, "tensor"),
        P("tensor", None),
        P(),
        P(None, "tensor"),
        P(None, "tensor"),
        P("tensor", None),
    )
    return jax.shard_map(
        on_device,
        mesh=mesh,
        in_specs=placed,
        out_specs=(
            P(("dp", "tensor"), None),
            P(("dp", "tensor"), None),
            P(),
            P("tensor", None),
            P("tensor", None),
            P("tensor", None),
            P("tensor", None),
            P("tensor", None),
            P("tensor", None),
            P("tensor"),
            P("tensor", None),
            P(),
            P(),
            P(),
            P(None, "tensor"),
            P(None, "tensor"),
            P("tensor", None),
            P(),
            P(None, "tensor"),
            P(None, "tensor"),
            P("tensor", None),
        ),
        check_vma=False,
    )
```

```python
import functools
import math
import types

import jax
import jax.numpy as jnp
from jax import lax
from jax.experimental import pallas as pl
from jax.experimental.pallas import tpu as pltpu
from jax.sharding import PartitionSpec as P

epsilon = 1e-05
masked_score = -1000000000.0
f32 = jnp.float32
bf16 = jnp.bfloat16
MESH = pl.DeviceIdType.MESH
LANES = 128
SUB = 8
SPAN = 64
MAX_DOC = 512
PACK_TAIL = 32
RING_SLOTS = 4
VMEM_BYTES = 62 * 2**20


def plain(left, right):
    return jnp.dot(left, right, preferred_element_type=f32)


def cross(left, right):
    return lax.dot_general(
        left, right, (((1,), (1,)), ((), ())), preferred_element_type=f32
    )


def inner(left, right):
    return lax.dot_general(
        left, right, (((0,), (0,)), ((), ())), preferred_element_type=f32
    )


def sigmoid(value):
    return 1.0 / (1.0 + jnp.exp(-value))


def at(index, size):
    return pl.ds(pl.multiple_of(index * size, size), size)


class Stage:
    def __init__(self, ins, outs, bare, scratch, alias, refs):
        self.pending = {}
        self.flushed = []
        count = len(ins)
        self.hbm_in = dict(zip(ins, refs[:count]))
        total = len(outs) + len(bare)
        self.hbm_out = dict(zip(list(outs) + list(bare), refs[count : count + total]))
        rest = refs[count + total :]
        names = list(ins) + list(outs) + list(scratch)
        self.refs = dict(zip(names, rest[: len(names)]))
        self.load_sem, self.flush_sem, self.send_sem, self.recv_sem = rest[len(names) :]
        self.order = {name: k for k, name in enumerate(ins)}
        self.out_order = {name: k for k, name in enumerate(self.hbm_out)}
        self.sends = self.receipts = 0
        self.sets = {}
        self.names = {id(ref): name for name, ref in self.refs.items()}
        for name, other in alias:
            self.refs[name] = self.refs[other]

    def __getitem__(self, name):
        return self.refs[name]

    def __getattr__(self, name):
        return self.refs[name]

    def load(self, *refs):
        for name in [self.names[id(ref)] for ref in refs]:
            copy = pltpu.make_async_copy(
                self.hbm_in[name], self.refs[name], self.load_sem.at[self.order[name]]
            )
            copy.start()
            self.pending[name] = copy

    def need(self, *refs):
        for name in [self.names[id(ref)] for ref in refs]:
            copy = self.pending.pop(name, None)
            if copy is not None:
                copy.wait()

    def flush(self, *refs):
        for name in [self.names[id(ref)] for ref in refs]:
            if name in self.hbm_out:
                self.store(self.refs[name], name)

    def store(self, source, name):
        copy = pltpu.make_async_copy(
            source, self.hbm_out[name], self.flush_sem.at[self.out_order[name]]
        )
        copy.start()
        self.flushed.append(copy)

    def close(self):
        assert self.sends <= self.send_sem.shape[0]
        assert self.receipts <= self.recv_sem.shape[0]
        for copy in self.flushed:
            copy.wait()


    def sems(self, count, sends=None, key=None):
        if key in self.sets:
            return self.sets[key]
        first = self.sends, self.receipts
        self.sends += count if sends is None else sends
        self.receipts += count
        if key:
            self.sets[key] = first
        return first

    def remote(self, source, target_ref, base, index, device, sent=None):
        return pltpu.make_async_remote_copy(
            src_ref=source,
            dst_ref=target_ref,
            send_sem=self.send_sem.at[base[0] + (index if sent is None else sent)],
            recv_sem=self.recv_sem.at[base[1] + index],
            device_id=device,
            device_id_type=MESH,
        )


def run_stage(body, ins, outs, scratch, sems, collective, bare=(), alias=()):
    ins = vars(ins)
    written = {**outs, **dict(bare)}

    def kernel(*refs):
        body(Stage(list(ins), list(outs), list(dict(bare)), list(scratch), alias, refs))

    buffers = [pltpu.VMEM(array.shape, array.dtype) for array in ins.values()]
    buffers += [pltpu.VMEM(shape, kind) for shape, kind in outs.values()]
    buffers += [pltpu.VMEM(shape, kind) for shape, kind in scratch.values()]
    results = pl.pallas_call(
        kernel,
        out_shape=tuple(jax.ShapeDtypeStruct(shape, kind) for shape, kind in written.values()),
        in_specs=[pl.BlockSpec(memory_space=pl.ANY)] * len(ins),
        out_specs=tuple(pl.BlockSpec(memory_space=pl.ANY) for _ in written),
        scratch_shapes=buffers
        + [
            pltpu.SemaphoreType.DMA((len(ins),)),
            pltpu.SemaphoreType.DMA((len(written),)),
            pltpu.SemaphoreType.DMA((max(sems[0], 1),)),
            pltpu.SemaphoreType.DMA((max(sems[1], 1),)),
        ],
        compiler_params=pltpu.CompilerParams(
            collective_id=collective,
            has_side_effects=collective is not None,
            vmem_limit_bytes=VMEM_BYTES,
        ),
    )(*ins.values())
    return types.SimpleNamespace(**dict(zip(written, results)))


class Group:
    def __init__(self):
        self.me = lax.axis_index("tensor")
        chip = self.me // 2
        core = self.me % 2
        self.sib = chip * 2 + (1 - core)
        self.opp = (1 - chip) * 2 + core
        self.diag = (1 - chip) * 2 + (1 - core)

    def greet(self, more=()):
        barrier = pltpu.get_barrier_semaphore()
        for device in more:
            pl.semaphore_signal(barrier, inc=1, device_id={"dp": device}, device_id_type=MESH)
        for device in (self.sib, self.opp, self.diag):
            pl.semaphore_signal(barrier, inc=1, device_id={"tensor": device}, device_id_type=MESH)
        pl.semaphore_wait(barrier, 3 + len(more))


class Gather:
    def __init__(self, stage, group, source, place, pieces, key=None):
        self.g = group
        self.pieces = pieces
        base = stage.sems(3 * pieces, key=key)
        opp = {"tensor": group.opp}
        sib = {"tensor": group.sib}
        self.to_opp = [
            stage.remote(source(s), place(group.me, s), base, s, opp) for s in range(pieces)
        ]
        self.to_sib = [
            stage.remote(source(s), place(group.me, s), base, pieces + s, sib)
            for s in range(pieces)
        ]
        self.passed = [
            stage.remote(place(group.opp, s), place(group.opp, s), base, 2 * pieces + s, sib)
            for s in range(pieces)
        ]

    def send(self, s):
        self.to_opp[s].start()
        self.to_sib[s].start()

    def forward(self, s):
        self.to_opp[s].wait_recv()
        self.passed[s].start()

    def near(self):
        for s in range(self.pieces):
            self.to_sib[s].wait_recv()

    def far(self):
        for s in range(self.pieces):
            self.passed[s].wait_recv()

    def close(self):
        for copy in self.to_opp + self.to_sib + self.passed:
            copy.wait_send()


class Scatter:
    def __init__(self, stage, group, name, pieces, order=None):
        self.order = list(order or range(pieces))
        self.out_diag = stage[name + "_od"]
        self.out_sib = stage[name + "_os"]
        self.out_opp = stage[name + "_oo"]
        self.in_opp = stage[name + "_io"]
        self.in_own = stage[name + "_iw"]
        self.in_far = stage[name + "_if"]
        self.rows = self.out_diag.shape[0] // pieces
        base = stage.sems(3 * pieces, key=name)

        def copies(source, target, first, device):
            return [
                stage.remote(
                    source.at[self.part(s)], target.at[self.part(s)], base, first + s, {"tensor": device}
                )
                for s in range(pieces)
            ]

        self.first = copies(self.out_diag, self.in_opp, 0, group.sib)
        self.second = copies(self.out_sib, self.in_own, pieces, group.sib)
        self.across = copies(self.out_opp, self.in_far, 2 * pieces, group.opp)

    def part(self, s):
        return pl.ds(s * self.rows, self.rows)

    def put_diag(self, value, only=None):
        for s in self.order if only is None else [only]:
            self.out_diag[self.part(s), :] = value(s).astype(bf16)
            self.first[s].start()

    def put_opp(self, value, only=None):
        for s in self.order if only is None else [only]:
            mine = value(s)
            self.first[s].wait_recv()
            total = mine + self.in_opp[self.part(s), :].astype(f32)
            self.out_opp[self.part(s), :] = total.astype(bf16)
            self.across[s].start()

    def put_sib(self, value):
        self.fill_sib(value)
        self.send_sib()

    def fill_sib(self, value):
        for s in self.order:
            self.out_sib[self.part(s), :] = value(s).astype(bf16)

    def send_sib(self):
        for s in self.order:
            self.second[s].start()

    def take(self, s, own):
        self.second[s].wait_recv()
        near = own + self.in_own[self.part(s), :].astype(f32)
        self.across[s].wait_recv()
        return near + self.in_far[self.part(s), :].astype(f32)

    def close(self):
        for copy in self.first + self.second + self.across:
            copy.wait_send()


def pieces_of(value, count):
    rows = value.shape[0] // count
    return lambda s: value[s * rows : (s + 1) * rows]


def scatter_buffers(name, rows, width):
    return {
        name + tail: ((rows, width), bf16) for tail in ("_od", "_os", "_oo", "_io", "_iw", "_if")
    }


def ring_seats(count):
    index = lax.axis_index("dp")
    place = jnp.where(index % 2 == 0, index // 2, count - 1 - index // 2)

    def seat(p):
        p = lax.rem(p + 2 * count, count)
        return jnp.where(2 * p < count, 2 * p, 2 * (count - 1 - p) + 1)

    return place, seat


def ring_rows(shape, kind, count):
    tile = 16 if kind == bf16 else SUB
    if shape[0] % (2 * count * tile) == 0:
        return shape[0] // (2 * count), shape[1]
    if shape[0] % (count * tile) == 0 and shape[1] % (2 * LANES) == 0:
        return shape[0] // count, shape[1] // 2
    return None


class Ring:
    def __init__(self, m, count, items):
        self.m = m
        self.count = count
        self.items = items
        self.place, self.seat = ring_seats(count)
        self.steps = 2 * (count - 1)
        self.ahead = self.pause = 0
        self.base = m.sems(len(items) * 2 * RING_SLOTS, len(items) * 2)
        self.step = 0

    def neighbours(self):
        return self.seat(self.place - 1), self.seat(self.place + 1)

    def view(self, ref, chunk, way):
        shape = ref.shape
        rows, columns = ring_rows(shape, ref.dtype, self.count)
        chunk = lax.rem(chunk + 2 * self.count, self.count)
        if columns == shape[1]:
            return ref.at[pl.ds(pl.multiple_of((2 * chunk + way) * rows, rows), rows), :]
        return ref.at[
            pl.ds(pl.multiple_of(chunk * rows, rows), rows), pl.ds(way * columns, columns)
        ]

    def slot(self, item, way, step):
        own, box, _ = self.items[item]
        if len(box.shape) == 4:
            return box.at[way, step]
        rows, columns = ring_rows(own.shape, own.dtype, self.count)
        first = (way * (self.count - 1) + step) * rows
        return box.at[pl.ds(first, rows), pl.ds(0, columns)]

    def copy(self, item, way, step):
        own = self.items[item][0]
        sign = 1 - 2 * way
        last = self.count - 1
        place = 2 * item + way
        index = place * RING_SLOTS + step % RING_SLOTS
        if step < last:
            source = self.view(own, self.place, way) if step == 0 else self.slot(item, way, step - 1)
            target = self.slot(item, way, step)
        else:
            source = self.view(own, self.place + sign - sign * (step - last), way)
            target = source
        device = {"dp": self.seat(self.place + sign)}
        return self.m.remote(source, target, self.base, index, device, place)

    def start(self, item, way, step):
        self.copy(item, way, step).start()

    def begin(self):
        for item in range(len(self.items)):
            for way in range(2):
                self.start(item, way, 0)

    def tick(self):
        last = self.count - 1
        step = self.step
        self.step = step + 1
        for item, (own, _, name) in enumerate(self.items):
            for way in range(2):
                sign = 1 - 2 * way
                self.copy(item, way, step).wait_recv()
                self.copy(item, way, step).wait_send()
                if step < last:
                    chunk = self.view(own, self.place - sign * (step + 1), way)
                    box = self.slot(item, way, step)
                    value = box[...].astype(f32) + chunk[...].astype(f32)
                    if step < last - 1:
                        box[...] = value.astype(own.dtype)
                    else:
                        chunk[...] = value.astype(own.dtype)
                if step + 1 < self.steps:
                    self.start(item, way, step + 1)
                if step >= last - 1:
                    self.keep(own, name, self.place + sign - sign * (step + 1 - last), way)
        return step + 1 == self.steps

    def keep(self, own, name, chunk, way):
        out = self.m.hbm_out[name]
        sem = self.m.flush_sem.at[self.m.out_order[name]]
        pltpu.make_async_copy(self.view(own, chunk, way), self.view(out, chunk, way), sem).start()

    def close(self):
        for own, _, name in self.items:
            sem = self.m.flush_sem.at[self.m.out_order[name]]
            pltpu.make_async_copy(own, self.m.hbm_out[name], sem).wait()


class Direct:
    def __init__(self, m, count, items):
        self.m = m
        self.count = count
        self.items = items
        self.me = lax.axis_index("dp")
        self.base = m.sems(2 * len(items) * (count - 1))
        self.step = 0
        self.steps = 2
        self.ahead = 2 * count
        self.pause = 3

    def share(self, ref, index):
        return ref.at[at(index, ref.shape[0] // self.count), :]

    def copies(self, step):
        made = []
        for item, (own, box, total, _) in enumerate(self.items):
            for r in range(1, self.count):
                there = lax.rem(self.me + r, self.count)
                index = (2 * item + step) * (self.count - 1) + r - 1
                if step == 0:
                    source, target = self.share(own, there), box.at[r - 1]
                else:
                    source = target = self.share(total, self.me)
                made.append(self.m.remote(source, target, self.base, index, {"dp": there}))
        return made

    def begin(self):
        for copy in self.copies(0):
            copy.start()

    def tick(self):
        for copy in self.copies(self.step):
            copy.wait_recv()
        if self.step == 0:
            for own, box, total, _ in self.items:
                value = self.share(own, self.me)[...].astype(f32)
                for r in range(self.count - 1):
                    value = value + box[r].astype(f32)
                self.share(total, self.me)[...] = value.astype(total.dtype)
            for copy in self.copies(1):
                copy.start()
        self.step += 1
        return self.step == 2

    def close(self):
        for copy in self.copies(0) + self.copies(1):
            copy.wait_send()
        for _, _, total, name in self.items:
            self.m.store(total, name)


class Turns:
    def __init__(self):
        self.waiting = []
        self.rings = []
        self.recent = []

    def begin(self, ring):
        ring.begin()
        self.waiting.append(ring)
        self.rings.append(ring)
        self.recent.append(ring)

    def tick(self, times=1):
        for _ in range(times):
            if self.waiting:
                others = [one for one in self.waiting if one not in self.recent[-1 - one.pause :]]
                others = others or [one for one in self.waiting if not one.pause] or self.waiting
                ring = max(others, key=lambda one: one.ahead + one.steps - one.step)
                self.recent.append(ring)
                if ring.tick():
                    self.waiting.remove(ring)

    def close(self):
        while self.waiting:
            self.tick()
        for ring in self.rings:
            ring.close()


def ring_box(shape, kind, count):
    rows, columns = ring_rows(shape, kind, count)
    return ((2, count - 1, rows, columns), kind)


def direct_box(shape, kind, count):
    return ((count - 1, shape[0] // count, shape[1]), kind)


def ring_fits(shapes, count):
    return (
        count > 1
        and count % 2 == 0
        and all(ring_rows(shape, kind, count) for shape, kind in shapes)
    )


def groups(array):
    halves = array.shape[0] // SUB
    sides = array.shape[1] // LANES
    return [
        array[SUB * s : SUB * s + SUB, LANES * l : LANES * l + LANES]
        for s in range(halves)
        for l in range(sides)
    ]


def spread_row(ref, index):
    return jnp.broadcast_to(ref[index], (SUB, LANES))


def advance(state, coefs, keep, signals, sides):
    root_real, root_imag = coefs
    half = len(state) // 2
    kept = [value * keep for value in state]
    fresh = [None] * len(state)
    for g in range(half):
        a_real, a_imag = kept[g], kept[half + g]
        fresh[g] = (root_real[g] * a_real - root_imag[g] * a_imag) + signals[g % sides]
        fresh[half + g] = root_real[g] * a_imag + root_imag[g] * a_real
    return kept, fresh


def filter_forward(m, first, count, state):
    sides = m.xl.shape[0]
    tables = m.tab
    root_real, root_imag = groups(tables[0]), groups(tables[1])
    out_real, out_imag = groups(tables[2]), groups(tables[3])
    half = len(root_real)
    unroll = 16

    def chunk(ch, state):
        for g in range(2 * half):
            m.st[ch, g] = state[g]

        def steps(i, state):
            state = list(state)
            for j in range(unroll):
                t = ch * SPAN + i * unroll + j
                keep = spread_row(m.kf, (pl.ds(t, 1), slice(None)))
                signals = [
                    spread_row(m.xl, (l, pl.ds(t, 1), slice(None))) for l in range(sides)
                ]
                _, state = advance(state, (root_real, root_imag), keep, signals, sides)
                for l in range(sides):
                    total = None
                    for g in range(l, half, sides):
                        term = out_real[g] * state[g] - out_imag[g] * state[half + g]
                        total = term if total is None else total + term
                    m.part[l, pl.ds(pl.multiple_of((i * unroll + j) * SUB, SUB), SUB), :] = total
            return tuple(state)

        state = lax.fori_loop(0, SPAN // unroll, steps, state)
        rows = at(ch, SPAN)
        for l in range(sides):
            lanes = slice(LANES * l, LANES * l + LANES)
            value = m.om[:, lanes] * m.xl[l, rows, :]
            for s in range(SUB):
                value = value + m.part[l, pl.ds(s, SPAN, stride=SUB), :]
            gate = sigmoid(value)
            m.mxl[rows, lanes] = (value * gate).astype(bf16)
            m.se[rows, lanes] = (gate * (1.0 + value * (1.0 - gate))).astype(bf16)
        return state

    return lax.fori_loop(first, first + count, chunk, state)


def window_mask(m, first_row, rows, first_key, keys):
    here = m.segb[pl.ds(pl.multiple_of(first_row + SUB, SUB), rows), :][:, :1]
    same = here == m.segr[:, pl.ds(pl.multiple_of(first_key, LANES), keys)].astype(f32)
    row = first_row + lax.broadcasted_iota(jnp.int32, (rows, keys), 0)
    key = first_key + lax.broadcasted_iota(jnp.int32, (rows, keys), 1)
    return same & (row >= key)


def window_of(index, block, length):
    back = -(-MAX_DOC // block)
    keys = min((back + 1) * block, length)
    first = jnp.maximum(index - back, 0) * block
    first = jnp.minimum(first, length - keys)
    return pl.multiple_of(first, LANES), keys


def keeping(m):
    length = m.segr.shape[1]
    m.segb[:SUB, :] = jnp.full((SUB, LANES), -1.0, f32)
    for k in range(length // LANES):
        row = m.segr[:, k * LANES : (k + 1) * LANES].astype(f32)
        m.segb[SUB + k * LANES : SUB + (k + 1) * LANES, :] = jnp.broadcast_to(row, (LANES, LANES)).T
    for k in range(length // LANES):
        now = m.segb[SUB + k * LANES : SUB + (k + 1) * LANES, :]
        before = m.segb[SUB - 1 + k * LANES : SUB - 1 + (k + 1) * LANES, :]
        m.kf[k * LANES : (k + 1) * LANES, :] = jnp.where(now == before, 1.0, 0.0)
    m.kf[length:, :] = jnp.zeros((SUB, LANES), f32)


def filter_tables(m):
    alpha, delta, theta, beta, e_re, e_im = (
        ref[...] for ref in (m.p0, m.p1, m.p2, m.p3, m.p4, m.p5)
    )
    magnitude = 1.0 - alpha * delta
    cosine, sine = jnp.cos(theta), jnp.sin(theta)
    scaled = alpha * beta
    entries = (
        magnitude * cosine, magnitude * sine, scaled * e_re, scaled * e_im,
        cosine, sine, alpha, delta, beta, e_re, e_im,
    )
    for k, entry in enumerate(entries):
        m.tab[k] = entry


def forward_attention(m, g):
    length, width = m.xt.shape
    block = m.tok.shape[0]
    blocks = length // block
    channels = m.mxl.shape[1]
    sides = channels // LANES
    own = at(g.me, block)
    half = block // 2
    tokens = Gather(
        m, g,
        lambda s: m.tok.at[pl.ds(s * half, half), :],
        lambda j, s: m.xt.at[pl.ds(pl.multiple_of(j * block + s * half, half), half), :],
        2, "rows",
    )
    shared = Gather(m, g, lambda s: m.wsh, lambda j, s: m.wsf.at[at(j, channels), :], 1)
    pieces = 8
    rows_piece = length // pieces
    mixed = Gather(
        m, g,
        lambda s: m.mxl.at[pl.ds(s * rows_piece, rows_piece), :],
        lambda j, s: m.mx.at[pl.ds(s * rows_piece, rows_piece), at(j, channels)],
        pieces,
    )
    cots = Gather(
        m, g,
        lambda s: m.cot.at[pl.ds(s * half, half), :],
        lambda j, s: m.cotf.at[pl.ds(pl.multiple_of(j * block + s * half, half), half), :],
        2,
    )
    normed = Gather(
        m, g,
        lambda s: m.yno.at[pl.ds(s * half, half), :],
        lambda j, s: m.yn.at[pl.ds(pl.multiple_of(j * block + s * half, half), half), :],
        2, "rows",
    )
    branch = Scatter(m, g, "xv", 2)

    m.need(m.tok, m.wsh)
    tokens.send(0)
    tokens.send(1)
    shared.send(0)
    m.need(m.cot)
    cots.send(0)
    m.xt[own, :] = m.tok[...]
    m.wsf[at(g.me, channels), :] = m.wsh[...]
    m.need(m.segr, m.p0, m.p1, m.p2, m.p3, m.p4, m.p5, m.gain, m.om)
    keeping(m)
    filter_tables(m)

    lane = lax.broadcasted_iota(jnp.int32, (SPAN, LANES), 1)

    def sums(j):
        def part(i, _):
            rows = pl.ds(pl.multiple_of(j * block + i * SPAN, SPAN), SPAN)
            one = jnp.zeros((SPAN, LANES), f32)
            two = jnp.zeros((SPAN, LANES), f32)
            for l in range(width // LANES):
                x = m.xt[rows, LANES * l : LANES * l + LANES].astype(f32)
                one = one + x
                two = two + x * x
            picked = jnp.where(lane == 6, 1.0, 0.0)
            for k, total in ((0, one), (3, two)):
                rest = jnp.sum(total, axis=1, keepdims=True)
                for n in range(3):
                    top = rest.astype(bf16).astype(f32)
                    picked = jnp.where(lane == k + n, top, picked)
                    rest = rest - top
            m.sums[rows, :] = picked.astype(bf16)
            return 0

        lax.fori_loop(0, block // SPAN, part, 0)

    sums(g.me)
    tokens.near()
    sums(g.sib)
    tokens.forward(0)
    tokens.forward(1)
    sums(g.opp)
    tokens.far()
    sums(g.diag)

    lane_wide = lax.broadcasted_iota(jnp.int32, (block, LANES), 1)

    def statistics(i, _):
        first, keys = window_of(i, block, length)
        seen = window_mask(m, i * block, block, first, keys).astype(bf16)
        got = plain(seen, m.sums[pl.ds(first, keys), :])
        pick = lambda low, high: jnp.sum(
            jnp.where((lane_wide >= low) & (lane_wide < high), got, 0.0), axis=1, keepdims=True
        )
        total = pick(6, 7) * width
        mean = pick(0, 3) / total
        var = pick(3, 6) / total - mean * mean
        rows = at(i, block)
        m.mean[rows, :] = jnp.broadcast_to(mean, (block, LANES))
        m.rstd[rows, :] = jnp.broadcast_to(lax.rsqrt(var + epsilon), (block, LANES))

        @pl.when(i == g.me)
        def _():
            m.so[0] = m.mean[rows, :]
            m.so[1] = m.rstd[rows, :]
            m.so[2] = jnp.broadcast_to(total, (block, LANES))

        return 0

    lax.fori_loop(0, blocks, statistics, 0)

    def normalise(i, _):
        rows = at(i, SPAN)
        mean, rstd = m.mean[rows, :], m.rstd[rows, :]
        for l in range(width // LANES):
            lanes = slice(LANES * l, LANES * l + LANES)
            x = m.xt[rows, lanes].astype(f32)
            m.xn[rows, lanes] = ((x - mean) * rstd * m.gain[:, lanes]).astype(bf16)
        for l in range(sides):
            lanes = pl.ds(pl.multiple_of(g.me * channels + LANES * l, LANES), LANES)
            x = m.xt[rows, lanes].astype(f32)
            m.xl[l, rows, :] = (x - mean) * rstd * m.gain[:, lanes]
        return 0

    lax.fori_loop(0, length // SPAN, normalise, 0)
    tokens.close()

    zero = jnp.zeros((SUB, LANES), f32)
    state = tuple(zero for _ in range(m.st.shape[1]))
    per = length // SPAN // pieces
    for p in range(pieces):
        state = filter_forward(m, p * per, per, state)
        mixed.send(p)
        if p >= 2:
            mixed.forward(p - 2)
    cots.send(1)
    for i in range(pieces):
        m.mx[pl.ds(i * rows_piece, rows_piece), at(g.me, channels)] = m.mxl[
            pl.ds(i * rows_piece, rows_piece), :
        ]
    m.cotf[own, :] = m.cot[...]
    m.need(m.wv)

    def values(i, _):
        rows = at(i, block)
        pre = plain(m.xn[rows, :], m.wv[...])
        gate = sigmoid(pre)
        m.v[rows, :] = (pre * gate).astype(bf16)
        m.sv[rows, :] = (gate * (1.0 + pre * (1.0 - gate))).astype(bf16)
        return 0

    lax.fori_loop(0, blocks, values, 0)
    for p in range(max(pieces - 2, 0), pieces):
        mixed.forward(p)
    shared.forward(0)
    shared.near()
    shared.far()
    mixed.near()
    mixed.far()
    m.need(m.qg, m.qb, m.kg, m.wag, m.wo, m.rg)

    def project(i, _):
        rows = at(i, block)
        z = plain(m.mx[rows, :], m.wsf[...])
        m.z[rows, :] = z.astype(bf16)
        m.q[rows, :] = (z * m.qg[...] + m.qb[...]).astype(bf16)
        m.k[rows, :] = (z * m.kg[...]).astype(bf16)
        return 0

    lax.fori_loop(0, blocks, project, 0)
    scale = 1.0 / math.sqrt(m.q.shape[1])

    def attend(i, part, count):
        size = block // count
        start = pl.multiple_of(i * block + part * size, size)
        rows = pl.ds(start, size)
        first, keys = window_of(i, block, length)
        window = pl.ds(first, keys)
        scores = cross(m.q[rows, :], m.k[window, :]) * scale
        scores = jnp.where(window_mask(m, start, size, first, keys), scores, masked_score)
        expo = jnp.exp(scores - jnp.max(scores, axis=1, keepdims=True))
        prob = (expo / jnp.sum(expo, axis=1, keepdims=True)).astype(bf16)
        m.p[i, pl.ds(part * size, size), :] = prob
        attended = plain(prob, m.v[window, :])
        pre = plain(m.mx[rows, :], m.wag[...])
        gate = sigmoid(pre)
        swish = pre * gate
        m.r[rows, :] = swish.astype(bf16)
        m.os[rows, :] = (attended * (gate * (1.0 + pre * (1.0 - gate)))).astype(bf16)
        m.w[rows, :] = (attended * swish).astype(bf16)
        return plain(m.w[rows, :], m.wo[...])

    for n in range(2):
        branch.put_diag(lambda s: attend(g.diag, s, 2), n)
        branch.put_opp(lambda s: attend(g.opp, s, 2), n)
    cots.forward(0)
    branch.put_sib(pieces_of(attend(g.sib, 0, 1), 2))
    cots.forward(1)
    m.bp[...] = attend(g.me, 0, 1)
    for s in range(2):
        piece = pl.ds(s * half, half)
        y = branch.take(s, m.bp[piece, :]) + m.tok[piece, :].astype(f32)
        m.y[piece, :] = y
        rms = lax.rsqrt(jnp.mean(y * y, axis=1, keepdims=True) + epsilon)
        m.rs[piece, :] = jnp.broadcast_to(rms, (half, LANES))
        m.yno[piece, :] = (y * rms * m.rg[...]).astype(bf16)
        normed.send(s)
    m.yn[own, :] = m.yno[...]
    for moved in (shared, mixed, branch):
        moved.close()
    return cots, normed


def transposed_product(left, right, out, step):
    def part(i, _):
        columns = at(i, step)
        out[columns, :] = inner(left[:, columns], right[...]).astype(bf16)
        return 0

    lax.fori_loop(0, left.shape[1] // step, part, 0)


def half_product(left, right, tokens, step, keep, done=None):
    def part(i, _):
        rows = at(i, step)
        value = inner(left[tokens, rows], right[tokens, :])
        keep(rows, value if done is None else value + done(rows))
        return 0

    lax.fori_loop(0, left.shape[1] // step, part, 0)


def strips(refs, width):
    size = refs[0].shape[1]
    spans = [(k * size, min((k + 1) * size, width)) for k in range(-(-width // size))]

    def store(rows, value):
        for ref, (low, high) in zip(refs, spans):
            ref[rows, : high - low] = value[:, low:high].astype(bf16)

    def load(rows):
        parts = [ref[rows, : high - low].astype(f32) for ref, (low, high) in zip(refs, spans)]
        return jnp.concatenate(parts, axis=1)

    return store, load


def feed_forward(m, g, cots, normed, turns, begin):
    length, width = m.yn.shape
    block = m.y.shape[0]
    half = block // 2
    grads = Scatter(m, g, "xv", 2)
    back = Gather(
        m, g,
        lambda s: m.dyo.at[pl.ds(s * half, half), :],
        lambda j, s: m.dyf.at[pl.ds(pl.multiple_of(j * block + s * half, half), half), :],
        2, "rows",
    )
    m.need(m.wg, m.wu, m.wd)

    def lead(j):
        rows = at(j, block)
        m.dg[rows, :] = cross(m.cotf[rows, :], m.wd[...]).astype(bf16)

    def feed(j):
        rows = at(j, block)
        low = m.yn[rows, :]
        gate = plain(low, m.wg[...])
        up = plain(low, m.wu[...])
        d_act = m.dg[rows, :].astype(f32)
        sig = sigmoid(gate)
        swish = gate * sig
        m.act[rows, :] = (swish * up).astype(bf16)
        m.dg[rows, :] = (d_act * up * (sig * (1.0 + gate * (1.0 - sig)))).astype(bf16)
        m.du[rows, :] = (d_act * swish).astype(bf16)
        return cross(m.dg[rows, :], m.wg[...]) + cross(m.du[rows, :], m.wu[...])

    lead(g.me)
    m.bp[...] = feed(g.me)
    cots.near()
    normed.near()
    lead(g.sib)
    grads.fill_sib(pieces_of(feed(g.sib), 2))
    normed.forward(0)
    cots.far()
    cots.close()
    lead(g.diag)
    lead(g.opp)
    chip = 2 * block
    near = at(g.me // 2, chip)
    far = at(1 - g.me // 2, chip)
    units = m.act.shape[1]

    def keep(ref):
        def store(rows, value):
            ref[rows, :] = value.astype(bf16)

        return store

    gate_store, gate_load = strips((m.dm_od, m.dm_os, m.dm_oo), units)
    up_store, up_load = strips((m.dm_io, m.dm_iw, m.dm_if), units)
    half_product(m.yn, m.dg, near, 2 * LANES, gate_store)
    half_product(m.yn, m.du, near, 2 * LANES, up_store)
    half_product(m.act, m.cotf, near, LANES, keep(m.gd))
    normed.forward(1)
    normed.far()
    grads.put_diag(pieces_of(feed(g.diag), 2))
    m.dy[...] = feed(g.opp)
    half_product(m.act, m.cotf, far, LANES, keep(m.gd), lambda rows: m.gd[rows, :].astype(f32))
    begin(0)
    grads.send_sib()
    grads.put_opp(lambda s: m.dy[pl.ds(s * half, half), :])
    half_product(m.yn, m.dg, far, 2 * LANES, keep(m.gg), gate_load)
    half_product(m.yn, m.du, far, 2 * LANES, keep(m.gu), up_load)
    begin(1)
    turns.tick(3)
    normed.close()
    m.need(m.y, m.rs, m.cot, m.rg)
    gain_sum = jnp.zeros((1, width), f32)
    for s in range(2):
        piece = pl.ds(s * half, half)
        d_yn = grads.take(s, m.bp[piece, :])
        rms = m.rs[piece, :][:, :1]
        hat = m.y[piece, :] * rms
        gain_sum = gain_sum + jnp.sum(d_yn * hat, axis=0, keepdims=True)
        d_hat = d_yn * m.rg[...]
        pull = d_hat - hat * jnp.mean(d_hat * hat, axis=1, keepdims=True)
        dy = m.cot[piece, :].astype(f32) + rms * pull
        m.dy[piece, :] = dy
        m.dyo[piece, :] = dy.astype(bf16)
        back.send(s)
    m.gr[...] = gain_sum
    m.dyf[at(g.me, block), :] = m.dyo[...]
    grads.close()
    return back


def filter_backward(m, last, count, gamma):
    sides = m.xl.shape[0]
    tables = m.tab
    root_real, root_imag = groups(tables[0]), groups(tables[1])
    out_real, out_imag = groups(tables[2]), groups(tables[3])
    half = len(root_real)
    unroll = 8

    def chunk(step, gamma):
        ch = last - step

        def again(i, state):
            state = list(state)
            for j in range(unroll):
                local = i * unroll + j
                t = ch * SPAN + local
                keep = spread_row(m.kf, (pl.ds(t, 1), slice(None)))
                signals = [
                    spread_row(m.xl, (l, pl.ds(t, 1), slice(None))) for l in range(sides)
                ]
                kept, state = advance(state, (root_real, root_imag), keep, signals, sides)
                for g in range(2 * half):
                    m.kept[local, g] = kept[g]
            return tuple(state)

        lax.fori_loop(0, SPAN // unroll, again, tuple(m.st[ch, g] for g in range(2 * half)))

        def reverse(i, carry):
            gamma, sums = list(carry[: 2 * half]), list(carry[2 * half :])
            for j in range(unroll):
                local = SPAN - 1 - (i * unroll + j)
                t = ch * SPAN + local
                keep = spread_row(m.kf, (pl.ds(t + 1, 1), slice(None)))
                signals = [
                    spread_row(m.dq, (l, pl.ds(t, 1), slice(None))) for l in range(sides)
                ]
                _, gamma = advance(gamma, (root_real, root_imag), keep, signals, sides)
                for l in range(sides):
                    total = None
                    for g in range(l, half, sides):
                        g_real, g_imag = gamma[g], gamma[half + g]
                        a_real, a_imag = m.kept[local, g], m.kept[local, half + g]
                        term = out_real[g] * g_real - out_imag[g] * g_imag
                        total = term if total is None else total + term
                        sums[g] = sums[g] + (g_real * a_real - g_imag * a_imag)
                        sums[half + g] = sums[half + g] + (g_real * a_imag + g_imag * a_real)
                        sums[2 * half + g] = sums[2 * half + g] + signals[l] * a_real
                        sums[3 * half + g] = sums[3 * half + g] + signals[l] * a_imag
                    m.part[l, pl.ds(pl.multiple_of(local * SUB, SUB), SUB), :] = total
            return tuple(gamma) + tuple(sums)

        start = tuple(gamma) + tuple(m.acc[g] for g in range(4 * half))
        done = lax.fori_loop(0, SPAN // unroll, reverse, start)
        for g in range(4 * half):
            m.acc[g] = done[2 * half + g]
        rows = at(ch, SPAN)
        for l in range(sides):
            lanes = slice(LANES * l, LANES * l + LANES)
            signal = m.dq[l, rows, :]
            value = m.om[:, lanes] * signal
            for s in range(SUB):
                value = value + m.part[l, pl.ds(s, SPAN, stride=SUB), :]
            m.dxb[rows, lanes] = value.astype(bf16)
            m.go[:, lanes] = m.go[:, lanes] + jnp.sum(
                signal * m.xl[l, rows, :], axis=0, keepdims=True
            )
        return done[: 2 * half]

    return lax.fori_loop(0, count, chunk, gamma)


def filter_gradients(m):
    sides = m.xl.shape[0]
    half = m.acc.shape[0] // 4
    dims = m.tab.shape[1]
    for g in range(half):
        s, l = g // sides, g % sides
        rows = slice(SUB * s, SUB * s + SUB)
        lanes = slice(LANES * l, LANES * l + LANES)
        q_re, q_im, c_re, c_im, cosine, sine, alpha, delta, beta, e_re, e_im = (
            m.tab[k, rows, lanes] for k in range(11)
        )
        lag_re, lag_im, sum_re, sum_im = (m.acc[k * half + g] for k in range(4))
        f_re = q_re * sum_re - q_im * sum_im + m.go[:, lanes]
        f_im = q_re * sum_im + q_im * sum_re
        scaled = alpha * beta
        d_scaled = e_re * f_re - e_im * f_im
        w_re = c_re * lag_re - c_im * lag_im
        w_im = c_re * lag_im + c_im * lag_re
        d_mag = w_re * cosine - w_im * sine
        m.pk[0 * dims + SUB * s : 0 * dims + SUB * s + SUB, lanes] = beta * d_scaled - delta * d_mag
        m.pk[1 * dims + SUB * s : 1 * dims + SUB * s + SUB, lanes] = -alpha * d_mag
        m.pk[2 * dims + SUB * s : 2 * dims + SUB * s + SUB, lanes] = -(w_re * q_im + w_im * q_re)
        m.pk[3 * dims + SUB * s : 3 * dims + SUB * s + SUB, lanes] = alpha * d_scaled
        m.pk[4 * dims + SUB * s : 4 * dims + SUB * s + SUB, lanes] = scaled * f_re
        m.pk[5 * dims + SUB * s : 5 * dims + SUB * s + SUB, lanes] = -scaled * f_im


def backward_attention(m, g, back, turns, begin):
    length, width = m.mx.shape
    block = m.tok.shape[0]
    blocks = length // block
    half = block // 2
    channels = m.se.shape[1]
    shared = m.q.shape[1]
    sides = channels // LANES
    fed = Scatter(m, g, "xv", 2)
    pieces = 4
    dm = Scatter(m, g, "dm", pieces, range(pieces - 1, -1, -1))
    sh = Scatter(m, g, "sh", 1)
    others = (g.sib, g.opp, g.diag)
    base = m.sems(9)
    parts = [
        m.remote(m.dxb.at[at(dev, block), :], m.dxr.at[k], base, k, {"tensor": dev})
        for k, dev in enumerate(others)
    ]
    small = [
        m.remote(m.smo, m.sm.at[g.me], base, 3 + k, {"tensor": dev})
        for k, dev in enumerate(others)
    ]
    tails = [
        m.remote(m.aro, m.ar.at[:, at(g.me, block)], base, 6 + k, {"tensor": dev})
        for k, dev in enumerate(others)
    ]

    scale = 1.0 / math.sqrt(shared)
    m.dk[...] = jnp.zeros(m.dk.shape, f32)
    m.dv[...] = jnp.zeros(m.dv.shape, f32)
    turns.tick(3)
    back.forward(0)
    turns.tick(2)
    back.forward(1)
    back.near()
    back.far()
    share = lambda j: plain(m.act[at(j, block), :], m.wd[...])
    fed.put_diag(pieces_of(share(g.diag), 2))
    turns.tick()
    fed.put_opp(pieces_of(share(g.opp), 2))
    turns.tick()
    fed.put_sib(pieces_of(share(g.sib), 2))
    m.bp[...] = share(g.me)
    m.need(m.w, m.wo, m.r, m.os, m.v, m.p, m.k, m.q)
    transposed_product(m.w, m.dyf, m.gao, 2 * LANES)
    turns.tick()

    def attend(i, _):
        rows = at(i, block)
        first, keys = window_of(i, block, length)
        window = pl.ds(first, keys)
        d_w = cross(m.dyf[rows, :], m.wo[...])
        d_o = (d_w * m.r[rows, :].astype(f32)).astype(bf16)
        m.drp[rows, :] = (d_w * m.os[rows, :].astype(f32)).astype(bf16)
        prob_low = m.p[i]
        prob = prob_low.astype(f32)
        weighed = prob * cross(d_o, m.v[window, :])
        d_s = (weighed - prob * jnp.sum(weighed, axis=1, keepdims=True)) * scale
        d_s = d_s.astype(bf16)
        d_q = plain(d_s, m.k[window, :])
        for l in range(shared // LANES):
            m.dq[l, rows, :] = d_q[:, LANES * l : LANES * l + LANES]
        m.dk[window, :] = m.dk[window, :] + inner(d_s, m.q[rows, :])
        m.dv[window, :] = m.dv[window, :] + inner(prob_low, d_o)
        return 0

    for n in range(blocks):
        attend(n, 0)
        turns.tick()
    m.need(m.z, m.qg, m.kg, m.sv, m.wsf, m.wag)

    def affine(i, sums):
        rows = at(i, block)
        d_q = jnp.concatenate([m.dq[l, rows, :] for l in range(shared // LANES)], axis=1)
        d_k, z = m.dk[rows, :], m.z[rows, :].astype(f32)
        m.dz[rows, :] = (d_q * m.qg[...] + d_k * m.kg[...]).astype(bf16)
        m.dvp[rows, :] = (m.dv[rows, :] * m.sv[rows, :].astype(f32)).astype(bf16)
        new = (d_q * z, d_q, d_k * z)
        return tuple(s + jnp.sum(n, axis=0, keepdims=True) for s, n in zip(sums, new))

    aff = lax.fori_loop(0, blocks, affine, tuple(jnp.zeros((1, shared), f32) for _ in range(3)))
    m.smo[...] = jnp.zeros(m.smo.shape, f32)
    for n in range(3):
        m.smo[2 + n : 3 + n, :shared] = aff[n]

    def mixing(j):
        def value(s):
            rows = pl.ds(s * (length // pieces), length // pieces)
            return cross(m.dz[rows, :], m.wsf[at(j, channels), :]) + cross(
                m.drp[rows, :], m.wag[at(j, channels), :]
            )

        return value

    m.need(m.y)
    for s in range(2):
        piece = pl.ds(s * half, half)
        m.out[piece, :] = (fed.take(s, m.bp[piece, :]) + m.y[piece, :]).astype(bf16)
    m.flush(m.out)
    fed.close()
    turns.tick()
    m.need(m.mx, m.xn)
    transposed_product(m.mx, m.drp, m.r, 2 * LANES)
    turns.tick()
    transposed_product(m.xn, m.dvp, m.os, 2 * LANES)
    begin(2)
    dm.put_diag(mixing(g.diag))
    turns.tick()
    dm.put_opp(mixing(g.opp))
    turns.tick()
    dm.put_sib(mixing(g.sib))
    turns.tick()
    m.need(m.wv)
    xv = Scatter(m, g, "xv", 2)
    spread = lambda j: pieces_of(cross(m.dvp[at(j, block), :], m.wv[...]), 2)
    split = lambda j: (lambda s: inner(m.mx[:, at(j, channels)], m.dz[...]))

    def spreading():
        xv.put_diag(spread(g.diag))
        xv.put_opp(spread(g.opp))
        turns.tick()
        xv.put_sib(spread(g.sib))
        m.bp[...] = cross(m.dvp[at(g.me, block), :], m.wv[...])
        turns.tick()
        sh.put_diag(split(g.diag))
        sh.put_opp(split(g.opp))
        turns.tick()
        sh.put_sib(split(g.sib))
        m.shp[...] = split(g.me)(0)
        turns.tick()

    m.need(m.se, m.st, m.xl, m.kf, m.tab, m.om)
    half_states = m.acc.shape[0] // 4
    m.acc[...] = jnp.zeros(m.acc.shape, f32)
    m.go[...] = jnp.zeros(m.go.shape, f32)
    gamma = tuple(jnp.zeros((SUB, LANES), f32) for _ in range(2 * half_states))
    per = length // SPAN // pieces
    own_mix = mixing(g.me)
    for s in range(pieces - 1, -1, -1):
        rows = pl.ds(s * (length // pieces), length // pieces)
        d_e = dm.take(s, own_mix(s)) * m.se[rows, :].astype(f32)
        for l in range(sides):
            m.dq[l, rows, :] = d_e[:, LANES * l : LANES * l + LANES]
        for n in range(per - 1, -1, -2):
            gamma = filter_backward(m, s * per + n, 2, gamma)
            turns.tick()
        for k, dev in enumerate(others):

            @pl.when(dev == s)
            def _():
                parts[k].start()

        if s == pieces - 1:
            spreading()
    filter_gradients(m)
    base_row = m.pk.shape[0] - PACK_TAIL
    m.pk[base_row:, :] = jnp.zeros((PACK_TAIL, channels), f32)
    m.pk[base_row : base_row + 1, :] = m.go[...]
    m.gs[...] = sh.take(0, m.shp[...]).astype(bf16)
    turns.tick()
    m.need(m.tok, m.so, m.gain, m.dy, m.gr, m.segb, m.segr)
    for s in range(2):
        piece = pl.ds(s * half, half)
        m.bp[piece, :] = xv.take(s, m.bp[piece, :])
    own_columns = at(g.me, channels)
    m.bp[:, own_columns] = m.bp[:, own_columns] + m.dxb[at(g.me, block), :].astype(f32)
    for k, dev in enumerate(others):
        parts[k].wait_recv()
        columns = at(dev, channels)
        m.bp[:, columns] = m.bp[:, columns] + m.dxr[k].astype(f32)
    gain_sum = jnp.zeros((1, width), f32)
    lane = lax.broadcasted_iota(jnp.int32, (half, LANES), 1)
    for s in range(2):
        piece = pl.ds(s * half, half)
        mean, rstd, total = (m.so[n, piece, :][:, :1] for n in range(3))
        centred = m.tok[piece, :].astype(f32) - mean
        d_xn = m.bp[piece, :]
        gain_sum = gain_sum + jnp.sum(d_xn * (centred * rstd), axis=0, keepdims=True)
        d_hat = d_xn * m.gain[...]
        d_var = -0.5 * rstd * rstd * rstd * jnp.sum(d_hat * centred, axis=1, keepdims=True)
        one = (-rstd * jnp.sum(d_hat, axis=1, keepdims=True) - 2.0 * mean * d_var) / total
        two = d_var / total
        m.bp[piece, :] = d_hat * rstd + m.dy[piece, :]
        m.aw[piece, :] = jnp.where(lane == 0, one, jnp.where(lane == 1, two, 0.0))
    m.smo[0:1, :] = gain_sum
    m.smo[1:2, :] = m.gr[...]
    turned = m.aw[...].T
    for n in range(2):
        rest = turned[n : n + 1, :]
        for k in range(3):
            top = rest.astype(bf16).astype(f32)
            m.art[3 * n + k : 3 * n + k + 1, :] = top
            rest = rest - top
    m.art[6:8, :] = jnp.zeros((2, block), f32)
    m.art[8:16, :] = jnp.zeros((8, block), f32)
    m.aro[...] = m.art[...].astype(bf16)
    for copy in tails + small:
        copy.start()
    m.ar[:, at(g.me, block)] = m.aro[...]
    m.sm[g.me] = m.smo[...]
    reach = -(-MAX_DOC // block)
    keys = min((reach + 1) * block, length)
    first_key = pl.multiple_of(jnp.minimum(g.me * block, length - keys), LANES)
    first_row = pl.multiple_of(g.me * block, LANES)
    here = m.segb[pl.ds(pl.multiple_of(first_row + SUB, SUB), block), :][:, :1]
    same = here == m.segr[:, pl.ds(first_key, keys)].astype(f32)
    row = first_row + lax.broadcasted_iota(jnp.int32, (block, keys), 0)
    key = first_key + lax.broadcasted_iota(jnp.int32, (block, keys), 1)
    seen = (same & (row <= key)).astype(bf16)
    for copy in tails:
        copy.wait_recv()
    pulled = cross(seen, m.ar[:, pl.ds(first_key, keys)])
    b_one = pulled[:, 0:1] + pulled[:, 1:2] + pulled[:, 2:3]
    b_two = pulled[:, 3:4] + pulled[:, 4:5] + pulled[:, 5:6]
    for s in range(2):
        piece = pl.ds(s * half, half)
        rows = slice(s * half, (s + 1) * half)
        x = m.tok[piece, :].astype(f32)
        m.gt[piece, :] = (m.bp[piece, :] + b_one[rows] + 2.0 * x * b_two[rows]).astype(bf16)
    m.flush(m.gt)
    turns.tick()
    for copy in small:
        copy.wait_recv()
    total = m.sm[0]
    for j in range(1, m.sm.shape[0]):
        total = total + m.sm[j]
    per = width // channels
    for n in range(2):
        for k in range(per):
            row = base_row + 1 + n * per + k
            m.pk[row : row + 1, :] = total[n : n + 1, k * channels : (k + 1) * channels]
    for n in range(3):
        row = base_row + 1 + 2 * per + n
        m.pk[row : row + 1, :shared] = total[2 + n : 3 + n, :shared]
    begin(3)
    turns.close()
    for moved in (dm, xv, sh, back):
        moved.close()
    for copy in parts + small + tails:
        copy.wait_send()


def body(count, m):
    g = Group()
    m.load(m.tok, m.wsh, m.cot, m.segr, m.p0, m.p1, m.p2, m.p3, m.p4, m.p5)
    m.load(m.gain, m.om, m.wv, m.wag, m.qg, m.qb, m.kg, m.wo, m.rg, m.wg, m.wu, m.wd)
    m.refs.update(mean=m.dq.at[0], rstd=m.dq.at[1])
    turns = Turns()
    plans = (
        [(m.gd, m.gdb, "gdt")],
        [(m.gg, m.ggb, "ggt"), (m.gu, m.gub, "gut")],
        [(m.gao, m.gaob, "gaot"), (m.r, m.gagb, "gagt"), (m.os, m.gvb, "gvt")],
    ) if count else ()
    rings = [Ring(m, count, plan) for plan in plans]
    if count:
        rings.append(Direct(m, count, [(m.gs, m.gsb, m.gss, "gst"), (m.pk, m.pkb, m.pks, "pkt")]))
        g.greet(rings[0].neighbours())
    else:
        g.greet()

    alone = (
        ((m.gd, "gdt"),),
        ((m.gg, "ggt"), (m.gu, "gut")),
        ((m.gao, "gaot"), (m.r, "gagt"), (m.os, "gvt")),
        ((m.gs, "gst"), (m.pk, "pkt")),
    )

    def begin(n):
        if rings:
            turns.begin(rings[n])
        else:
            for ref, name in alone[n]:
                m.store(ref, name)

    cots, normed = forward_attention(m, g)
    back = feed_forward(m, g, cots, normed, turns, begin)
    backward_attention(m, g, back, turns, begin)
    m.close()


def run(arrays, sizes, count):
    length, width, block, channels, shared, values, units = sizes
    blocks = length // block
    keys = min((-(-MAX_DOC // block) + 1) * block, length)
    sides = channels // LANES
    dims = arrays.p0.shape[0]
    half_states = sides * (dims // SUB)
    late = dict(
        gao=((values, width), bf16),
        gag=((width, values), bf16),
        gv=((width, values), bf16),
        gs=((channels, shared), bf16),
        pk=((6 * dims + PACK_TAIL, channels), f32),
    )
    summed = dict(
        gd=((units, width), bf16),
        gg=((width, units), bf16),
        gu=((width, units), bf16),
        **late,
    )
    if not ring_fits(summed.values(), count):
        count = 0
    outs = dict(
        gt=((block, width), bf16),
        out=((block, width), bf16),
    )
    scratch = dict(
        xt=((length, width), bf16),
        cotf=((length, width), bf16),
        xn=((length, width), bf16),
        mx=((length, width), bf16),
        xl=((sides, length, LANES), f32),
        tab=((11, dims, channels), f32),
        kf=((length + SUB, LANES), f32),
        segb=((length + SUB, LANES), f32),
        so=((3, block, LANES), f32),
        sums=((length, LANES), bf16),
        se=((length, channels), bf16),
        st=((length // SPAN, 2 * half_states, SUB, LANES), f32),
        v=((length, values), bf16),
        sv=((length, values), bf16),
        z=((length, shared), bf16),
        q=((length, shared), bf16),
        k=((length, shared), bf16),
        wsf=((width, shared), bf16),
        p=((blocks, block, keys), bf16),
        r=((length, values), bf16),
        os=((length, values), bf16),
        w=((length, values), bf16),
        y=((block, width), f32),
        rs=((block, LANES), f32),
        yno=((block, width), bf16),
        bp=((block, width), f32),
        act=((length, units), bf16),
        dg=((length, units), bf16),
        du=((length, units), bf16),
        gd=summed["gd"],
        dy=((block, width), f32),
        gr=((1, width), f32),
        dk=((length, shared), f32),
        dv=((length, values), f32),
        dq=((max(sides, shared // LANES), length, LANES), f32),
        shp=((channels, shared), f32),
        go=((1, channels), f32),
        acc=((4 * half_states, SUB, LANES), f32),
        kept=((SPAN, 2 * half_states, SUB, LANES), f32),
        part=((sides, SPAN * SUB, LANES), f32),
        dxr=((3, block, channels), bf16),
        art=((16, block), f32),
        aro=((16, block), bf16),
        ar=((16, length), bf16),
        smo=((SUB, width), f32),
        sm=((length // block, SUB, width), f32),
        gao=late["gao"],
        gs=late["gs"],
        pk=late["pk"],
        **scatter_buffers("dm", length, channels),
        **scatter_buffers("xv", block, width),
        **scatter_buffers("sh", channels, shared),
    )
    alias = dict(yn="xt", dyf="cotf", gg="wg", gu="wu", dyo="yno", dvp="v", aw="rs")
    alias.update(dz="q", dxb="k", drp="w", mxl="dm_os")
    shared_boxes = dict(gag="dg", gv="du")
    sems = [69, 69]
    if count:
        for name, (shape, kind) in summed.items():
            small = name in ("gs", "pk")
            used = count - 1, *(ring_rows(shape, kind, count) or ())
            if name in shared_boxes and 2 * used[0] * used[1] <= length and used[2] <= units:
                alias[name + "b"] = shared_boxes[name]
                continue
            scratch[name + "b"] = (direct_box if small else ring_box)(shape, kind, count)
        scratch.update(gss=summed["gs"], pks=summed["pk"])
        sems = [69 + 12 + 4 * (count - 1), 69 + 12 * RING_SLOTS + 4 * (count - 1)]
    bare = {name + "t": entry for name, entry in summed.items()}
    done = run_stage(
        functools.partial(body, count), arrays, outs, scratch, sems, 1, bare.items(), alias.items()
    )
    done.dims = dims
    done.summed = bool(count)
    return done


def body_f(dims, shared, m):
    wide = ((m.gd, m.gdt), (m.gg, m.ggt), (m.gu, m.gut), (m.gao, m.gaot), (m.gag, m.gagt))
    wide += ((m.gv, m.gvt), (m.gs, m.gst))
    m.load(m.out, m.gt, m.gd, m.gg, m.gu, m.gao, m.gag, m.gv, m.gs, m.pk)
    for source, target in ((m.out, m.outt), (m.gt, m.gtt)):
        m.need(source)
        target[...] = source[...]
        m.flush(target)
    for source, target in wide:
        m.need(source)
        rows = source.shape[0] // 2
        for n in range(2):

            def part(i, _):
                piece = pl.ds(pl.multiple_of(n * rows + i * 16, 16), 16)
                target[piece, :] = source[piece, :].astype(f32)
                return 0

            lax.fori_loop(0, rows // 16, part, 0, unroll=4)
        m.flush(target)
    m.need(m.pk)
    for k, out in enumerate((m.e0, m.e1, m.e2, m.e3, m.e4, m.e5)):
        out[...] = m.pk[k * dims : (k + 1) * dims, :]
    top = 6 * dims
    channels = m.pk.shape[1]
    m.om[...] = m.pk[top : top + 1, :]
    per = m.norm.shape[1] // channels
    for n, out in enumerate((m.norm, m.rms)):
        for k in range(per):
            row = top + 1 + n * per + k
            out[:, k * channels : (k + 1) * channels] = m.pk[row : row + 1, :]
    for n, out in enumerate((m.qg, m.qb, m.kg)):
        row = top + 1 + 2 * per + n
        out[...] = m.pk[row : row + 1, :shared]
    m.flush(m.e0, m.e1, m.e2, m.e3, m.e4, m.e5, m.om, m.norm, m.rms, m.qg, m.qb, m.kg)
    m.close()


def finish(c, shared):
    sums = dict(gd=c.gdt, gg=c.ggt, gu=c.gut, gao=c.gaot, gag=c.gagt, gv=c.gvt, gs=c.gst, pk=c.pkt)
    if not c.summed:
        total = lax.psum([value.astype(f32) for value in sums.values()], "dp")
        sums = {name: v.astype(old.dtype) for (name, old), v in zip(sums.items(), total)}
    channels, width = sums["pk"].shape[1], sums["gd"].shape[1]
    outs = dict(
        e0=((c.dims, channels), f32),
        e1=((c.dims, channels), f32),
        e2=((c.dims, channels), f32),
        e3=((c.dims, channels), f32),
        e4=((c.dims, channels), f32),
        e5=((c.dims, channels), f32),
        om=((1, channels), f32),
        norm=((1, width), f32),
        rms=((1, width), f32),
        qg=((1, shared), f32),
        qb=((1, shared), f32),
        kg=((1, shared), f32),
    )
    for name, value in sums.items():
        if value is not sums["pk"]:
            outs[name + "t"] = (value.shape, f32)
    outs.update(outt=(c.out.shape, bf16), gtt=(c.gt.shape, bf16))
    f = run_stage(
        functools.partial(body_f, c.dims, shared),
        types.SimpleNamespace(out=c.out, gt=c.gt, **sums), outs, {}, (0, 0), None,
    )
    tables = [table.T for table in (f.e0, f.e1, f.e2, f.e3, f.e4, f.e5)]
    return (
        f.outt, f.gtt, f.norm[0], *tables, f.om[0], f.gst,
        f.qg[0], f.qb[0], f.kg[0], f.gagt, f.gvt, f.gaot, f.rms[0], f.ggt, f.gut, f.gdt,
    )


def on_device(
    tokens,
    segments,
    cotangent,
    timestep_norm_gain,
    ema_alpha,
    ema_delta,
    ema_theta,
    ema_beta,
    eta_real,
    eta_imag,
    ema_omega,
    w_shared,
    q_gain,
    q_bias,
    k_gain,
    w_attgate,
    w_value,
    w_attout,
    rms_gain,
    w_gate,
    w_up,
    w_down,
):
    block, width = tokens.shape
    length = segments.shape[1]
    channels, dims = ema_alpha.shape
    shared = w_shared.shape[1]
    values = w_value.shape[1]
    units = w_gate.shape[1]
    om = ema_omega[None]
    gain, rg = timestep_norm_gain[None], rms_gain[None]
    qg, qb, kg = q_gain[None], q_bias[None], k_gain[None]
    segr = segments
    done = run(
        types.SimpleNamespace(
            tok=tokens, cot=cotangent, wsh=w_shared, segr=segr, gain=gain,
            p0=ema_alpha.T, p1=ema_delta.T, p2=ema_theta.T,
            p3=ema_beta.T, p4=eta_real.T, p5=eta_imag.T, om=om, qg=qg, qb=qb, kg=kg,
            wag=w_attgate, wv=w_value, wo=w_attout, rg=rg, wg=w_gate, wu=w_up, wd=w_down,
        ),
        (length, width, block, channels, shared, values, units),
        lax.axis_size("dp"),
    )
    return finish(done, shared)


def solution(mesh):
    placed = (
        P(("dp", "tensor"), None),
        P("dp", None),
        P(("dp", "tensor"), None),
        P(),
        P("tensor", None),
        P("tensor", None),
        P("tensor", None),
        P("tensor", None),
        P("tensor", None),
        P("tensor", None),
        P("tensor"),
        P("tensor", None),
        P(),
        P(),
        P(),
        P(None, "tensor"),
        P(None, "tensor"),
        P("tensor", None),
        P(),
        P(None, "tensor"),
        P(None, "tensor"),
        P("tensor", None),
    )
    return jax.shard_map(
        on_device,
        mesh=mesh,
        in_specs=placed,
        out_specs=(
            P(("dp", "tensor"), None),
            P(("dp", "tensor"), None),
            P(),
            P("tensor", None),
            P("tensor", None),
            P("tensor", None),
            P("tensor", None),
            P("tensor", None),
            P("tensor", None),
            P("tensor"),
            P("tensor", None),
            P(),
            P(),
            P(),
            P(None, "tensor"),
            P(None, "tensor"),
            P("tensor", None),
            P(),
            P(None, "tensor"),
            P(None, "tensor"),
            P("tensor", None),
        ),
        check_vma=False,
    )
```
